256 devices in a mesh: gx: 16 (over x, y), gy: 8 (over z), gz: 2 (over core).
Axes of the slice: x: 4, y: 4, z: 8, core: 2. Of those that a mesh axis runs over, the one named last changes fastest.
Arguments:
- displacement: float32 [3, 128, 64, 512], P(None, 'gx', 'gy', 'gz'), may hold values from -6 to 6
- physical: float32 [128, 64, 512], P('gx', 'gy', 'gz'), may hold values from 0.1 to 1
- design: float32 [128, 64, 512], P('gx', 'gy', 'gz'), may hold values from 0.05 to 0.95
- passive: int32 [128, 64, 512], P('gx', 'gy', 'gz'), may hold values 0 or 1
- supports: int32 [1024], replicated, may hold values from 0 to 4194303
Outputs:
- new_design: float32 [128, 64, 512], P('gx', 'gy', 'gz')
- new_physical: float32 [128, 64, 512], P('gx', 'gy', 'gz')
- node_blocks: float32 [6, 128, 64, 512], P(None, 'gx', 'gy', 'gz')
The draws below stay inside these ranges and needn't reach their ends.
Inputs may be any that keep to these rules, and one draw needn't show every extreme that they name: `supports`: node number (i * 64 + j) * 512 + k for node (i, j, k); repeats may occur.
All inputs are finite; a program needn't handle non-finite values. No bound on the sum of `passive` on one device may be relied on, other than what follows from the above.
Results may differ from the reference program's by a relative error of at most 0.0003.
Values sent between devices are 32-bit elements; how exact they have to be, the bound alone decides.
No kernel may reach another device: no remote copies, remote signals or barrier semaphores. Data moves between devices by JAX's collectives and lax.ppermute only.
A program may use at most 64 MiB of HBM per device.

```python
import math
import jax
import jax.numpy as jnp
import numpy as np
from jax import lax

STEPS = 10
NSUP = 1024
NX = 128
NY = 64
NZ = 512


def with_ends(values, stream_key, least, largest):
    longest = values.shape.index(max(values.shape))
    spots = []
    for shift in (0, 1):
        where = [jax.random.randint(jax.random.fold_in(stream_key, axis), (), 0, length) for axis, length in enumerate(values.shape)]
        where[longest] = (where[longest] + shift) % values.shape[longest]
        spots.append(tuple(where))
    return values.at[spots[0]].set(least).at[spots[1]].set(largest)


def shard_levels(rng, extent, cuts, least, high):
    loudness = 1.0
    for position, shards_of in cuts:
        draws = jax.random.uniform(jax.random.fold_in(jax.random.fold_in(rng, 6), position), (shards_of,), jnp.float32, least / len(cuts), high / len(cuts))
        loudness = loudness * jnp.repeat(jnp.exp(draws), extent[position] // shards_of).reshape((-1,) + (1,) * (len(extent) - 1 - position))
    return loudness


def bell_draw(stream_key, dims, width, reach, split=(), held_as=jnp.bfloat16):
    factor_of = shard_levels(stream_key, dims, split, -0.22, 0.18) if split else 1.0
    drawn = jax.random.normal(stream_key, dims, jnp.float32) * width * factor_of
    return jnp.minimum(jnp.maximum(drawn, -reach), reach).astype(held_as)


def setup_inputs(seed: int = 0) -> dict:
    splits = jax.random.split(jax.random.key(seed), 6)
    displacement = bell_draw(splits[0], (3, NX, NY, NZ), 1.0, 6.0, ((1, 16), (2, 8), (3, 2)), jnp.float32)
    physical = jnp.clip(0.1 + 0.9 * jax.random.uniform(splits[1], (NX, NY, NZ), jnp.float32) ** shard_levels(splits[1], (NX, NY, NZ), ((0, 16), (1, 8), (2, 2)), -0.2, 0.2), 0.1, 1.0)
    design = jnp.clip(0.05 + 0.9 * jax.random.uniform(splits[2], (NX, NY, NZ), jnp.float32) ** shard_levels(splits[2], (NX, NY, NZ), ((0, 16), (1, 8), (2, 2)), -0.2, 0.2), 0.05, 0.95)
    passive = with_ends((jax.random.randint(splits[3], (NX, NY, NZ), 0, 8) < 1).astype(jnp.int32), jax.random.fold_in(splits[3], 1), 0, 1)
    supports = with_ends(jax.random.randint(splits[4], (NSUP,), 0, NX * NY * NZ), jax.random.fold_in(splits[4], 1), 0, (NX * NY * NZ) - 1).astype(jnp.int32)
    return {"displacement": displacement, "physical": physical, "design": design, "passive": passive, "supports": supports}


filter_radius = 2.5
penalty = 3.0
move_limit = 0.2
stiff_floor = 1e-09
volume_share = 0.5
log_lower = -20.0
log_upper = 20.0
poisson = 0.3

def corner_offsets():
    return [(q // 4, q // 2 % 2, q % 2) for q in range(8)]

def hex_stiffness():
    lame_first = poisson / ((1.0 + poisson) * (1.0 - 2.0 * poisson))
    shear_modulus = 0.5 / (1.0 + poisson)
    elastic = np.zeros((6, 6))
    elastic[:3, :3] = lame_first
    for d in range(3):
        elastic[d, d] += 2.0 * shear_modulus
        elastic[d + 3, d + 3] = shear_modulus
    corners = corner_offsets()
    points = [0.5 - 0.5 / math.sqrt(3.0), 0.5 + 0.5 / math.sqrt(3.0)]
    matrix = np.zeros((24, 24))
    for p in points:
        for q in points:
            for r in points:
                location = [p, q, r]
                gradients = np.zeros((8, 3))
                for n in range(8):
                    factors = [location[e] if corners[n][e] == 1 else 1.0 - location[e] for e in range(3)]
                    for d in range(3):
                        sign_value = 1.0 if corners[n][d] == 1 else -1.0
                        gradients[n, d] = sign_value * factors[(d + 1) % 3] * factors[(d + 2) % 3]
                strain = np.zeros((6, 24))
                for n in range(8):
                    column = 3 * n
                    strain[0, column] = gradients[n, 0]
                    strain[1, column + 1] = gradients[n, 1]
                    strain[2, column + 2] = gradients[n, 2]
                    strain[3, column + 1] = gradients[n, 2]
                    strain[3, column + 2] = gradients[n, 1]
                    strain[4, column] = gradients[n, 2]
                    strain[4, column + 2] = gradients[n, 0]
                    strain[5, column] = gradients[n, 1]
                    strain[5, column + 1] = gradients[n, 0]
                matrix += strain.T @ elastic @ strain / 8.0
    return matrix

def corner_blocks():
    matrix = hex_stiffness()
    entry_pairs = [(0, 0), (1, 1), (2, 2), (1, 2), (0, 2), (0, 1)]
    block_table = np.zeros((8, 6))
    for n in range(8):
        for m, (i, j) in enumerate(entry_pairs):
            block_table[n, m] = matrix[3 * n + i, 3 * n + j]
    return block_table

def filter_taps():
    tap_list = []
    for a in range(-2, 3):
        for b in range(-2, 3):
            for c in range(-2, 3):
                weight = filter_radius - math.sqrt(a * a + b * b + c * c)
                if weight > 0.0:
                    tap_list.append((a, b, c, weight))
    return tap_list

def stencil(padded, offset, counts):
    accumulated = jnp.zeros(counts, jnp.float32)
    for a, b, c, weight in filter_taps():
        accumulated = accumulated + weight * padded[offset + a:offset + a + counts[0], offset + b:offset + b + counts[1], offset + c:offset + c + counts[2]]
    return accumulated

def element_energy(ghosted, plane_index, width_y, width_z, stiffness):
    node_slab = lax.dynamic_slice_in_dim(ghosted, plane_index, 2, 1)
    vectors = jnp.stack([node_slab[:, a, b:b + width_y, c:c + width_z] for a, b, c in corner_offsets()]).reshape(24, width_y * width_z)
    product = jnp.dot(stiffness, vectors, preferred_element_type=jnp.float32, precision=lax.Precision.HIGHEST)
    return lax.optimization_barrier(jnp.sum(vectors * product, axis=0)).reshape(width_y, width_z)

def reference(displacement, physical, design, passive, supports):
    stiffness = jnp.asarray(hex_stiffness(), jnp.float32)
    blocks = jnp.asarray(corner_blocks(), jnp.float32)
    counts = (NX, NY, NZ)
    ghosted = jnp.pad(displacement, ((0, 0), (0, 1), (0, 1), (0, 1)))
    energy = lax.map(lambda plane_index: element_energy(ghosted, plane_index, NY, NZ, stiffness), jnp.arange(NX, dtype=jnp.int32))
    sensitivity = -penalty * (1.0 - stiff_floor) * physical * physical * energy
    weight_sum = stencil(jnp.pad(jnp.ones(counts, jnp.float32), 2), 2, counts)
    filtered = stencil(jnp.pad(sensitivity / weight_sum, 2), 2, counts)
    volume_weight = stencil(jnp.pad(1.0 / weight_sum, 2), 2, counts)
    scaled_design = design * jnp.sqrt(-filtered / volume_weight)
    floor_bound = jnp.maximum(0.0, design - move_limit)
    ceiling = jnp.minimum(1.0, design + move_limit)
    solid_mask = passive == 1

    def candidate(log_mult):
        return jnp.where(solid_mask, 1.0, jnp.clip(scaled_design * jnp.exp(-0.5 * log_mult), floor_bound, ceiling))
    target = volume_share * (NX * NY * NZ)
    bracket_low = jnp.float32(log_lower)
    bracket_high = jnp.float32(log_upper)
    for t in range(STEPS):
        middle = 0.5 * (bracket_low + bracket_high)
        volume = jnp.sum(volume_weight * candidate(middle))
        too_full = volume > target
        bracket_low = jnp.where(too_full, middle, bracket_low)
        bracket_high = jnp.where(too_full, bracket_high, middle)
    new_design = candidate(0.5 * (bracket_low + bracket_high))
    new_physical = stencil(jnp.pad(new_design, 2), 2, counts) / weight_sum
    stiffness_scale = stiff_floor + new_physical * new_physical * new_physical * (1.0 - stiff_floor)
    shifted = jnp.pad(stiffness_scale, ((1, 0), (1, 0), (1, 0)))
    assembled = jnp.zeros((6, NX, NY, NZ), jnp.float32)
    for n, (a, b, c) in enumerate(corner_offsets()):
        assembled = assembled + blocks[n][:, None, None, None] * shifted[1 - a:1 - a + NX, 1 - b:1 - b + NY, 1 - c:1 - c + NZ][None]
    support_marks = jnp.zeros(NX * NY * NZ, jnp.int32).at[supports].set(1).reshape(counts)
    identity = jnp.array([1.0, 1.0, 1.0, 0.0, 0.0, 0.0], jnp.float32)
    node_blocks = jnp.where(support_marks[None] == 1, identity[:, None, None, None], assembled)
    return (new_design, new_physical, node_blocks)
```

```python
import functools
import math

import jax
import jax.numpy as jnp
import numpy as np
from jax import lax
from jax.experimental import pallas as pl
from jax.experimental.pallas import tpu as pltpu
from jax.sharding import PartitionSpec as P

STEPS = 10

filter_radius = 2.5
penalty = 3.0
move_limit = 0.2
stiff_floor = 1e-09
volume_share = 0.5
log_lower = -20.0
log_upper = 20.0
poisson = 0.3

SX, SY, SZ = 8, 8, 256
ROWS, LANES, SIDE = 16, 384, 128
POINTS = 2**STEPS
F32 = jnp.float32


def corner_offsets():
    return [(q // 4, q // 2 % 2, q % 2) for q in range(8)]


def hex_stiffness():
    lame_first = poisson / ((1.0 + poisson) * (1.0 - 2.0 * poisson))
    shear_modulus = 0.5 / (1.0 + poisson)
    elastic = np.zeros((6, 6))
    elastic[:3, :3] = lame_first
    for d in range(3):
        elastic[d, d] += 2.0 * shear_modulus
        elastic[d + 3, d + 3] = shear_modulus
    corners = corner_offsets()
    points = [0.5 - 0.5 / math.sqrt(3.0), 0.5 + 0.5 / math.sqrt(3.0)]
    matrix = np.zeros((24, 24))
    for p in points:
        for q in points:
            for r in points:
                location = [p, q, r]
                gradients = np.zeros((8, 3))
                for n in range(8):
                    factors = [
                        location[e] if corners[n][e] == 1 else 1.0 - location[e] for e in range(3)
                    ]
                    for d in range(3):
                        sign_value = 1.0 if corners[n][d] == 1 else -1.0
                        gradients[n, d] = sign_value * factors[(d + 1) % 3] * factors[(d + 2) % 3]
                strain = np.zeros((6, 24))
                for n in range(8):
                    column = 3 * n
                    strain[0, column] = gradients[n, 0]
                    strain[1, column + 1] = gradients[n, 1]
                    strain[2, column + 2] = gradients[n, 2]
                    strain[3, column + 1] = gradients[n, 2]
                    strain[3, column + 2] = gradients[n, 1]
                    strain[4, column] = gradients[n, 2]
                    strain[4, column + 2] = gradients[n, 0]
                    strain[5, column] = gradients[n, 1]
                    strain[5, column + 1] = gradients[n, 0]
                matrix += strain.T @ elastic @ strain / 8.0
    return matrix


def energy_squares():
    corners = corner_offsets()
    modes = np.zeros((24, 24))
    for s in range(8):
        bits = (s // 4, s // 2 % 2, s % 2)
        for n in range(8):
            sign_value = 1.0
            for e in range(3):
                if bits[e] == 1 and corners[n][e] == 0:
                    sign_value = -sign_value
            for d in range(3):
                modes[3 * n + d, 3 * s + d] = sign_value
    form = modes.T @ hex_stiffness() @ modes / 64.0
    used = np.zeros((24, 24))
    squares = []
    for parity in range(8):
        members = [3 * (parity ^ (4, 2, 1)[d]) + d for d in range(3)]
        block = form[np.ix_(members, members)].copy()
        used[np.ix_(members, members)] = block
        for r in range(3):
            if block[r, r] < 1e-9:
                continue
            factors = block[r] / math.sqrt(block[r, r])
            block -= np.outer(factors, factors)
            squares.append([(members[c], factors[c]) for c in range(3) if abs(factors[c]) > 1e-9])
        assert np.abs(block).max() < 1e-9
    assert np.abs(used - form).max() < 1e-9
    return squares


def corner_factors():
    matrix = hex_stiffness()
    factors = (matrix[0, 0], matrix[1, 2], matrix[0, 2], matrix[0, 1])
    for n, corner in enumerate(corner_offsets()):
        sign = [1.0 if c == 1 else -1.0 for c in corner]
        block = matrix[3 * n : 3 * n + 3, 3 * n : 3 * n + 3]
        assert np.allclose(np.diag(block), factors[0])
        assert np.allclose(block[1, 2], factors[1] * sign[1] * sign[2])
        assert np.allclose(block[0, 2], factors[2] * sign[0] * sign[2])
        assert np.allclose(block[0, 1], factors[3] * sign[0] * sign[1])
    return factors


def tap(square):
    return max(0.0, filter_radius - math.sqrt(square))


def rolled(value, steps, dim):
    return pltpu.roll(value, (-steps) % value.shape[dim], dim)


def row_pairs(plane):
    return (
        rolled(plane, 1, 0) + rolled(plane, -1, 0),
        rolled(plane, 2, 0) + rolled(plane, -2, 0),
    )


def filtered_plane(plane_of, near_of, far_of, p):
    ring_0 = plane_of(p)
    ring_1 = near_of(p) + plane_of(p - 1) + plane_of(p + 1)
    ring_2 = near_of(p - 1) + near_of(p + 1)
    ring_4 = far_of(p) + plane_of(p - 2) + plane_of(p + 2)
    ring_5 = far_of(p - 1) + far_of(p + 1) + near_of(p - 2) + near_of(p + 2)
    layers = []
    for c in (0, 1, 2):
        total = None
        for square, ring in ((0, ring_0), (1, ring_1), (2, ring_2), (4, ring_4), (5, ring_5)):
            weight = tap(square + c * c)
            if weight > 0.0:
                total = weight * ring if total is None else total + weight * ring
        layers.append(total)
    middle, near, far = layers
    return middle + (rolled(near, 1, 1) + rolled(near, -1, 1)) + (rolled(far, 2, 1) + rolled(far, -2, 1))


def weights_kernel(place_ref, support_ref, inverse_ref, volume_ref, mark_ref, near_ref, far_ref, *, extents):
    total_x, total_y, total_z = extents
    first_x = place_ref[0] * SX
    first_y = place_ref[1] * SY
    first_z = place_ref[2] * SZ
    row = lax.broadcasted_iota(jnp.int32, (ROWS, LANES), 0)
    lane = lax.broadcasted_iota(jnp.int32, (ROWS, LANES), 1)
    y = first_y + jnp.where(row < 12, row, row - ROWS)
    z = first_z + jnp.where(lane < SZ + SIDE // 2, lane, lane - LANES)
    inside = jnp.where((y >= 0) & (y < total_y) & (z >= 0) & (z < total_z), 1.0, 0.0).astype(F32)
    near, far = row_pairs(inside)

    def present(p):
        x = first_x + p
        return jnp.where((x >= 0) & (x < total_x), 1.0, 0.0).astype(F32)

    for p in range(SX + 4):
        x = p - 2
        weight_sum = filtered_plane(
            lambda q: inside * present(q), lambda q: near * present(q), lambda q: far * present(q), x
        )
        here = inside * present(x)
        inverse = jnp.where(here > 0.0, 1.0 / jnp.where(here > 0.0, weight_sum, 1.0), 0.0)
        inverse_ref[p] = inverse
        inverse_near, inverse_far = row_pairs(inverse)
        near_ref[p] = inverse_near
        far_ref[p] = inverse_far
    for p in range(SX):
        volume = filtered_plane(
            lambda q: inverse_ref[q, 0:SY], lambda q: near_ref[q, 0:SY], lambda q: far_ref[q, 0:SY], p + 2
        )
        volume_ref[p] = volume[:, 0:SZ]
    node = support_ref[...]
    node_x = node // (total_y * total_z) - first_x
    node_y = node // total_z % total_y - first_y
    node_z = node % total_z - first_z
    owned = (node_x >= 0) & (node_x < SX) & (node_y >= 0) & (node_y < SY)
    line = jnp.where(owned, node_x * SY + node_y, -1)
    count = node.shape[1]
    lines = jnp.where(lax.broadcasted_iota(jnp.int32, (SX * SY, count), 0) == line, 1.0, 0.0)
    lanes = jnp.where(lax.broadcasted_iota(jnp.int32, (SZ, count), 0) == node_z, 1.0, 0.0)
    hits = lax.dot_general(
        lines.astype(jnp.bfloat16),
        lanes.astype(jnp.bfloat16),
        (((1,), (1,)), ((), ())),
        preferred_element_type=F32,
    )
    for p in range(SX):
        mark_ref[p] = hits[p * SY : (p + 1) * SY]


def side_mask(first_z_index, upper, lower):
    lane = lax.broadcasted_iota(jnp.int32, (ROWS, SIDE), 1)
    start = jnp.where(first_z_index == 0, 0, SIDE - lower)
    stop = jnp.where(first_z_index == 0, upper, SIDE)
    return (lane >= start) & (lane < stop)


def assemble(ext_ref, fields, low, high, up_rows, low_rows, own, x_low, x_high, y_low, y_high, side, keep):
    planes = low + SX + high
    for f in range(fields):
        for p in range(planes):
            if p < low:
                middle = x_low[f, p]
            elif p < low + SX:
                middle = own(f, p - low)
            else:
                middle = x_high[f, p - low - SX]
            ext_ref[f, p, 0:SY, 0:SZ] = middle
            filler = jnp.zeros((SY - up_rows - low_rows, SZ), F32)
            ext_ref[f, p, SY:ROWS, 0:SZ] = jnp.concatenate([y_high[f, p], filler, y_low[f, p]], axis=0)
            ext_ref[f, p, :, SZ:LANES] = jnp.where(keep, side[f, p], 0.0)


def design_kernel(
    place_ref, shift_ref, physical_ref, x_low, x_high, y_low, y_high, side, inverse_ref, volume_ref, design_ref,
    passive_ref, out_ref, up_ref, down_ref, ext_ref, sens_ref, near_ref, far_ref, *, squares
):
    keep = side_mask(place_ref[2], 3, 2)
    assemble(
        ext_ref, 4, 2, 3, 3, 2, lambda f, p: shift_ref[f, p] if f < 3 else physical_ref[p],
        x_low, x_high, y_low, y_high, side, keep,
    )
    scale = penalty * (1.0 - stiff_floor)

    @pl.loop(0, SX + 4)
    def _(p):
        modes = {}
        for d in range(3):
            here, above = ext_ref[d, p], ext_ref[d, p + 1]
            for a, along_x in enumerate((here + above, above - here)):
                beyond = rolled(along_x, 1, 0)
                for b, along_y in enumerate((along_x + beyond, beyond - along_x)):
                    next_lane = rolled(along_y, 1, 1)
                    for c, mode in enumerate((along_y + next_lane, next_lane - along_y)):
                        modes[3 * (4 * a + 2 * b + c) + d] = mode
        energy = None
        for terms in squares:
            line = None
            for mode, factor in terms:
                term = float(factor) * modes[mode]
                line = term if line is None else line + term
            energy = line * line if energy is None else energy + line * line
        density = ext_ref[3, p]
        sens = scale * density * density * energy * inverse_ref[p]
        sens_ref[p] = sens
        near, far = row_pairs(sens)
        near_ref[p] = near
        far_ref[p] = far

    for p in range(SX):
        filtered = filtered_plane(
            lambda q: sens_ref[q, 0:SY], lambda q: near_ref[q, 0:SY], lambda q: far_ref[q, 0:SY], p + 2
        )[:, 0:SZ]
        design = design_ref[p]
        solid = passive_ref[p] == 1
        scaled = design * jnp.sqrt(filtered / volume_ref[p])
        floor_bound = jnp.where(solid, 1.0, jnp.maximum(0.0, design - move_limit))
        ceiling = jnp.where(solid, 1.0, jnp.minimum(1.0, design + move_limit))
        for f, value in enumerate((scaled, floor_bound, ceiling)):
            out_ref[f, p] = value
            if p < 2:
                down_ref[f, p] = value
            if p >= SX - 3:
                up_ref[f, p - (SX - 3)] = value


def volumes_kernel(exp_ref, bounds_ref, volume_ref, out_ref, weighted_ref, sums_ref):
    for p in range(SX):
        weight = volume_ref[p]
        for f in range(3):
            weighted = weight * bounds_ref[f, p]
            for h in range(2):
                weighted_ref[f, 2 * p + h] = weighted[:, h * 128 : (h + 1) * 128]

    @pl.loop(0, POINTS // 8)
    def _(g):
        factors = [exp_ref[g * 8 + j] for j in range(8)]
        totals = [None] * 8
        for v in range(2 * SX):
            scaled, floor_bound, ceiling = weighted_ref[0, v], weighted_ref[1, v], weighted_ref[2, v]
            for j in range(8):
                value = jnp.minimum(jnp.maximum(scaled * factors[j], floor_bound), ceiling)
                totals[j] = value if totals[j] is None else totals[j] + value
        rows = [jnp.sum(total, axis=0, keepdims=True) for total in totals]
        sums_ref[pl.ds(pl.multiple_of(g * 8, 8), 8), :] = jnp.concatenate(rows, axis=0)

    copies = out_ref.shape[0]
    result = lax.dot_general(
        jnp.ones((copies, 128), F32),
        sums_ref[...],
        (((1,), (1,)), ((), ())),
        precision=lax.Precision.HIGHEST,
        preferred_element_type=F32,
    )
    for i in range(8):
        out_ref[:, i, :] = result[:, i * 128 : (i + 1) * 128]


def repeat_kernel(part_ref, out_ref):
    total = part_ref[0]
    for i in range(1, part_ref.shape[0]):
        total = total + part_ref[i]
    for i in range(out_ref.shape[0]):
        out_ref[i] = total


def final_kernel(
    place_ref, part_ref, own_ref, x_low, x_high, y_low, y_high, side, inverse_ref, mark_ref, new_design_ref,
    new_physical_ref, blocks_ref, ext_ref, near_ref, far_ref, stiff_ref, *, factors, target
):
    total = part_ref[0]
    for i in range(1, part_ref.shape[0]):
        total = total + part_ref[i]
    low_end = jnp.minimum(jnp.sum(jnp.where(total > target, 1.0, 0.0)), POINTS - 1.0)
    multiplier = log_lower + (log_upper - log_lower) / POINTS * (low_end + 0.5)
    factor = jnp.exp(jnp.broadcast_to(-0.5 * multiplier, (ROWS, LANES)))
    keep = side_mask(place_ref[2], 2, 3)
    assemble(ext_ref, 3, 3, 2, 2, 3, lambda f, p: own_ref[f, p], x_low, x_high, y_low, y_high, side, keep)
    planes = SX + 5
    for p in range(planes):
        chosen = jnp.minimum(jnp.maximum(ext_ref[0, p] * factor, ext_ref[1, p]), ext_ref[2, p])
        ext_ref[0, p] = chosen
        near, far = row_pairs(chosen)
        near_ref[p] = near
        far_ref[p] = far
        if 3 <= p < SX + 3:
            new_design_ref[p - 3] = chosen[0:SY, 0:SZ]
    for p in range(SX + 1):
        inverse = inverse_ref[p + 1]
        density = (
            filtered_plane(lambda q: ext_ref[0, q], lambda q: near_ref[q], lambda q: far_ref[q], p + 2) * inverse
        )
        if p >= 1:
            new_physical_ref[p - 1] = density[0:SY, 0:SZ]
        cube = stiff_floor + density * density * density * (1.0 - stiff_floor)
        stiff_ref[p] = jnp.where(inverse > 0.0, cube, 0.0)
    for p in range(SX):
        below, here = stiff_ref[p], stiff_ref[p + 1]
        x_sum, x_diff = here + below, below - here
        x_sum_back, x_diff_back = rolled(x_sum, -1, 0), rolled(x_diff, -1, 0)
        sum_sum = (x_sum + x_sum_back)[0:SY]
        sum_diff = (x_sum_back - x_sum)[0:SY]
        diff_sum = (x_diff + x_diff_back)[0:SY]
        diff_diff = (x_diff_back - x_diff)[0:SY]
        marked = mark_ref[p] > 0.5
        even = factors[0] * (sum_sum + rolled(sum_sum, -1, 1))[:, 0:SZ]
        even = jnp.where(marked, 1.0, even)
        blocks_ref[0, p] = even
        blocks_ref[1, p] = even
        blocks_ref[2, p] = even
        yz = factors[1] * (rolled(sum_diff, -1, 1) - sum_diff)[:, 0:SZ]
        xz = factors[2] * (rolled(diff_sum, -1, 1) - diff_sum)[:, 0:SZ]
        xy = factors[3] * (diff_diff + rolled(diff_diff, -1, 1))[:, 0:SZ]
        blocks_ref[3, p] = jnp.where(marked, 0.0, yz)
        blocks_ref[4, p] = jnp.where(marked, 0.0, xz)
        blocks_ref[5, p] = jnp.where(marked, 0.0, xy)


def call(kernel, smem, vmem, shapes, scratch, flops):
    specs = [pl.BlockSpec(memory_space=pltpu.SMEM)] * smem + [pl.BlockSpec(memory_space=pltpu.VMEM)] * vmem
    outs = [jax.ShapeDtypeStruct(shape, F32) for shape in shapes]
    return pl.pallas_call(
        kernel,
        out_shape=outs,
        in_specs=specs,
        out_specs=[pl.BlockSpec(memory_space=pltpu.VMEM)] * len(outs),
        scratch_shapes=[pltpu.VMEM(shape, F32) for shape in scratch],
        compiler_params=pltpu.CompilerParams(vmem_limit_bytes=32 * 2**20),
        cost_estimate=pl.CostEstimate(flops=flops, bytes_accessed=10**6, transcendentals=0),
    )


def exchange(up, down, axis):
    count = lax.axis_size(axis)
    low = lax.ppermute(up, axis, [(i, i + 1) for i in range(count - 1)])
    high = lax.ppermute(down, axis, [(i + 1, i) for i in range(count - 1)])
    return low, high


def side_lanes(ext, place_z):
    half = jnp.where(place_z == 0, ext[..., SZ - SIDE : SZ], ext[..., 0:SIDE])
    return lax.ppermute(half, "gz", [(0, 1), (1, 0)])


def body(displacement, physical, design, passive, supports):
    assert design.shape == (SX, SY, SZ) and lax.axis_size("gz") == 2
    sizes = [lax.axis_size(axis) for axis in ("gx", "gy", "gz")]
    extents = (SX * sizes[0], SY * sizes[1], SZ * sizes[2])
    place_z = lax.axis_index("gz")
    place = jnp.stack([lax.axis_index("gx"), lax.axis_index("gy"), place_z]).astype(jnp.int32)

    fields = jnp.concatenate([displacement, physical[None]], axis=0)
    x_low, x_high = exchange(fields[:, SX - 2 :], fields[:, 0:3], "gx")

    frame = (SX + 4, ROWS, LANES)
    inverse, volume_weight, marks = call(
        functools.partial(weights_kernel, extents=extents), 1, 1,
        [frame, (SX, SY, SZ), (SX, SY, SZ)], [frame, frame], 10**7,
    )(place, supports.reshape(1, -1))

    wide = jnp.concatenate([x_low, fields, x_high], axis=1)
    y_low, y_high = exchange(wide[:, :, SY - 2 :], wide[:, :, 0:3], "gy")
    filler = jnp.zeros((4, SX + 5, 3, SZ), F32)
    side = side_lanes(jnp.concatenate([wide, y_high, filler, y_low], axis=2), place_z)
    bounds, up, down = call(
        functools.partial(design_kernel, squares=energy_squares()), 1, 11,
        [(3, SX, SY, SZ), (3, 3, SY, SZ), (3, 2, SY, SZ)], [(4, SX + 5, ROWS, LANES), frame, frame, frame], 10**7,
    )(place, displacement, physical, x_low, x_high, y_low, y_high, side, inverse, volume_weight, design, passive)

    x_low, x_high = exchange(up, down, "gx")
    multipliers = log_lower + (log_upper - log_lower) / POINTS * np.arange(1, POINTS + 1)
    table = jnp.asarray(np.exp(-0.5 * multipliers), F32)
    inner, outer = sizes[1] * sizes[2], sizes[0]
    (part,) = call(
        volumes_kernel, 1, 2, [(inner, 8, 128)], [(3, 2 * SX, SY, 128), (POINTS, 128)], 10**8,
    )(table, bounds, volume_weight)
    part = lax.all_to_all(part, ("gy", "gz"), 0, 0, tiled=True)
    wide = jnp.concatenate([x_low, bounds, x_high], axis=1)
    y_low, y_high = exchange(wide[:, :, SY - 3 :], wide[:, :, 0:2], "gy")
    (part,) = call(repeat_kernel, 0, 1, [(outer, 8, 128)], [], 10**5)(part)
    part = lax.all_to_all(part, "gx", 0, 0, tiled=True)
    filler = jnp.zeros((3, SX + 5, 3, SZ), F32)
    side = side_lanes(jnp.concatenate([wide, y_high, filler, y_low], axis=2), place_z)

    ext = (SX + 5, ROWS, LANES)
    new_design, new_physical, node_blocks = call(
        functools.partial(
            final_kernel, factors=[float(f) for f in corner_factors()],
            target=volume_share * (extents[0] * extents[1] * extents[2]),
        ), 1, 9,
        [(SX, SY, SZ), (SX, SY, SZ), (6, SX, SY, SZ)], [(3,) + ext, ext, ext, (SX + 1, ROWS, LANES)], 10**7,
    )(place, part, bounds, x_low, x_high, y_low, y_high, side, inverse, marks)
    return (new_design, new_physical, node_blocks)


def solution(mesh):
    in_specs = (
        P(None, "gx", "gy", "gz"),
        P("gx", "gy", "gz"),
        P("gx", "gy", "gz"),
        P("gx", "gy", "gz"),
        P(),
    )
    out_specs = (P("gx", "gy", "gz"), P("gx", "gy", "gz"), P(None, "gx", "gy", "gz"))
    return jax.shard_map(body, mesh=mesh, in_specs=in_specs, out_specs=out_specs, check_vma=False)
```

```python
import functools
import math

import jax
import jax.numpy as jnp
import numpy as np
from jax import lax
from jax.experimental import pallas as pl
from jax.experimental.pallas import tpu as pltpu
from jax.sharding import PartitionSpec as P

STEPS = 10

filter_radius = 2.5
penalty = 3.0
move_limit = 0.2
stiff_floor = 1e-09
volume_share = 0.5
log_lower = -20.0
log_upper = 20.0
poisson = 0.3

SX, SY, SZ = 8, 8, 256
ROWS, LANES, SIDE = 16, 384, 128
POINTS = 2**STEPS
F32 = jnp.float32


def corner_offsets():
    return [(q // 4, q // 2 % 2, q % 2) for q in range(8)]


def hex_stiffness():
    lame_first = poisson / ((1.0 + poisson) * (1.0 - 2.0 * poisson))
    shear_modulus = 0.5 / (1.0 + poisson)
    elastic = np.zeros((6, 6))
    elastic[:3, :3] = lame_first
    for d in range(3):
        elastic[d, d] += 2.0 * shear_modulus
        elastic[d + 3, d + 3] = shear_modulus
    corners = corner_offsets()
    points = [0.5 - 0.5 / math.sqrt(3.0), 0.5 + 0.5 / math.sqrt(3.0)]
    matrix = np.zeros((24, 24))
    for p in points:
        for q in points:
            for r in points:
                location = [p, q, r]
                gradients = np.zeros((8, 3))
                for n in range(8):
                    factors = [
                        location[e] if corners[n][e] == 1 else 1.0 - location[e] for e in range(3)
                    ]
                    for d in range(3):
                        sign_value = 1.0 if corners[n][d] == 1 else -1.0
                        gradients[n, d] = sign_value * factors[(d + 1) % 3] * factors[(d + 2) % 3]
                strain = np.zeros((6, 24))
                for n in range(8):
                    column = 3 * n
                    strain[0, column] = gradients[n, 0]
                    strain[1, column + 1] = gradients[n, 1]
                    strain[2, column + 2] = gradients[n, 2]
                    strain[3, column + 1] = gradients[n, 2]
                    strain[3, column + 2] = gradients[n, 1]
                    strain[4, column] = gradients[n, 2]
                    strain[4, column + 2] = gradients[n, 0]
                    strain[5, column] = gradients[n, 1]
                    strain[5, column + 1] = gradients[n, 0]
                matrix += strain.T @ elastic @ strain / 8.0
    return matrix


def energy_squares():
    corners = corner_offsets()
    modes = np.zeros((24, 24))
    for s in range(8):
        bits = (s // 4, s // 2 % 2, s % 2)
        for n in range(8):
            sign_value = 1.0
            for e in range(3):
                if bits[e] == 1 and corners[n][e] == 0:
                    sign_value = -sign_value
            for d in range(3):
                modes[3 * n + d, 3 * s + d] = sign_value
    form = modes.T @ hex_stiffness() @ modes / 64.0
    used = np.zeros((24, 24))
    squares = []
    for parity in range(8):
        members = [3 * (parity ^ (4, 2, 1)[d]) + d for d in range(3)]
        block = form[np.ix_(members, members)].copy()
        used[np.ix_(members, members)] = block
        for r in range(3):
            if block[r, r] < 1e-9:
                continue
            factors = block[r] / math.sqrt(block[r, r])
            block -= np.outer(factors, factors)
            squares.append([(members[c], factors[c]) for c in range(3) if abs(factors[c]) > 1e-9])
        assert np.abs(block).max() < 1e-9
    assert np.abs(used - form).max() < 1e-9
    return squares


def corner_factors():
    matrix = hex_stiffness()
    factors = (matrix[0, 0], matrix[1, 2], matrix[0, 2], matrix[0, 1])
    for n, corner in enumerate(corner_offsets()):
        sign = [1.0 if c == 1 else -1.0 for c in corner]
        block = matrix[3 * n : 3 * n + 3, 3 * n : 3 * n + 3]
        assert np.allclose(np.diag(block), factors[0])
        assert np.allclose(block[1, 2], factors[1] * sign[1] * sign[2])
        assert np.allclose(block[0, 2], factors[2] * sign[0] * sign[2])
        assert np.allclose(block[0, 1], factors[3] * sign[0] * sign[1])
    return factors


def tap(square):
    return max(0.0, filter_radius - math.sqrt(square))


def rolled(value, steps, dim):
    return pltpu.roll(value, (-steps) % value.shape[dim], dim)


def row_pairs(plane):
    return (
        rolled(plane, 1, 0) + rolled(plane, -1, 0),
        rolled(plane, 2, 0) + rolled(plane, -2, 0),
    )


def filtered_plane(plane_of, near_of, far_of, p):
    ring_0 = plane_of(p)
    ring_1 = near_of(p) + plane_of(p - 1) + plane_of(p + 1)
    ring_2 = near_of(p - 1) + near_of(p + 1)
    ring_4 = far_of(p) + plane_of(p - 2) + plane_of(p + 2)
    ring_5 = far_of(p - 1) + far_of(p + 1) + near_of(p - 2) + near_of(p + 2)
    layers = []
    for c in (0, 1, 2):
        total = None
        for square, ring in ((0, ring_0), (1, ring_1), (2, ring_2), (4, ring_4), (5, ring_5)):
            weight = tap(square + c * c)
            if weight > 0.0:
                total = weight * ring if total is None else total + weight * ring
        layers.append(total)
    middle, near, far = layers
    return middle + (rolled(near, 1, 1) + rolled(near, -1, 1)) + (rolled(far, 2, 1) + rolled(far, -2, 1))


def weights_kernel(place_ref, support_ref, inverse_ref, volume_ref, mark_ref, near_ref, far_ref, *, extents):
    total_x, total_y, total_z = extents
    first_x = place_ref[0] * SX
    first_y = place_ref[1] * SY
    first_z = place_ref[2] * SZ
    row = lax.broadcasted_iota(jnp.int32, (ROWS, LANES), 0)
    lane = lax.broadcasted_iota(jnp.int32, (ROWS, LANES), 1)
    y = first_y + jnp.where(row < 12, row, row - ROWS)
    z = first_z + jnp.where(lane < SZ + SIDE // 2, lane, lane - LANES)
    inside = jnp.where((y >= 0) & (y < total_y) & (z >= 0) & (z < total_z), 1.0, 0.0).astype(F32)
    near, far = row_pairs(inside)

    def present(p):
        x = first_x + p
        return jnp.where((x >= 0) & (x < total_x), 1.0, 0.0).astype(F32)

    for p in range(SX + 4):
        x = p - 2
        weight_sum = filtered_plane(
            lambda q: inside * present(q), lambda q: near * present(q), lambda q: far * present(q), x
        )
        here = inside * present(x)
        inverse = jnp.where(here > 0.0, 1.0 / jnp.where(here > 0.0, weight_sum, 1.0), 0.0)
        inverse_ref[p] = inverse
        inverse_near, inverse_far = row_pairs(inverse)
        near_ref[p] = inverse_near
        far_ref[p] = inverse_far
    for p in range(SX):
        volume = filtered_plane(
            lambda q: inverse_ref[q, 0:SY], lambda q: near_ref[q, 0:SY], lambda q: far_ref[q, 0:SY], p + 2
        )
        volume_ref[p] = volume[:, 0:SZ]
    node = support_ref[...]
    node_x = node // (total_y * total_z) - first_x
    node_y = node // total_z % total_y - first_y
    node_z = node % total_z - first_z
    owned = (node_x >= 0) & (node_x < SX) & (node_y >= 0) & (node_y < SY)
    line = jnp.where(owned, node_x * SY + node_y, -1)
    count = node.shape[1]
    lines = jnp.where(lax.broadcasted_iota(jnp.int32, (SX * SY, count), 0) == line, 1.0, 0.0)
    lanes = jnp.where(lax.broadcasted_iota(jnp.int32, (SZ, count), 0) == node_z, 1.0, 0.0)
    hits = lax.dot_general(
        lines.astype(jnp.bfloat16),
        lanes.astype(jnp.bfloat16),
        (((1,), (1,)), ((), ())),
        preferred_element_type=F32,
    )
    for p in range(SX):
        mark_ref[p] = hits[p * SY : (p + 1) * SY]


def side_mask(first_z_index, upper, lower):
    lane = lax.broadcasted_iota(jnp.int32, (ROWS, SIDE), 1)
    start = jnp.where(first_z_index == 0, 0, SIDE - lower)
    stop = jnp.where(first_z_index == 0, upper, SIDE)
    return (lane >= start) & (lane < stop)


def assemble(ext_ref, fields, low, high, up_rows, low_rows, own, x_low, x_high, y_low, y_high, side, keep):
    planes = low + SX + high
    for f in range(fields):
        for p in range(planes):
            if p < low:
                middle = x_low[f, p]
            elif p < low + SX:
                middle = own(f, p - low)
            else:
                middle = x_high[f, p - low - SX]
            ext_ref[f, p, 0:SY, 0:SZ] = middle
            filler = jnp.zeros((SY - up_rows - low_rows, SZ), F32)
            ext_ref[f, p, SY:ROWS, 0:SZ] = jnp.concatenate([y_high[f, p], filler, y_low[f, p]], axis=0)
            ext_ref[f, p, :, SZ:LANES] = jnp.where(keep, side[f, p], 0.0)


def design_kernel(
    place_ref, shift_ref, physical_ref, x_low, x_high, y_low, y_high, side, inverse_ref, volume_ref, design_ref,
    passive_ref, out_ref, up_ref, down_ref, ext_ref, sens_ref, near_ref, far_ref, *, squares
):
    keep = side_mask(place_ref[2], 3, 2)
    assemble(
        ext_ref, 4, 2, 3, 3, 2, lambda f, p: shift_ref[f, p] if f < 3 else physical_ref[p],
        x_low, x_high, y_low, y_high, side, keep,
    )
    scale = penalty * (1.0 - stiff_floor)

    @pl.loop(0, SX + 4)
    def _(p):
        modes = {}
        for d in range(3):
            here, above = ext_ref[d, p], ext_ref[d, p + 1]
            for a, along_x in enumerate((here + above, above - here)):
                beyond = rolled(along_x, 1, 0)
                for b, along_y in enumerate((along_x + beyond, beyond - along_x)):
                    next_lane = rolled(along_y, 1, 1)
                    for c, mode in enumerate((along_y + next_lane, next_lane - along_y)):
                        modes[3 * (4 * a + 2 * b + c) + d] = mode
        energy = None
        for terms in squares:
            line = None
            for mode, factor in terms:
                term = float(factor) * modes[mode]
                line = term if line is None else line + term
            energy = line * line if energy is None else energy + line * line
        density = ext_ref[3, p]
        sens = scale * density * density * energy * inverse_ref[p]
        sens_ref[p] = sens
        near, far = row_pairs(sens)
        near_ref[p] = near
        far_ref[p] = far

    for p in range(SX):
        filtered = filtered_plane(
            lambda q: sens_ref[q, 0:SY], lambda q: near_ref[q, 0:SY], lambda q: far_ref[q, 0:SY], p + 2
        )[:, 0:SZ]
        design = design_ref[p]
        solid = passive_ref[p] == 1
        scaled = design * jnp.sqrt(filtered / volume_ref[p])
        floor_bound = jnp.where(solid, 1.0, jnp.maximum(0.0, design - move_limit))
        ceiling = jnp.where(solid, 1.0, jnp.minimum(1.0, design + move_limit))
        for f, value in enumerate((scaled, floor_bound, ceiling)):
            out_ref[f, p] = value
            if p < 3:
                down_ref[f, p] = value
            if p >= SX - 3:
                up_ref[f, p - (SX - 3)] = value


def volumes_kernel(exp_ref, bounds_ref, volume_ref, out_ref, weighted_ref, sums_ref):
    for p in range(SX):
        weight = volume_ref[p]
        for f in range(3):
            weighted = weight * bounds_ref[f, p]
            for h in range(2):
                weighted_ref[f, 2 * p + h] = weighted[:, h * 128 : (h + 1) * 128]

    @pl.loop(0, POINTS // 8)
    def _(g):
        factors = [exp_ref[g * 8 + j] for j in range(8)]
        totals = [None] * 8
        for v in range(2 * SX):
            scaled, floor_bound, ceiling = weighted_ref[0, v], weighted_ref[1, v], weighted_ref[2, v]
            for j in range(8):
                value = jnp.minimum(jnp.maximum(scaled * factors[j], floor_bound), ceiling)
                totals[j] = value if totals[j] is None else totals[j] + value
        rows = [jnp.sum(total, axis=0, keepdims=True) for total in totals]
        sums_ref[pl.ds(pl.multiple_of(g * 8, 8), 8), :] = jnp.concatenate(rows, axis=0)

    copies = out_ref.shape[0]
    result = lax.dot_general(
        jnp.ones((copies, 128), F32),
        sums_ref[...],
        (((1,), (1,)), ((), ())),
        precision=lax.Precision.HIGHEST,
        preferred_element_type=F32,
    )
    for i in range(8):
        out_ref[:, i, :] = result[:, i * 128 : (i + 1) * 128]


def repeat_kernel(part_ref, out_ref):
    total = part_ref[0]
    for i in range(1, part_ref.shape[0]):
        total = total + part_ref[i]
    for i in range(out_ref.shape[0]):
        out_ref[i] = total


def final_kernel(
    place_ref, part_ref, own_ref, x_low, x_high, y_low, y_high, side, inverse_ref, mark_ref, new_design_ref,
    new_physical_ref, blocks_ref, ext_ref, near_ref, far_ref, stiff_ref, *, factors, target
):
    total = part_ref[0]
    for i in range(1, part_ref.shape[0]):
        total = total + part_ref[i]
    low_end = jnp.minimum(jnp.sum(jnp.where(total > target, 1.0, 0.0)), POINTS - 1.0)
    multiplier = log_lower + (log_upper - log_lower) / POINTS * (low_end + 0.5)
    factor = jnp.exp(jnp.broadcast_to(-0.5 * multiplier, (ROWS, LANES)))
    keep = side_mask(place_ref[2], 2, 3)
    assemble(ext_ref, 3, 3, 2, 2, 3, lambda f, p: own_ref[f, p], x_low, x_high, y_low, y_high, side, keep)
    planes = SX + 5
    for p in range(planes):
        chosen = jnp.minimum(jnp.maximum(ext_ref[0, p] * factor, ext_ref[1, p]), ext_ref[2, p])
        ext_ref[0, p] = chosen
        near, far = row_pairs(chosen)
        near_ref[p] = near
        far_ref[p] = far
        if 3 <= p < SX + 3:
            new_design_ref[p - 3] = chosen[0:SY, 0:SZ]
    for p in range(SX + 1):
        inverse = inverse_ref[p + 1]
        density = (
            filtered_plane(lambda q: ext_ref[0, q], lambda q: near_ref[q], lambda q: far_ref[q], p + 2) * inverse
        )
        if p >= 1:
            new_physical_ref[p - 1] = density[0:SY, 0:SZ]
        cube = stiff_floor + density * density * density * (1.0 - stiff_floor)
        stiff_ref[p] = jnp.where(inverse > 0.0, cube, 0.0)
    for p in range(SX):
        below, here = stiff_ref[p], stiff_ref[p + 1]
        x_sum, x_diff = here + below, below - here
        x_sum_back, x_diff_back = rolled(x_sum, -1, 0), rolled(x_diff, -1, 0)
        sum_sum = (x_sum + x_sum_back)[0:SY]
        sum_diff = (x_sum_back - x_sum)[0:SY]
        diff_sum = (x_diff + x_diff_back)[0:SY]
        diff_diff = (x_diff_back - x_diff)[0:SY]
        marked = mark_ref[p] > 0.5
        even = factors[0] * (sum_sum + rolled(sum_sum, -1, 1))[:, 0:SZ]
        even = jnp.where(marked, 1.0, even)
        blocks_ref[0, p] = even
        blocks_ref[1, p] = even
        blocks_ref[2, p] = even
        yz = factors[1] * (rolled(sum_diff, -1, 1) - sum_diff)[:, 0:SZ]
        xz = factors[2] * (rolled(diff_sum, -1, 1) - diff_sum)[:, 0:SZ]
        xy = factors[3] * (diff_diff + rolled(diff_diff, -1, 1))[:, 0:SZ]
        blocks_ref[3, p] = jnp.where(marked, 0.0, yz)
        blocks_ref[4, p] = jnp.where(marked, 0.0, xz)
        blocks_ref[5, p] = jnp.where(marked, 0.0, xy)


def call(kernel, smem, vmem, shapes, scratch, flops):
    specs = [pl.BlockSpec(memory_space=pltpu.SMEM)] * smem + [pl.BlockSpec(memory_space=pltpu.VMEM)] * vmem
    outs = [jax.ShapeDtypeStruct(shape, F32) for shape in shapes]
    return pl.pallas_call(
        kernel,
        out_shape=outs,
        in_specs=specs,
        out_specs=[pl.BlockSpec(memory_space=pltpu.VMEM)] * len(outs),
        scratch_shapes=[pltpu.VMEM(shape, F32) for shape in scratch],
        compiler_params=pltpu.CompilerParams(vmem_limit_bytes=32 * 2**20),
        cost_estimate=pl.CostEstimate(flops=flops, bytes_accessed=10**6, transcendentals=0),
    )


def start_exchange(top, bottom, axis):
    count = lax.axis_size(axis)
    even = lax.axis_index(axis) % 2 == 0
    results = []
    for start, (first, second) in enumerate(((top, bottom), (bottom, top))):
        pairs = [(i, i + 1) for i in range(start, count - 1, 2)]
        moves = pairs + [(j, i) for i, j in pairs]
        results.append(lax.ppermute(jnp.where(even, first, second), axis, moves))
    return results


def end_exchange(results, axis):
    even = lax.axis_index(axis) % 2 == 0
    return jnp.where(even, results[1], results[0]), jnp.where(even, results[0], results[1])


def side_lanes(ext, place_z):
    half = jnp.where(place_z == 0, ext[..., SZ - SIDE : SZ], ext[..., 0:SIDE])
    return lax.ppermute(half, "gz", [(0, 1), (1, 0)])


def body(displacement, physical, design, passive, supports):
    assert design.shape == (SX, SY, SZ) and lax.axis_size("gz") == 2
    sizes = [lax.axis_size(axis) for axis in ("gx", "gy", "gz")]
    extents = (SX * sizes[0], SY * sizes[1], SZ * sizes[2])
    place_z = lax.axis_index("gz")
    place = jnp.stack([lax.axis_index("gx"), lax.axis_index("gy"), place_z]).astype(jnp.int32)

    fields = jnp.concatenate([displacement, physical[None]], axis=0)
    swaps = start_exchange(fields[:, SX - 3 :], fields[:, 0:3], "gx")

    frame = (SX + 4, ROWS, LANES)
    inverse, volume_weight, marks = call(
        functools.partial(weights_kernel, extents=extents), 1, 1,
        [frame, (SX, SY, SZ), (SX, SY, SZ)], [frame, frame], 10**7,
    )(place, supports.reshape(1, -1))
    swaps, inverse, volume_weight, marks = lax.optimization_barrier((swaps, inverse, volume_weight, marks))

    x_low, x_high = end_exchange(swaps, "gx")
    x_low = x_low[:, 1:]
    wide = jnp.concatenate([x_low, fields, x_high], axis=1)
    y_low, y_high = end_exchange(start_exchange(wide[:, :, SY - 3 :], wide[:, :, 0:3], "gy"), "gy")
    y_low = y_low[:, :, 1:]
    filler = jnp.zeros((4, SX + 5, 3, SZ), F32)
    side = side_lanes(jnp.concatenate([wide, y_high, filler, y_low], axis=2), place_z)
    bounds, up, down = call(
        functools.partial(design_kernel, squares=energy_squares()), 1, 11,
        [(3, SX, SY, SZ), (3, 3, SY, SZ), (3, 3, SY, SZ)], [(4, SX + 5, ROWS, LANES), frame, frame, frame], 10**7,
    )(place, displacement, physical, x_low, x_high, y_low, y_high, side, inverse, volume_weight, design, passive)

    swaps = start_exchange(up, down, "gx")
    multipliers = log_lower + (log_upper - log_lower) / POINTS * np.arange(1, POINTS + 1)
    table = jnp.asarray(np.exp(-0.5 * multipliers), F32)
    inner, outer = sizes[1] * sizes[2], sizes[0]
    (part,) = call(
        volumes_kernel, 1, 2, [(inner, 8, 128)], [(3, 2 * SX, SY, 128), (POINTS, 128)], 10**8,
    )(table, bounds, volume_weight)
    swaps, part = lax.optimization_barrier((swaps, part))
    x_low, x_high = end_exchange(swaps, "gx")
    x_high = x_high[:, 0:2]
    wide = jnp.concatenate([x_low, bounds, x_high], axis=1)
    swaps = start_exchange(wide[:, :, SY - 3 :], wide[:, :, 0:3], "gy")
    part = lax.all_to_all(part, ("gy", "gz"), 0, 0, tiled=True)
    swaps, part = lax.optimization_barrier((swaps, part))
    y_low, y_high = end_exchange(swaps, "gy")
    y_high = y_high[:, :, 0:2]
    filler = jnp.zeros((3, SX + 5, 3, SZ), F32)
    side = side_lanes(jnp.concatenate([wide, y_high, filler, y_low], axis=2), place_z)
    (part,) = call(repeat_kernel, 0, 1, [(outer, 8, 128)], [], 10**5)(part)
    part = lax.all_to_all(part, "gx", 0, 0, tiled=True)

    ext = (SX + 5, ROWS, LANES)
    new_design, new_physical, node_blocks = call(
        functools.partial(
            final_kernel, factors=[float(f) for f in corner_factors()],
            target=volume_share * (extents[0] * extents[1] * extents[2]),
        ), 1, 9,
        [(SX, SY, SZ), (SX, SY, SZ), (6, SX, SY, SZ)], [(3,) + ext, ext, ext, (SX + 1, ROWS, LANES)], 10**7,
    )(place, part, bounds, x_low, x_high, y_low, y_high, side, inverse, marks)
    return (new_design, new_physical, node_blocks)


def solution(mesh):
    in_specs = (
        P(None, "gx", "gy", "gz"),
        P("gx", "gy", "gz"),
        P("gx", "gy", "gz"),
        P("gx", "gy", "gz"),
        P(),
    )
    out_specs = (P("gx", "gy", "gz"), P("gx", "gy", "gz"), P(None, "gx", "gy", "gz"))
    return jax.shard_map(body, mesh=mesh, in_specs=in_specs, out_specs=out_specs, check_vma=False)
```

```python
import functools
import math

import jax
import jax.numpy as jnp
import numpy as np
from jax import lax
from jax.experimental import pallas as pl
from jax.experimental.pallas import tpu as pltpu
from jax.sharding import PartitionSpec as P

STEPS = 10

filter_radius = 2.5
penalty = 3.0
move_limit = 0.2
stiff_floor = 1e-09
volume_share = 0.5
log_lower = -20.0
log_upper = 20.0
poisson = 0.3

SX, SY, SZ = 8, 8, 256
ROWS, LANES, SIDE = 16, 384, 128
NODES, ELEMENTS, CHOSEN = SX + 10, SX + 9, SX + 5
POINTS = 2**STEPS
F32 = jnp.float32


def corner_offsets():
    return [(q // 4, q // 2 % 2, q % 2) for q in range(8)]


def hex_stiffness():
    lame_first = poisson / ((1.0 + poisson) * (1.0 - 2.0 * poisson))
    shear_modulus = 0.5 / (1.0 + poisson)
    elastic = np.zeros((6, 6))
    elastic[:3, :3] = lame_first
    for d in range(3):
        elastic[d, d] += 2.0 * shear_modulus
        elastic[d + 3, d + 3] = shear_modulus
    corners = corner_offsets()
    points = [0.5 - 0.5 / math.sqrt(3.0), 0.5 + 0.5 / math.sqrt(3.0)]
    matrix = np.zeros((24, 24))
    for p in points:
        for q in points:
            for r in points:
                location = [p, q, r]
                gradients = np.zeros((8, 3))
                for n in range(8):
                    factors = [
                        location[e] if corners[n][e] == 1 else 1.0 - location[e] for e in range(3)
                    ]
                    for d in range(3):
                        sign_value = 1.0 if corners[n][d] == 1 else -1.0
                        gradients[n, d] = sign_value * factors[(d + 1) % 3] * factors[(d + 2) % 3]
                strain = np.zeros((6, 24))
                for n in range(8):
                    column = 3 * n
                    strain[0, column] = gradients[n, 0]
                    strain[1, column + 1] = gradients[n, 1]
                    strain[2, column + 2] = gradients[n, 2]
                    strain[3, column + 1] = gradients[n, 2]
                    strain[3, column + 2] = gradients[n, 1]
                    strain[4, column] = gradients[n, 2]
                    strain[4, column + 2] = gradients[n, 0]
                    strain[5, column] = gradients[n, 1]
                    strain[5, column + 1] = gradients[n, 0]
                matrix += strain.T @ elastic @ strain / 8.0
    return matrix


def energy_squares():
    corners = corner_offsets()
    modes = np.zeros((24, 24))
    for s in range(8):
        bits = (s // 4, s // 2 % 2, s % 2)
        for n in range(8):
            sign_value = 1.0
            for e in range(3):
                if bits[e] == 1 and corners[n][e] == 0:
                    sign_value = -sign_value
            for d in range(3):
                modes[3 * n + d, 3 * s + d] = sign_value
    form = modes.T @ hex_stiffness() @ modes / 64.0
    used = np.zeros((24, 24))
    squares = []
    for parity in range(8):
        members = [3 * (parity ^ (4, 2, 1)[d]) + d for d in range(3)]
        block = form[np.ix_(members, members)].copy()
        used[np.ix_(members, members)] = block
        for r in range(3):
            if block[r, r] < 1e-9:
                continue
            factors = block[r] / math.sqrt(block[r, r])
            block -= np.outer(factors, factors)
            squares.append([(members[c], factors[c]) for c in range(3) if abs(factors[c]) > 1e-9])
        assert np.abs(block).max() < 1e-9
    assert np.abs(used - form).max() < 1e-9
    return squares


def corner_factors():
    matrix = hex_stiffness()
    factors = (matrix[0, 0], matrix[1, 2], matrix[0, 2], matrix[0, 1])
    for n, corner in enumerate(corner_offsets()):
        sign = [1.0 if c == 1 else -1.0 for c in corner]
        block = matrix[3 * n : 3 * n + 3, 3 * n : 3 * n + 3]
        assert np.allclose(np.diag(block), factors[0])
        assert np.allclose(block[1, 2], factors[1] * sign[1] * sign[2])
        assert np.allclose(block[0, 2], factors[2] * sign[0] * sign[2])
        assert np.allclose(block[0, 1], factors[3] * sign[0] * sign[1])
    return factors


def tap(square):
    return max(0.0, filter_radius - math.sqrt(square))


def rolled(value, steps, dim):
    return pltpu.roll(value, (-steps) % value.shape[dim], dim)


def row_pairs(plane):
    return (
        rolled(plane, 1, 0) + rolled(plane, -1, 0),
        rolled(plane, 2, 0) + rolled(plane, -2, 0),
    )


def filtered_plane(plane_of, near_of, far_of, p):
    ring_0 = plane_of(p)
    ring_1 = near_of(p) + plane_of(p - 1) + plane_of(p + 1)
    ring_2 = near_of(p - 1) + near_of(p + 1)
    ring_4 = far_of(p) + plane_of(p - 2) + plane_of(p + 2)
    ring_5 = far_of(p - 1) + far_of(p + 1) + near_of(p - 2) + near_of(p + 2)
    layers = []
    for c in (0, 1, 2):
        total = None
        for square, ring in ((0, ring_0), (1, ring_1), (2, ring_2), (4, ring_4), (5, ring_5)):
            weight = tap(square + c * c)
            if weight > 0.0:
                total = weight * ring if total is None else total + weight * ring
        layers.append(total)
    middle, near, far = layers
    return middle + (rolled(near, 1, 1) + rolled(near, -1, 1)) + (rolled(far, 2, 1) + rolled(far, -2, 1))


def weights_kernel(place_ref, support_ref, inverse_ref, volume_ref, mark_ref, near_ref, far_ref, *, extents):
    total_x, total_y, total_z = extents
    first_x = place_ref[0] * SX
    first_y = place_ref[1] * SY
    first_z = place_ref[2] * SZ
    row = lax.broadcasted_iota(jnp.int32, (ROWS, LANES), 0)
    lane = lax.broadcasted_iota(jnp.int32, (ROWS, LANES), 1)
    y = first_y + jnp.where(row < 12, row, row - ROWS)
    z = first_z + jnp.where(lane < SZ + SIDE // 2, lane, lane - LANES)
    inside = jnp.where((y >= 0) & (y < total_y) & (z >= 0) & (z < total_z), 1.0, 0.0).astype(F32)
    near, far = row_pairs(inside)

    def present(p):
        x = first_x + p
        return jnp.where((x >= 0) & (x < total_x), 1.0, 0.0).astype(F32)

    for p in range(ELEMENTS):
        x = p - 5
        weight_sum = filtered_plane(
            lambda q: inside * present(q), lambda q: near * present(q), lambda q: far * present(q), x
        )
        here = inside * present(x)
        inverse = jnp.where(here > 0.0, 1.0 / jnp.where(here > 0.0, weight_sum, 1.0), 0.0)
        inverse_ref[p] = inverse
        inverse_near, inverse_far = row_pairs(inverse)
        near_ref[p] = inverse_near[0:SY]
        far_ref[p] = inverse_far[0:SY]
    for p in range(CHOSEN):
        volume_ref[p] = filtered_plane(
            lambda q: inverse_ref[q, 0:SY], lambda q: near_ref[q], lambda q: far_ref[q], p + 2
        )
    node = support_ref[...]
    node_x = node // (total_y * total_z) - first_x
    node_y = node // total_z % total_y - first_y
    node_z = node % total_z - first_z
    owned = (node_x >= 0) & (node_x < SX) & (node_y >= 0) & (node_y < SY)
    line = jnp.where(owned, node_x * SY + node_y, -1)
    count = node.shape[1]
    lines = jnp.where(lax.broadcasted_iota(jnp.int32, (SX * SY, count), 0) == line, 1.0, 0.0)
    lanes = jnp.where(lax.broadcasted_iota(jnp.int32, (SZ, count), 0) == node_z, 1.0, 0.0)
    hits = lax.dot_general(
        lines.astype(jnp.bfloat16),
        lanes.astype(jnp.bfloat16),
        (((1,), (1,)), ((), ())),
        preferred_element_type=F32,
    )
    for p in range(SX):
        mark_ref[p] = hits[p * SY : (p + 1) * SY]


def is_even(place_ref, axis):
    return place_ref[axis] % 2 == 0


def place_pair(even, first_ref, second_ref, top, bottom, place):
    first_ref[place] = jnp.where(even, top, bottom)
    second_ref[place] = jnp.where(even, bottom, top)


def low_high(even, first_ref, second_ref, place):
    first, second = first_ref[place], second_ref[place]
    return jnp.where(even, second, first), jnp.where(even, first, second)


def row_tile(even, first_ref, second_ref, plane):
    low, high = low_high(even, first_ref, second_ref, slice(3 * plane, 3 * plane + 3))
    return jnp.concatenate([high, jnp.zeros((SY - 6, low.shape[1]), F32), low], axis=0)


def faces_x_kernel(place_ref, shift_ref, physical_ref, design_ref, passive_ref, first_ref, second_ref):
    even = is_even(place_ref, 0)
    fields = [shift_ref.at[0], shift_ref.at[1], shift_ref.at[2], physical_ref]
    for f, field in enumerate(fields):
        place_pair(even, first_ref, second_ref, field[SX - 5 :], field[0:5], slice(5 * f, 5 * f + 5))
    for f, field in enumerate((design_ref, passive_ref)):
        top, bottom = field[SX - 3 :].astype(F32), field[0:3].astype(F32)
        place_pair(even, first_ref, second_ref, top, bottom, slice(20 + 3 * f, 23 + 3 * f))


def plane_reader(even, shift_ref, physical_ref, design_ref, passive_ref, x_first, x_second):
    def read(index):
        if index < 4 * NODES:
            f, x, depth, base = index // NODES, index % NODES - 5, 5, 5 * (index // NODES)
        else:
            f, x = divmod(index - 4 * NODES, CHOSEN)
            f, x, depth, base = f + 4, x - 3, 3, 20 + 3 * f
        if 0 <= x < SX:
            if f < 3:
                return shift_ref[f, x]
            return (physical_ref, design_ref, passive_ref)[f - 3][x].astype(F32)
        low, high = low_high(even, x_first, x_second, base + (x + depth if x < 0 else x - SX))
        return low if x < 0 else high

    return read


def faces_y_kernel(
    place_ref, shift_ref, physical_ref, design_ref, passive_ref, x_first, x_second, first_ref, second_ref, side_ref
):
    even = is_even(place_ref, 1)
    lower_core = place_ref[2] == 0
    read = plane_reader(
        is_even(place_ref, 0), shift_ref, physical_ref, design_ref, passive_ref, x_first, x_second
    )
    for index in range(4 * NODES + 2 * CHOSEN):
        plane = read(index)
        if index < 4 * NODES:
            rows = slice(3 * index, 3 * index + 3)
            place_pair(even, first_ref, second_ref, plane[SY - 3 :], plane[0:3], rows)
        side_ref[index] = jnp.where(lower_core, plane[:, SZ - SIDE :], plane[:, 0:SIDE])


def faces_z_kernel(place_ref, y_first, y_second, side_ref):
    even = is_even(place_ref, 1)
    lower_core = place_ref[2] == 0
    for index in range(4 * NODES):
        tile = row_tile(even, y_first, y_second, index)
        side_ref[index] = jnp.where(lower_core, tile[:, SZ - SIDE :], tile[:, 0:SIDE])


def design_kernel(
    place_ref, shift_ref, physical_ref, design_ref, passive_ref, x_first, x_second, y_first, y_second, side,
    y_side, inverse_ref, volume_ref, out_ref, first_ref, second_ref, ext_ref, sens_ref, near_ref, far_ref, *, squares
):
    lane = lax.broadcasted_iota(jnp.int32, (SY, SIDE), 1)
    start = place_ref[2] * (SIDE // 2)
    keep = (lane >= start) & (lane < start + SIDE // 2)
    even = is_even(place_ref, 1)
    read = plane_reader(
        is_even(place_ref, 0), shift_ref, physical_ref, design_ref, passive_ref, x_first, x_second
    )
    for f in range(4):
        for p in range(NODES):
            index = NODES * f + p
            ext_ref[f, p, 0:SY, 0:SZ] = read(index)
            ext_ref[f, p, 0:SY, SZ:LANES] = jnp.where(keep, side[index], 0.0)
            ext_ref[f, p, SY:ROWS, 0:SZ] = row_tile(even, y_first, y_second, index)
            ext_ref[f, p, SY:ROWS, SZ:LANES] = jnp.where(keep, y_side[index], 0.0)
    scale = penalty * (1.0 - stiff_floor)

    @pl.loop(0, ELEMENTS)
    def _(p):
        modes = {}
        for d in range(3):
            here, above = ext_ref[d, p], ext_ref[d, p + 1]
            for a, along_x in enumerate((here + above, above - here)):
                beyond = rolled(along_x, 1, 0)
                for b, along_y in enumerate((along_x + beyond, beyond - along_x)):
                    next_lane = rolled(along_y, 1, 1)
                    for c, mode in enumerate((along_y + next_lane, next_lane - along_y)):
                        modes[3 * (4 * a + 2 * b + c) + d] = mode
        energy = None
        for terms in squares:
            line = None
            for mode, factor in terms:
                term = float(factor) * modes[mode]
                line = term if line is None else line + term
            energy = line * line if energy is None else energy + line * line
        density = ext_ref[3, p]
        sens = scale * density * density * energy * inverse_ref[p]
        sens_ref[p] = sens[0:SY]
        near, far = row_pairs(sens)
        near_ref[p] = near[0:SY]
        far_ref[p] = far[0:SY]

    for p in range(CHOSEN):
        filtered = filtered_plane(lambda q: sens_ref[q], lambda q: near_ref[q], lambda q: far_ref[q], p + 2)
        index = 4 * NODES + p
        design = jnp.concatenate([read(index), side[index]], axis=1)
        solid = jnp.concatenate([read(index + CHOSEN), side[index + CHOSEN]], axis=1) > 0.5
        inside = inverse_ref[p + 2, 0:SY] > 0.0
        scaled = design * jnp.sqrt(filtered / jnp.where(inside, volume_ref[p], 1.0))
        floor_bound = jnp.where(solid, 1.0, jnp.maximum(0.0, design - move_limit))
        ceiling = jnp.where(solid, 1.0, jnp.minimum(1.0, design + move_limit))
        for f, value in enumerate((scaled, floor_bound, ceiling)):
            value = jnp.where(inside, value, 0.0)
            out_ref[f, p] = value
            row = 3 * (CHOSEN * f + p)
            place_pair(even, first_ref, second_ref, value[SY - 3 :], value[0:3], slice(row, row + 3))


def three_parts(value):
    first = value.astype(jnp.bfloat16).astype(F32)
    second = (value - first).astype(jnp.bfloat16).astype(F32)
    return first, second, value - first - second


def volumes_kernel(bounds_ref, volume_ref, out_ref, high_ref, low_ref, value_ref):
    step = (log_upper - log_lower) / POINTS
    ceilings = jnp.zeros((SY, 128), F32)
    for v in range(2 * SX):
        place = (3 + v // 2, slice(None), slice(128 * (v % 2), 128 * (v % 2 + 1)))
        weight = volume_ref[place]
        scaled, floor_bound, ceiling = [bounds_ref[(f,) + place] for f in range(3)]
        ceilings = ceilings + weight * ceiling
        log_scaled = jnp.log(jnp.maximum(scaled, 1e-30))
        for t, bound in enumerate((ceiling, floor_bound)):
            reached = (2.0 * (log_scaled - jnp.log(jnp.maximum(bound, 1e-30))) - log_lower) / step
            index = jnp.minimum(jnp.maximum(jnp.ceil(reached), 1.0), POINTS + 1.0) - 1.0
            index = jnp.where(bound > 0.0, index, float(POINTS))
            high = jnp.floor(index * (1.0 / 128.0))
            high_ref[t, v] = high
            low_ref[t, v] = index - 128.0 * high
            sign = -1.0 if t == 0 else 1.0
            parts = three_parts(sign * weight * bound) + three_parts(-sign * weight * scaled)
            for n, part in enumerate(parts):
                value_ref[t, n, v] = part

    rows = lax.broadcasted_iota(jnp.int32, (8, 128), 0).astype(F32)
    columns = lax.broadcasted_iota(jnp.int32, (128, 128), 0).astype(F32)

    def add_group(v, total):
        lefts, rights = [], []
        for t in range(2):
            for r in range(SY):
                hit = rows == high_ref[t, v, r : r + 1, :]
                left = [jnp.where(hit, value_ref[t, n, v, r : r + 1, :], 0.0) for n in range(6)]
                lefts.append(jnp.concatenate(left, axis=0).astype(jnp.bfloat16))
                right = jnp.where(columns == low_ref[t, v, r : r + 1, :], 1.0, 0.0)
                rights.append(right.astype(jnp.bfloat16))
        return total + lax.dot_general(
            jnp.concatenate(lefts, axis=1),
            jnp.concatenate(rights, axis=1),
            (((1,), (1,)), ((), ())),
            preferred_element_type=F32,
        )

    total = lax.fori_loop(0, 2 * SX, add_group, jnp.zeros((48, 128), F32))
    constant = total[0:8] + total[8:16] + total[16:24]
    slope = total[24:32] + total[32:40] + total[40:48]
    upto = jnp.where(
        lax.broadcasted_iota(jnp.int32, (128, 128), 0) <= lax.broadcasted_iota(jnp.int32, (128, 128), 1), 1.0, 0.0
    )
    running = lax.dot_general(
        jnp.concatenate([constant, slope], axis=0),
        upto,
        (((1,), (0,)), ((), ())),
        precision=lax.Precision.HIGHEST,
        preferred_element_type=F32,
    )
    row = lax.broadcasted_iota(jnp.int32, (8, 128), 0)
    lane = lax.broadcasted_iota(jnp.int32, (8, 128), 1)
    cumulated = []
    for part in (running[0:8], running[8:16]):
        ends = jnp.broadcast_to(part[:, 127:128], (8, 128))
        before = ends
        for shift in (1, 2, 4):
            before = before + jnp.where(row >= shift, rolled(before, -shift, 0), 0.0)
        cumulated.append(part + (before - ends))
    index = (row * 128 + lane + 1).astype(F32)
    factor = jnp.exp(-0.5 * (log_lower + step * index))
    result = jnp.sum(ceilings) + cumulated[0] + factor * cumulated[1]
    for i in range(out_ref.shape[0]):
        out_ref[i] = result


def repeat_kernel(part_ref, out_ref):
    total = part_ref[0]
    for i in range(1, part_ref.shape[0]):
        total = total + part_ref[i]
    for i in range(out_ref.shape[0]):
        out_ref[i] = total


def final_kernel(
    place_ref, part_ref, own_ref, y_first, y_second, inverse_ref, mark_ref, new_design_ref, new_physical_ref,
    blocks_ref, chosen_ref, near_ref, far_ref, stiff_ref, *, factors, target
):
    total = part_ref[0]
    for i in range(1, part_ref.shape[0]):
        total = total + part_ref[i]
    low_end = jnp.minimum(jnp.sum(jnp.where(total > target, 1.0, 0.0)), POINTS - 1.0)
    multiplier = log_lower + (log_upper - log_lower) / POINTS * (low_end + 0.5)
    factor = jnp.exp(jnp.broadcast_to(-0.5 * multiplier, (SY, LANES)))
    even = is_even(place_ref, 1)
    for p in range(CHOSEN):
        tiles = []
        own = [own_ref[f, p] for f in range(3)]
        beside = [row_tile(even, y_first, y_second, CHOSEN * f + p) for f in range(3)]
        for scaled, floor_bound, ceiling in (own, beside):
            tiles.append(jnp.minimum(jnp.maximum(scaled * factor, floor_bound), ceiling))
        chosen = jnp.concatenate(tiles, axis=0)
        chosen_ref[p] = chosen
        near, far = row_pairs(chosen)
        near_ref[p] = near
        far_ref[p] = far
        if 3 <= p < SX + 3:
            new_design_ref[p - 3] = tiles[0][:, 0:SZ]
    for p in range(SX + 1):
        inverse = inverse_ref[p + 4]
        density = (
            filtered_plane(lambda q: chosen_ref[q], lambda q: near_ref[q], lambda q: far_ref[q], p + 2) * inverse
        )
        if p >= 1:
            new_physical_ref[p - 1] = density[0:SY, 0:SZ]
        cube = stiff_floor + density * density * density * (1.0 - stiff_floor)
        stiff_ref[p] = jnp.where(inverse > 0.0, cube, 0.0)
    for p in range(SX):
        below, here = stiff_ref[p], stiff_ref[p + 1]
        x_sum, x_diff = here + below, below - here
        x_sum_back, x_diff_back = rolled(x_sum, -1, 0), rolled(x_diff, -1, 0)
        sum_sum = (x_sum + x_sum_back)[0:SY]
        sum_diff = (x_sum_back - x_sum)[0:SY]
        diff_sum = (x_diff + x_diff_back)[0:SY]
        diff_diff = (x_diff_back - x_diff)[0:SY]
        marked = mark_ref[p] > 0.5
        even = factors[0] * (sum_sum + rolled(sum_sum, -1, 1))[:, 0:SZ]
        even = jnp.where(marked, 1.0, even)
        blocks_ref[0, p] = even
        blocks_ref[1, p] = even
        blocks_ref[2, p] = even
        yz = factors[1] * (rolled(sum_diff, -1, 1) - sum_diff)[:, 0:SZ]
        xz = factors[2] * (rolled(diff_sum, -1, 1) - diff_sum)[:, 0:SZ]
        xy = factors[3] * (diff_diff + rolled(diff_diff, -1, 1))[:, 0:SZ]
        blocks_ref[3, p] = jnp.where(marked, 0.0, yz)
        blocks_ref[4, p] = jnp.where(marked, 0.0, xz)
        blocks_ref[5, p] = jnp.where(marked, 0.0, xy)


def call(kernel, smem, vmem, shapes, scratch, flops):
    specs = [pl.BlockSpec(memory_space=pltpu.SMEM)] * smem + [pl.BlockSpec(memory_space=pltpu.VMEM)] * vmem
    outs = [jax.ShapeDtypeStruct(shape, F32) for shape in shapes]
    return pl.pallas_call(
        kernel,
        out_shape=outs,
        in_specs=specs,
        out_specs=[pl.BlockSpec(memory_space=pltpu.VMEM)] * len(outs),
        scratch_shapes=[pltpu.VMEM(shape, F32) for shape in scratch],
        compiler_params=pltpu.CompilerParams(vmem_limit_bytes=32 * 2**20),
        cost_estimate=pl.CostEstimate(flops=flops, bytes_accessed=10**6, transcendentals=0),
    )


def exchange(first, second, axis):
    count = lax.axis_size(axis)
    results = []
    for start, faces in enumerate((first, second)):
        pairs = [(i, i + 1) for i in range(start, count - 1, 2)]
        results.append(lax.ppermute(faces, axis, pairs + [(j, i) for i, j in pairs]))
    return results


def other_core(values):
    return lax.ppermute(values, "gz", [(0, 1), (1, 0)])


def body(displacement, physical, design, passive, supports):
    assert design.shape == (SX, SY, SZ) and lax.axis_size("gz") == 2
    sizes = [lax.axis_size(axis) for axis in ("gx", "gy", "gz")]
    extents = (SX * sizes[0], SY * sizes[1], SZ * sizes[2])
    place = jnp.stack([lax.axis_index(axis) for axis in ("gx", "gy", "gz")]).astype(jnp.int32)
    own = (displacement, physical, design, passive)

    x_faces = exchange(*call(faces_x_kernel, 1, 4, [(26, SY, SZ)] * 2, [], 10**6)(place, *own), "gx")
    frame = (ELEMENTS, ROWS, LANES)
    own_frame = (ELEMENTS, SY, LANES)
    inverse, volume_weight, marks = call(
        functools.partial(weights_kernel, extents=extents), 1, 1,
        [frame, (CHOSEN, SY, LANES), (SX, SY, SZ)], [own_frame, own_frame], 10**7,
    )(place, supports.reshape(1, -1))
    x_faces, inverse, volume_weight, marks = lax.optimization_barrier((x_faces, inverse, volume_weight, marks))

    y_shape = (12 * NODES, SZ)
    *y_faces, side = call(
        faces_y_kernel, 1, 6, [y_shape, y_shape, (4 * NODES + 2 * CHOSEN, SY, SIDE)], [], 10**6
    )(place, *own, *x_faces)
    y_faces = exchange(*y_faces, "gy")
    side = other_core(side)
    (y_side,) = call(faces_z_kernel, 1, 2, [(4 * NODES, SY, SIDE)], [], 10**6)(place, *y_faces)
    y_side = other_core(y_side)

    y_shape = (9 * CHOSEN, LANES)
    bounds, *y_bounds = call(
        functools.partial(design_kernel, squares=energy_squares()), 1, 12,
        [(3, CHOSEN, SY, LANES), y_shape, y_shape],
        [(4, NODES, ROWS, LANES), own_frame, own_frame, own_frame], 10**7,
    )(place, *own, *x_faces, *y_faces, side, y_side, inverse, volume_weight)

    y_bounds = exchange(*y_bounds, "gy")
    inner, outer = sizes[1] * sizes[2], sizes[0]
    elements = (2 * SX, SY, 128)
    (part,) = call(
        volumes_kernel, 0, 2, [(inner, 8, 128)], [(2,) + elements, (2,) + elements, (2, 6) + elements], 10**8,
    )(bounds, volume_weight)
    part = lax.all_to_all(part, ("gy", "gz"), 0, 0, tiled=True)
    (part,) = call(repeat_kernel, 0, 1, [(outer, 8, 128)], [], 10**5)(part)
    y_bounds, part = lax.optimization_barrier((y_bounds, part))
    part = lax.all_to_all(part, "gx", 0, 0, tiled=True)

    chosen = (CHOSEN, ROWS, LANES)
    new_design, new_physical, node_blocks = call(
        functools.partial(
            final_kernel, factors=[float(f) for f in corner_factors()],
            target=volume_share * (extents[0] * extents[1] * extents[2]),
        ), 1, 6,
        [(SX, SY, SZ), (SX, SY, SZ), (6, SX, SY, SZ)], [chosen, chosen, chosen, (SX + 1, ROWS, LANES)], 10**7,
    )(place, part, bounds, *y_bounds, inverse, marks)
    return (new_design, new_physical, node_blocks)


def solution(mesh):
    in_specs = (
        P(None, "gx", "gy", "gz"),
        P("gx", "gy", "gz"),
        P("gx", "gy", "gz"),
        P("gx", "gy", "gz"),
        P(),
    )
    out_specs = (P("gx", "gy", "gz"), P("gx", "gy", "gz"), P(None, "gx", "gy", "gz"))
    return jax.shard_map(body, mesh=mesh, in_specs=in_specs, out_specs=out_specs, check_vma=False)
```

```python
import functools
import math

import jax
import jax.numpy as jnp
import numpy as np
from jax import lax
from jax.experimental import pallas as pl
from jax.experimental.pallas import tpu as pltpu
from jax.sharding import PartitionSpec as P

STEPS = 10

filter_radius = 2.5
penalty = 3.0
move_limit = 0.2
stiff_floor = 1e-09
volume_share = 0.5
log_lower = -20.0
log_upper = 20.0
poisson = 0.3

SX, SY, SZ = 8, 8, 256
ROWS, LANES, SIDE = 16, 384, 128
NODES, ELEMENTS, CHOSEN = SX + 10, SX + 9, SX + 5
POINTS = 2**STEPS
F32 = jnp.float32


def corner_offsets():
    return [(q // 4, q // 2 % 2, q % 2) for q in range(8)]


def hex_stiffness():
    lame_first = poisson / ((1.0 + poisson) * (1.0 - 2.0 * poisson))
    shear_modulus = 0.5 / (1.0 + poisson)
    elastic = np.zeros((6, 6))
    elastic[:3, :3] = lame_first
    for d in range(3):
        elastic[d, d] += 2.0 * shear_modulus
        elastic[d + 3, d + 3] = shear_modulus
    corners = corner_offsets()
    points = [0.5 - 0.5 / math.sqrt(3.0), 0.5 + 0.5 / math.sqrt(3.0)]
    matrix = np.zeros((24, 24))
    for p in points:
        for q in points:
            for r in points:
                location = [p, q, r]
                gradients = np.zeros((8, 3))
                for n in range(8):
                    factors = [
                        location[e] if corners[n][e] == 1 else 1.0 - location[e] for e in range(3)
                    ]
                    for d in range(3):
                        sign_value = 1.0 if corners[n][d] == 1 else -1.0
                        gradients[n, d] = sign_value * factors[(d + 1) % 3] * factors[(d + 2) % 3]
                strain = np.zeros((6, 24))
                for n in range(8):
                    column = 3 * n
                    strain[0, column] = gradients[n, 0]
                    strain[1, column + 1] = gradients[n, 1]
                    strain[2, column + 2] = gradients[n, 2]
                    strain[3, column + 1] = gradients[n, 2]
                    strain[3, column + 2] = gradients[n, 1]
                    strain[4, column] = gradients[n, 2]
                    strain[4, column + 2] = gradients[n, 0]
                    strain[5, column] = gradients[n, 1]
                    strain[5, column + 1] = gradients[n, 0]
                matrix += strain.T @ elastic @ strain / 8.0
    return matrix


def energy_squares():
    corners = corner_offsets()
    modes = np.zeros((24, 24))
    for s in range(8):
        bits = (s // 4, s // 2 % 2, s % 2)
        for n in range(8):
            sign_value = 1.0
            for e in range(3):
                if bits[e] == 1 and corners[n][e] == 0:
                    sign_value = -sign_value
            for d in range(3):
                modes[3 * n + d, 3 * s + d] = sign_value
    form = modes.T @ hex_stiffness() @ modes / 64.0
    used = np.zeros((24, 24))
    squares = []
    for parity in range(8):
        members = [3 * (parity ^ (4, 2, 1)[d]) + d for d in range(3)]
        block = form[np.ix_(members, members)].copy()
        used[np.ix_(members, members)] = block
        for r in range(3):
            if block[r, r] < 1e-9:
                continue
            factors = block[r] / math.sqrt(block[r, r])
            block -= np.outer(factors, factors)
            squares.append([(members[c], factors[c]) for c in range(3) if abs(factors[c]) > 1e-9])
        assert np.abs(block).max() < 1e-9
    assert np.abs(used - form).max() < 1e-9
    return squares


def corner_factors():
    matrix = hex_stiffness()
    factors = (matrix[0, 0], matrix[1, 2], matrix[0, 2], matrix[0, 1])
    for n, corner in enumerate(corner_offsets()):
        sign = [1.0 if c == 1 else -1.0 for c in corner]
        block = matrix[3 * n : 3 * n + 3, 3 * n : 3 * n + 3]
        assert np.allclose(np.diag(block), factors[0])
        assert np.allclose(block[1, 2], factors[1] * sign[1] * sign[2])
        assert np.allclose(block[0, 2], factors[2] * sign[0] * sign[2])
        assert np.allclose(block[0, 1], factors[3] * sign[0] * sign[1])
    return factors


def tap(square):
    return max(0.0, filter_radius - math.sqrt(square))


def rolled(value, steps, dim):
    return pltpu.roll(value, (-steps) % value.shape[dim], dim)


def row_pairs(plane):
    return (
        rolled(plane, 1, 0) + rolled(plane, -1, 0),
        rolled(plane, 2, 0) + rolled(plane, -2, 0),
    )


def filtered_plane(plane_of, near_of, far_of, p):
    ring_0 = plane_of(p)
    ring_1 = near_of(p) + plane_of(p - 1) + plane_of(p + 1)
    ring_2 = near_of(p - 1) + near_of(p + 1)
    ring_4 = far_of(p) + plane_of(p - 2) + plane_of(p + 2)
    ring_5 = far_of(p - 1) + far_of(p + 1) + near_of(p - 2) + near_of(p + 2)
    layers = []
    for c in (0, 1, 2):
        total = None
        for square, ring in ((0, ring_0), (1, ring_1), (2, ring_2), (4, ring_4), (5, ring_5)):
            weight = tap(square + c * c)
            if weight > 0.0:
                total = weight * ring if total is None else total + weight * ring
        layers.append(total)
    middle, near, far = layers
    return middle + (rolled(near, 1, 1) + rolled(near, -1, 1)) + (rolled(far, 2, 1) + rolled(far, -2, 1))


def weights_kernel(support_ref, inverse_ref, volume_ref, mark_ref, near_ref, far_ref, *, extents):
    total_x, total_y, total_z = extents
    first_x = lax.axis_index("gx") * SX
    first_y = lax.axis_index("gy") * SY
    first_z = lax.axis_index("gz") * SZ
    row = lax.broadcasted_iota(jnp.int32, (ROWS, LANES), 0)
    lane = lax.broadcasted_iota(jnp.int32, (ROWS, LANES), 1)
    y = first_y + jnp.where(row < 12, row, row - ROWS)
    z = first_z + jnp.where(lane < SZ + SIDE // 2, lane, lane - LANES)
    inside = jnp.where((y >= 0) & (y < total_y) & (z >= 0) & (z < total_z), 1.0, 0.0).astype(F32)
    near, far = row_pairs(inside)

    def present(p):
        x = first_x + p
        return jnp.where((x >= 0) & (x < total_x), 1.0, 0.0).astype(F32)

    for p in range(ELEMENTS):
        x = p - 5
        weight_sum = filtered_plane(
            lambda q: inside * present(q), lambda q: near * present(q), lambda q: far * present(q), x
        )
        here = inside * present(x)
        inverse = jnp.where(here > 0.0, 1.0 / jnp.where(here > 0.0, weight_sum, 1.0), 0.0)
        inverse_ref[p] = inverse
        inverse_near, inverse_far = row_pairs(inverse)
        near_ref[p] = inverse_near[0:SY]
        far_ref[p] = inverse_far[0:SY]
    for p in range(CHOSEN):
        volume_ref[p] = filtered_plane(
            lambda q: inverse_ref[q, 0:SY], lambda q: near_ref[q], lambda q: far_ref[q], p + 2
        )
    node = support_ref[...]
    node_x = node // (total_y * total_z) - first_x
    node_y = node // total_z % total_y - first_y
    node_z = node % total_z - first_z
    owned = (node_x >= 0) & (node_x < SX) & (node_y >= 0) & (node_y < SY)
    line = jnp.where(owned, node_x * SY + node_y, -1)
    count = node.shape[1]
    lines = jnp.where(lax.broadcasted_iota(jnp.int32, (SX * SY, count), 0) == line, 1.0, 0.0)
    lanes = jnp.where(lax.broadcasted_iota(jnp.int32, (SZ, count), 0) == node_z, 1.0, 0.0)
    hits = lax.dot_general(
        lines.astype(jnp.bfloat16),
        lanes.astype(jnp.bfloat16),
        (((1,), (1,)), ((), ())),
        preferred_element_type=F32,
    )
    for p in range(SX):
        mark_ref[p] = hits[p * SY : (p + 1) * SY]


def is_even(axis):
    return lax.axis_index(axis) % 2 == 0


def place_pair(even, first_ref, second_ref, top, bottom, place):
    first_ref[place] = jnp.where(even, top, bottom)
    second_ref[place] = jnp.where(even, bottom, top)


def low_high(even, first_ref, second_ref, place):
    first, second = first_ref[place], second_ref[place]
    return jnp.where(even, second, first), jnp.where(even, first, second)


def row_tile(even, first_ref, second_ref, plane):
    low, high = low_high(even, first_ref, second_ref, slice(3 * plane, 3 * plane + 3))
    return jnp.concatenate([high, jnp.zeros((SY - 6, low.shape[1]), F32), low], axis=0)


def faces_x_kernel(
    shift_ref, physical_ref, design_ref, passive_ref, own_ref, first_ref, second_ref, passive_own, semaphores
):
    copies = [
        pltpu.make_async_copy(source, target, semaphores.at[n])
        for n, (source, target) in enumerate(
            (
                (shift_ref, own_ref.at[0:3]),
                (physical_ref, own_ref.at[3]),
                (design_ref, own_ref.at[4]),
                (passive_ref, passive_own),
            )
        )
    ]
    for copy in copies:
        copy.start()
    for copy in copies:
        copy.wait()
    own_ref[5] = passive_own[...].astype(F32)
    even = is_even("gx")
    for f in range(6):
        depth = 5 if f < 4 else 3
        row = 5 * f if f < 4 else 8 + 3 * f
        place_pair(
            even, first_ref, second_ref, own_ref[f, SX - depth :], own_ref[f, 0:depth], slice(row, row + depth)
        )


def plane_reader(own_ref, x_first, x_second):
    even = is_even("gx")

    def read(index):
        if index < 4 * NODES:
            f, x = index // NODES, index % NODES - 5
            depth, base = 5, 5 * f
        else:
            f, x = 4 + (index - 4 * NODES) // CHOSEN, (index - 4 * NODES) % CHOSEN - 3
            depth, base = 3, 8 + 3 * f
        if 0 <= x < SX:
            return own_ref[f, x]
        low, high = low_high(even, x_first, x_second, base + (x + depth if x < 0 else x - SX))
        return low if x < 0 else high

    return read


def faces_y_kernel(
    own_ref, x_first, x_second, first_ref, second_ref, side_ref
):
    even = is_even("gy")
    lower_core = lax.axis_index("gz") == 0
    read = plane_reader(own_ref, x_first, x_second)
    for index in range(4 * NODES + 2 * CHOSEN):
        plane = read(index)
        if index < 4 * NODES:
            rows = slice(3 * index, 3 * index + 3)
            place_pair(even, first_ref, second_ref, plane[SY - 3 :], plane[0:3], rows)
        side_ref[index] = jnp.where(lower_core, plane[:, SZ - SIDE :], plane[:, 0:SIDE])


def faces_z_kernel(y_first, y_second, side_ref):
    even = is_even("gy")
    lower_core = lax.axis_index("gz") == 0
    for index in range(4 * NODES):
        tile = row_tile(even, y_first, y_second, index)
        side_ref[index] = jnp.where(lower_core, tile[:, SZ - SIDE :], tile[:, 0:SIDE])


def design_kernel(
    own_ref, x_first, x_second, y_first, y_second, side, y_side, inverse_ref, volume_ref, out_ref, first_ref,
    second_ref, ext_ref, sens_ref, near_ref, far_ref, *, squares
):
    lane = lax.broadcasted_iota(jnp.int32, (SY, SIDE), 1)
    start = lax.axis_index("gz") * (SIDE // 2)
    keep = (lane >= start) & (lane < start + SIDE // 2)
    even = is_even("gy")
    read = plane_reader(own_ref, x_first, x_second)
    for f in range(4):
        for p in range(NODES):
            index = NODES * f + p
            ext_ref[f, p, 0:SY, 0:SZ] = read(index)
            ext_ref[f, p, 0:SY, SZ:LANES] = jnp.where(keep, side[index], 0.0)
            ext_ref[f, p, SY:ROWS, 0:SZ] = row_tile(even, y_first, y_second, index)
            ext_ref[f, p, SY:ROWS, SZ:LANES] = jnp.where(keep, y_side[index], 0.0)
    scale = penalty * (1.0 - stiff_floor)

    @pl.loop(0, ELEMENTS)
    def _(p):
        modes = {}
        for d in range(3):
            here, above = ext_ref[d, p], ext_ref[d, p + 1]
            for a, along_x in enumerate((here + above, above - here)):
                beyond = rolled(along_x, 1, 0)
                for b, along_y in enumerate((along_x + beyond, beyond - along_x)):
                    next_lane = rolled(along_y, 1, 1)
                    for c, mode in enumerate((along_y + next_lane, next_lane - along_y)):
                        modes[3 * (4 * a + 2 * b + c) + d] = mode
        energy = None
        for terms in squares:
            line = None
            for mode, factor in terms:
                term = float(factor) * modes[mode]
                line = term if line is None else line + term
            energy = line * line if energy is None else energy + line * line
        density = ext_ref[3, p]
        sens = scale * density * density * energy * inverse_ref[p]
        sens_ref[p] = sens[0:SY]
        near, far = row_pairs(sens)
        near_ref[p] = near[0:SY]
        far_ref[p] = far[0:SY]

    for p in range(CHOSEN):
        filtered = filtered_plane(lambda q: sens_ref[q], lambda q: near_ref[q], lambda q: far_ref[q], p + 2)
        index = 4 * NODES + p
        design = jnp.concatenate([read(index), side[index]], axis=1)
        solid = jnp.concatenate([read(index + CHOSEN), side[index + CHOSEN]], axis=1) > 0.5
        inside = inverse_ref[p + 2, 0:SY] > 0.0
        scaled = design * jnp.sqrt(filtered / jnp.where(inside, volume_ref[p], 1.0))
        floor_bound = jnp.where(solid, 1.0, jnp.maximum(0.0, design - move_limit))
        ceiling = jnp.where(solid, 1.0, jnp.minimum(1.0, design + move_limit))
        for f, value in enumerate((scaled, floor_bound, ceiling)):
            value = jnp.where(inside, value, 0.0)
            out_ref[f, p] = value
            row = 3 * (CHOSEN * f + p)
            place_pair(even, first_ref, second_ref, value[SY - 3 :], value[0:3], slice(row, row + 3))


def three_parts(value):
    first = value.astype(jnp.bfloat16).astype(F32)
    second = (value - first).astype(jnp.bfloat16).astype(F32)
    return first, second, value - first - second


def volumes_kernel(bounds_ref, volume_ref, out_ref, high_ref, low_ref, value_ref):
    step = (log_upper - log_lower) / POINTS
    ceilings = jnp.zeros((SY, 128), F32)
    for v in range(2 * SX):
        place = (3 + v // 2, slice(None), slice(128 * (v % 2), 128 * (v % 2 + 1)))
        weight = volume_ref[place]
        scaled, floor_bound, ceiling = [bounds_ref[(f,) + place] for f in range(3)]
        ceilings = ceilings + weight * ceiling
        log_scaled = jnp.log(jnp.maximum(scaled, 1e-30))
        for t, bound in enumerate((ceiling, floor_bound)):
            reached = (2.0 * (log_scaled - jnp.log(jnp.maximum(bound, 1e-30))) - log_lower) / step
            index = jnp.minimum(jnp.maximum(jnp.ceil(reached), 1.0), POINTS + 1.0) - 1.0
            index = jnp.where(bound > 0.0, index, float(POINTS))
            high = jnp.floor(index * (1.0 / 128.0))
            high_ref[t, v] = high
            low_ref[t, v] = index - 128.0 * high
            sign = -1.0 if t == 0 else 1.0
            parts = three_parts(sign * weight * bound) + three_parts(-sign * weight * scaled)
            for n, part in enumerate(parts):
                value_ref[t, n, v] = part

    rows = lax.broadcasted_iota(jnp.int32, (8, 128), 0).astype(F32)
    columns = lax.broadcasted_iota(jnp.int32, (128, 128), 0).astype(F32).astype(jnp.bfloat16)

    def add_group(v, total):
        lefts, rights = [], []
        for t in range(2):
            for r in range(SY):
                hit = rows == high_ref[t, v, r : r + 1, :]
                left = [jnp.where(hit, value_ref[t, n, v, r : r + 1, :], 0.0) for n in range(6)]
                lefts.append(jnp.concatenate(left, axis=0).astype(jnp.bfloat16))
                low = jnp.broadcast_to(low_ref[t, v, r : r + 1, :], (16, 128)).astype(jnp.bfloat16)
                low = jnp.concatenate([low] * 8, axis=0)
                rights.append(jnp.where(columns == low, jnp.bfloat16(1.0), jnp.bfloat16(0.0)))
        return total + lax.dot_general(
            jnp.concatenate(rights, axis=1),
            jnp.concatenate(lefts, axis=1),
            (((1,), (1,)), ((), ())),
            preferred_element_type=F32,
        )

    total = lax.fori_loop(0, 2 * SX, add_group, jnp.zeros((128, 48), F32), unroll=4).T
    constant = total[0:8] + total[8:16] + total[16:24]
    slope = total[24:32] + total[32:40] + total[40:48]
    upto = jnp.where(
        lax.broadcasted_iota(jnp.int32, (128, 128), 0) <= lax.broadcasted_iota(jnp.int32, (128, 128), 1), 1.0, 0.0
    )
    running = lax.dot_general(
        jnp.concatenate([constant, slope], axis=0),
        upto,
        (((1,), (0,)), ((), ())),
        precision=lax.Precision.HIGHEST,
        preferred_element_type=F32,
    )
    row = lax.broadcasted_iota(jnp.int32, (8, 128), 0)
    lane = lax.broadcasted_iota(jnp.int32, (8, 128), 1)
    cumulated = []
    for part in (running[0:8], running[8:16]):
        ends = jnp.broadcast_to(part[:, 127:128], (8, 128))
        before = ends
        for shift in (1, 2, 4):
            before = before + jnp.where(row >= shift, rolled(before, -shift, 0), 0.0)
        cumulated.append(part + (before - ends))
    index = (row * 128 + lane + 1).astype(F32)
    factor = jnp.exp(-0.5 * (log_lower + step * index))
    result = jnp.sum(ceilings) + cumulated[0] + factor * cumulated[1]
    for i in range(out_ref.shape[0]):
        out_ref[i] = result


def repeat_kernel(part_ref, out_ref):
    total = part_ref[0]
    for i in range(1, part_ref.shape[0]):
        total = total + part_ref[i]
    for i in range(out_ref.shape[0]):
        out_ref[i] = total


def final_kernel(
    part_ref, own_ref, y_first, y_second, inverse_ref, mark_ref, new_design_ref, new_physical_ref,
    blocks_ref, chosen_ref, near_ref, far_ref, stiff_ref, *, factors, target
):
    total = part_ref[0]
    for i in range(1, part_ref.shape[0]):
        total = total + part_ref[i]
    low_end = jnp.minimum(jnp.sum(jnp.where(total > target, 1.0, 0.0)), POINTS - 1.0)
    multiplier = log_lower + (log_upper - log_lower) / POINTS * (low_end + 0.5)
    factor = jnp.exp(jnp.broadcast_to(-0.5 * multiplier, (SY, LANES)))
    even = is_even("gy")
    for p in range(CHOSEN):
        tiles = []
        own = [own_ref[f, p] for f in range(3)]
        beside = [row_tile(even, y_first, y_second, CHOSEN * f + p) for f in range(3)]
        for scaled, floor_bound, ceiling in (own, beside):
            tiles.append(jnp.minimum(jnp.maximum(scaled * factor, floor_bound), ceiling))
        chosen = jnp.concatenate(tiles, axis=0)
        chosen_ref[p] = chosen
        near, far = row_pairs(chosen)
        near_ref[p] = near
        far_ref[p] = far
        if 3 <= p < SX + 3:
            new_design_ref[p - 3] = tiles[0][:, 0:SZ]
    for p in range(SX + 1):
        inverse = inverse_ref[p + 4]
        density = (
            filtered_plane(lambda q: chosen_ref[q], lambda q: near_ref[q], lambda q: far_ref[q], p + 2) * inverse
        )
        if p >= 1:
            new_physical_ref[p - 1] = density[0:SY, 0:SZ]
        cube = stiff_floor + density * density * density * (1.0 - stiff_floor)
        stiff_ref[p] = jnp.where(inverse > 0.0, cube, 0.0)
    for p in range(SX):
        below, here = stiff_ref[p], stiff_ref[p + 1]
        x_sum, x_diff = here + below, below - here
        x_sum_back, x_diff_back = rolled(x_sum, -1, 0), rolled(x_diff, -1, 0)
        sum_sum = (x_sum + x_sum_back)[0:SY]
        sum_diff = (x_sum_back - x_sum)[0:SY]
        diff_sum = (x_diff + x_diff_back)[0:SY]
        diff_diff = (x_diff_back - x_diff)[0:SY]
        marked = mark_ref[p] > 0.5
        even = factors[0] * (sum_sum + rolled(sum_sum, -1, 1))[:, 0:SZ]
        even = jnp.where(marked, 1.0, even)
        blocks_ref[0, p] = even
        blocks_ref[1, p] = even
        blocks_ref[2, p] = even
        yz = factors[1] * (rolled(sum_diff, -1, 1) - sum_diff)[:, 0:SZ]
        xz = factors[2] * (rolled(diff_sum, -1, 1) - diff_sum)[:, 0:SZ]
        xy = factors[3] * (diff_diff + rolled(diff_diff, -1, 1))[:, 0:SZ]
        blocks_ref[3, p] = jnp.where(marked, 0.0, yz)
        blocks_ref[4, p] = jnp.where(marked, 0.0, xz)
        blocks_ref[5, p] = jnp.where(marked, 0.0, xy)


def call(kernel, inputs, shapes, scratch, flops, space=pltpu.VMEM, grant=32):
    outs = [jax.ShapeDtypeStruct(shape, F32) for shape in shapes]
    return pl.pallas_call(
        kernel,
        out_shape=outs,
        in_specs=[pl.BlockSpec(memory_space=space)] * len(inputs),
        out_specs=[pl.BlockSpec(memory_space=pltpu.VMEM)] * len(outs),
        scratch_shapes=[pltpu.VMEM(shape, F32) if isinstance(shape, tuple) else shape for shape in scratch],
        compiler_params=pltpu.CompilerParams(vmem_limit_bytes=grant * 2**20),
        cost_estimate=pl.CostEstimate(flops=flops, bytes_accessed=10**6, transcendentals=0),
    )(*inputs)


def exchange(first, second, axis):
    count = lax.axis_size(axis)
    results = []
    for start, faces in enumerate((first, second)):
        pairs = [(i, i + 1) for i in range(start, count - 1, 2)]
        results.append(lax.ppermute(faces, axis, pairs + [(j, i) for i, j in pairs]))
    return results


def other_core(values):
    return lax.ppermute(values, "gz", [(0, 1), (1, 0)])


def body(displacement, physical, design, passive, supports):
    assert design.shape == (SX, SY, SZ) and lax.axis_size("gz") == 2
    sizes = [lax.axis_size(axis) for axis in ("gx", "gy", "gz")]
    extents = (SX * sizes[0], SY * sizes[1], SZ * sizes[2])
    block = (SX, SY, SZ)
    faces = (26, SY, SZ)
    own, *x_faces = call(
        faces_x_kernel, (displacement, physical, design, passive), [(6,) + block, faces, faces],
        [pltpu.VMEM(block, jnp.int32), pltpu.SemaphoreType.DMA((4,))], 10**6, pltpu.HBM, 62,
    )
    x_faces = exchange(*x_faces, "gx")
    frame = (ELEMENTS, ROWS, LANES)
    own_frame = (ELEMENTS, SY, LANES)
    inverse, volume_weight, marks = call(
        functools.partial(weights_kernel, extents=extents), (supports.reshape(1, -1),),
        [frame, (CHOSEN, SY, LANES), block], [own_frame, own_frame], 10**7,
    )
    x_faces, inverse, volume_weight, marks = lax.optimization_barrier((x_faces, inverse, volume_weight, marks))

    faces = (12 * NODES, SZ)
    *y_faces, side = call(
        faces_y_kernel, (own, *x_faces), [faces, faces, (4 * NODES + 2 * CHOSEN, SY, SIDE)], [], 10**6
    )
    y_faces = exchange(*y_faces, "gy")
    side = other_core(side)
    (y_side,) = call(faces_z_kernel, y_faces, [(4 * NODES, SY, SIDE)], [], 10**6)
    y_side = other_core(y_side)

    faces = (9 * CHOSEN, LANES)
    bounds, *y_bounds = call(
        functools.partial(design_kernel, squares=energy_squares()),
        (own, *x_faces, *y_faces, side, y_side, inverse, volume_weight),
        [(3, CHOSEN, SY, LANES), faces, faces],
        [(4, NODES, ROWS, LANES), own_frame, own_frame, own_frame], 10**7,
    )

    y_bounds = exchange(*y_bounds, "gy")
    inner, outer = sizes[1] * sizes[2], sizes[0]
    elements = (2 * SX, SY, 128)
    (part,) = call(
        volumes_kernel, (bounds, volume_weight), [(inner, 8, 128)],
        [(2,) + elements, (2,) + elements, (2, 6) + elements], 10**8,
    )
    part = lax.all_to_all(part, ("gy", "gz"), 0, 0, tiled=True)
    (part,) = call(repeat_kernel, (part,), [(outer, 8, 128)], [], 10**5)
    y_bounds, part = lax.optimization_barrier((y_bounds, part))
    part = lax.all_to_all(part, "gx", 0, 0, tiled=True)

    chosen = (CHOSEN, ROWS, LANES)
    target = volume_share * (extents[0] * extents[1] * extents[2])
    new_design, new_physical, node_blocks = call(
        functools.partial(final_kernel, factors=[float(f) for f in corner_factors()], target=target),
        (part, bounds, *y_bounds, inverse, marks), [block, block, (6,) + block],
        [chosen, chosen, chosen, (SX + 1, ROWS, LANES)], 10**7,
    )
    return (new_design, new_physical, node_blocks)


def solution(mesh):
    in_specs = (
        P(None, "gx", "gy", "gz"),
        P("gx", "gy", "gz"),
        P("gx", "gy", "gz"),
        P("gx", "gy", "gz"),
        P(),
    )
    out_specs = (P("gx", "gy", "gz"), P("gx", "gy", "gz"), P(None, "gx", "gy", "gz"))
    return jax.shard_map(body, mesh=mesh, in_specs=in_specs, out_specs=out_specs, check_vma=False)
```

```python
import functools
import math

import jax
import jax.numpy as jnp
import numpy as np
from jax import lax
from jax.experimental import pallas as pl
from jax.experimental.pallas import tpu as pltpu
from jax.sharding import PartitionSpec as P

STEPS = 10

filter_radius = 2.5
penalty = 3.0
move_limit = 0.2
stiff_floor = 1e-09
volume_share = 0.5
log_lower = -20.0
log_upper = 20.0
poisson = 0.3

SX, SY, SZ = 8, 8, 256
ROWS, LANES, SIDE = 16, 384, 128
NODES, ELEMENTS, CHOSEN = SX + 10, SX + 9, SX + 5
POINTS = 2**STEPS
F32 = jnp.float32


def corner_offsets():
    return [(q // 4, q // 2 % 2, q % 2) for q in range(8)]


def hex_stiffness():
    lame_first = poisson / ((1.0 + poisson) * (1.0 - 2.0 * poisson))
    shear_modulus = 0.5 / (1.0 + poisson)
    elastic = np.zeros((6, 6))
    elastic[:3, :3] = lame_first
    for d in range(3):
        elastic[d, d] += 2.0 * shear_modulus
        elastic[d + 3, d + 3] = shear_modulus
    corners = corner_offsets()
    points = [0.5 - 0.5 / math.sqrt(3.0), 0.5 + 0.5 / math.sqrt(3.0)]
    matrix = np.zeros((24, 24))
    for p in points:
        for q in points:
            for r in points:
                location = [p, q, r]
                gradients = np.zeros((8, 3))
                for n in range(8):
                    factors = [
                        location[e] if corners[n][e] == 1 else 1.0 - location[e] for e in range(3)
                    ]
                    for d in range(3):
                        sign_value = 1.0 if corners[n][d] == 1 else -1.0
                        gradients[n, d] = sign_value * factors[(d + 1) % 3] * factors[(d + 2) % 3]
                strain = np.zeros((6, 24))
                for n in range(8):
                    column = 3 * n
                    strain[0, column] = gradients[n, 0]
                    strain[1, column + 1] = gradients[n, 1]
                    strain[2, column + 2] = gradients[n, 2]
                    strain[3, column + 1] = gradients[n, 2]
                    strain[3, column + 2] = gradients[n, 1]
                    strain[4, column] = gradients[n, 2]
                    strain[4, column + 2] = gradients[n, 0]
                    strain[5, column] = gradients[n, 1]
                    strain[5, column + 1] = gradients[n, 0]
                matrix += strain.T @ elastic @ strain / 8.0
    return matrix


def energy_groups():
    corners = corner_offsets()
    modes = np.zeros((24, 24))
    for s in range(8):
        bits = (s // 4, s // 2 % 2, s % 2)
        for n in range(8):
            sign_value = 1.0
            for e in range(3):
                if bits[e] == 1 and corners[n][e] == 0:
                    sign_value = -sign_value
            for d in range(3):
                modes[3 * n + d, 3 * s + d] = sign_value
    form = modes.T @ hex_stiffness() @ modes / 64.0
    groups = []

    def add(coefficient, members):
        if abs(coefficient) < 1e-9:
            return
        for group in groups:
            if abs(group[0] - coefficient) < 1e-9:
                group[1].append(members)
                return
        groups.append((coefficient, [members]))

    for parity in range(8):
        left = [3 * (parity ^ (4, 2, 1)[d]) + d for d in range(3)]
        while left:
            first = left[0]
            block = [m for m in left if m == first or abs(form[first, m]) > 1e-9]
            left = [m for m in left if m not in block]
            beside = form[block[0], block[1]] if len(block) > 1 else 0.0
            add(beside, block)
            for m in block:
                add(form[m, m] - beside, [m])
    rebuilt = np.zeros((24, 24))
    for coefficient, sums in groups:
        for members in sums:
            rebuilt[np.ix_(members, members)] += coefficient
    assert np.abs(rebuilt - form).max() < 1e-9
    return groups


def corner_factors():
    matrix = hex_stiffness()
    factors = (matrix[0, 0], matrix[1, 2], matrix[0, 2], matrix[0, 1])
    for n, corner in enumerate(corner_offsets()):
        sign = [1.0 if c == 1 else -1.0 for c in corner]
        block = matrix[3 * n : 3 * n + 3, 3 * n : 3 * n + 3]
        assert np.allclose(np.diag(block), factors[0])
        assert np.allclose(block[1, 2], factors[1] * sign[1] * sign[2])
        assert np.allclose(block[0, 2], factors[2] * sign[0] * sign[2])
        assert np.allclose(block[0, 1], factors[3] * sign[0] * sign[1])
    return factors


def tap(square):
    return max(0.0, filter_radius - math.sqrt(square))


def rolled(value, steps, dim):
    return pltpu.roll(value, (-steps) % value.shape[dim], dim)


def row_pairs(plane):
    return (
        rolled(plane, 1, 0) + rolled(plane, -1, 0),
        rolled(plane, 2, 0) + rolled(plane, -2, 0),
    )


def filtered_plane(plane_of, near_of, far_of, p):
    ring_0 = plane_of(p)
    ring_1 = near_of(p) + plane_of(p - 1) + plane_of(p + 1)
    ring_2 = near_of(p - 1) + near_of(p + 1)
    ring_4 = far_of(p) + plane_of(p - 2) + plane_of(p + 2)
    ring_5 = far_of(p - 1) + far_of(p + 1) + near_of(p - 2) + near_of(p + 2)
    layers = []
    for c in (0, 1, 2):
        total = None
        for square, ring in ((0, ring_0), (1, ring_1), (2, ring_2), (4, ring_4), (5, ring_5)):
            weight = tap(square + c * c)
            if weight > 0.0:
                total = weight * ring if total is None else total + weight * ring
        layers.append(total)
    middle, near, far = layers
    return middle + (rolled(near, 1, 1) + rolled(near, -1, 1)) + (rolled(far, 2, 1) + rolled(far, -2, 1))


def weights_kernel(
    own_ref, support_ref, own_copy, inverse_ref, volume_ref, mark_ref, near_ref, far_ref, semaphore, *, extents
):
    copy = pltpu.make_async_copy(own_ref, own_copy, semaphore)
    copy.start()
    total_x, total_y, total_z = extents
    first_x = lax.axis_index("gx") * SX
    first_y = lax.axis_index("gy") * SY
    first_z = lax.axis_index("gz") * SZ
    row = lax.broadcasted_iota(jnp.int32, (ROWS, LANES), 0)
    lane = lax.broadcasted_iota(jnp.int32, (ROWS, LANES), 1)
    y = first_y + jnp.where(row < 12, row, row - ROWS)
    z = first_z + jnp.where(lane < SZ + SIDE // 2, lane, lane - LANES)
    inside = jnp.where((y >= 0) & (y < total_y) & (z >= 0) & (z < total_z), 1.0, 0.0).astype(F32)
    near, far = row_pairs(inside)

    def present(p):
        x = first_x + p
        return jnp.where((x >= 0) & (x < total_x), 1.0, 0.0).astype(F32)

    for p in range(ELEMENTS):
        x = p - 5
        weight_sum = filtered_plane(
            lambda q: inside * present(q), lambda q: near * present(q), lambda q: far * present(q), x
        )
        here = inside * present(x)
        inverse = jnp.where(here > 0.0, 1.0 / jnp.where(here > 0.0, weight_sum, 1.0), 0.0)
        inverse_ref[p] = inverse
        inverse_near, inverse_far = row_pairs(inverse)
        near_ref[p] = inverse_near[0:SY]
        far_ref[p] = inverse_far[0:SY]
    for p in range(CHOSEN):
        volume_ref[p] = filtered_plane(
            lambda q: inverse_ref[q, 0:SY], lambda q: near_ref[q], lambda q: far_ref[q], p + 2
        )
    node = support_ref[...]
    node_x = node // (total_y * total_z) - first_x
    node_y = node // total_z % total_y - first_y
    node_z = node % total_z - first_z
    owned = (node_x >= 0) & (node_x < SX) & (node_y >= 0) & (node_y < SY)
    line = jnp.where(owned, node_x * SY + node_y, -1)
    count = node.shape[1]
    lines = jnp.where(lax.broadcasted_iota(jnp.int32, (SX * SY, count), 0) == line, 1.0, 0.0)
    lanes = jnp.where(lax.broadcasted_iota(jnp.int32, (SZ, count), 0) == node_z, 1.0, 0.0)
    hits = lax.dot_general(
        lines.astype(jnp.bfloat16),
        lanes.astype(jnp.bfloat16),
        (((1,), (1,)), ((), ())),
        preferred_element_type=F32,
    )
    for p in range(SX):
        mark_ref[p] = hits[p * SY : (p + 1) * SY]
    copy.wait()


def is_even(axis):
    return lax.axis_index(axis) % 2 == 0


def place_pair(even, first_ref, second_ref, top, bottom, place):
    first_ref[place] = jnp.where(even, top, bottom)
    second_ref[place] = jnp.where(even, bottom, top)


def low_high(even, first_ref, second_ref, place):
    first, second = first_ref[place], second_ref[place]
    return jnp.where(even, second, first), jnp.where(even, first, second)


def row_tile(even, first_ref, second_ref, plane):
    low, high = low_high(even, first_ref, second_ref, slice(3 * plane, 3 * plane + 3))
    return jnp.concatenate([high, jnp.zeros((SY - 6, low.shape[1]), F32), low], axis=0)


def faces_x_kernel(
    shift_ref, physical_ref, design_ref, passive_ref, own_ref, first_ref, second_ref, passive_own, semaphores
):
    pairs = (
        (shift_ref, own_ref.at[0:3]),
        (physical_ref, own_ref.at[3]),
        (design_ref, own_ref.at[4]),
        (passive_ref, passive_own),
    )
    copies = [pltpu.make_async_copy(*pair, semaphores.at[n]) for n, pair in enumerate(pairs)]
    for copy in copies:
        copy.start()
    for copy in copies:
        copy.wait()
    own_ref[5] = passive_own[...].astype(F32)
    even = is_even("gx")
    for f in range(6):
        depth = 5 if f < 4 else 3
        row = 5 * f if f < 4 else 8 + 3 * f
        place_pair(
            even, first_ref, second_ref, own_ref[f, SX - depth :], own_ref[f, 0:depth], slice(row, row + depth)
        )


def plane_reader(own_ref, x_first, x_second):
    even = is_even("gx")

    def read(index):
        if index < 4 * NODES:
            f, x = index // NODES, index % NODES - 5
            depth, base = 5, 5 * f
        else:
            f, x = 4 + (index - 4 * NODES) // CHOSEN, (index - 4 * NODES) % CHOSEN - 3
            depth, base = 3, 8 + 3 * f
        if 0 <= x < SX:
            return own_ref[f, x]
        low, high = low_high(even, x_first, x_second, base + (x + depth if x < 0 else x - SX))
        return low if x < 0 else high

    return read


def faces_y_kernel(
    own_ref, x_first, x_second, first_ref, second_ref, side_ref
):
    even = is_even("gy")
    lower_core = lax.axis_index("gz") == 0
    read = plane_reader(own_ref, x_first, x_second)
    for index in range(4 * NODES + 2 * CHOSEN):
        plane = read(index)
        if index < 4 * NODES:
            rows = slice(3 * index, 3 * index + 3)
            place_pair(even, first_ref, second_ref, plane[SY - 3 :], plane[0:3], rows)
        side_ref[index] = jnp.where(lower_core, plane[:, SZ - SIDE :], plane[:, 0:SIDE])


def faces_z_kernel(y_first, y_second, side_ref):
    even = is_even("gy")
    lower_core = lax.axis_index("gz") == 0
    for index in range(4 * NODES):
        tile = row_tile(even, y_first, y_second, index)
        side_ref[index] = jnp.where(lower_core, tile[:, SZ - SIDE :], tile[:, 0:SIDE])


def design_kernel(
    own_ref, x_first, x_second, y_first, y_second, side, y_side, inverse_ref, volume_ref, out_ref, first_ref,
    second_ref, part_ref, ext_ref, sens_ref, near_ref, far_ref, high_ref, low_ref, value_ref, *, groups
):
    lane = lax.broadcasted_iota(jnp.int32, (SY, SIDE), 1)
    start = lax.axis_index("gz") * (SIDE // 2)
    keep = (lane >= start) & (lane < start + SIDE // 2)
    even = is_even("gy")
    read = plane_reader(own_ref, x_first, x_second)
    for f in range(4):
        for p in range(NODES):
            index = NODES * f + p
            ext_ref[f, p, 0:SY, 0:SZ] = read(index)
            ext_ref[f, p, 0:SY, SZ:LANES] = jnp.where(keep, side[index], 0.0)
            ext_ref[f, p, SY:ROWS, 0:SZ] = row_tile(even, y_first, y_second, index)
            ext_ref[f, p, SY:ROWS, SZ:LANES] = jnp.where(keep, y_side[index], 0.0)
    scale = penalty * (1.0 - stiff_floor)

    @pl.loop(0, ELEMENTS)
    def _(p):
        modes = {}
        for d in range(3):
            here, above = ext_ref[d, p], ext_ref[d, p + 1]
            for a, along_x in enumerate((here + above, above - here)):
                beyond = rolled(along_x, 1, 0)
                for b, along_y in enumerate((along_x + beyond, beyond - along_x)):
                    next_lane = rolled(along_y, 1, 1)
                    for c, mode in enumerate((along_y + next_lane, next_lane - along_y)):
                        modes[3 * (4 * a + 2 * b + c) + d] = mode
        energy = None
        for coefficient, sums in groups:
            squares = None
            for members in sums:
                value = functools.reduce(lambda left, right: left + right, [modes[m] for m in members])
                squares = value * value if squares is None else squares + value * value
            squares = float(coefficient) * squares
            energy = squares if energy is None else energy + squares
        density = ext_ref[3, p]
        sens = scale * density * density * energy * inverse_ref[p]
        sens_ref[p] = sens[0:SY]
        near, far = row_pairs(sens)
        near_ref[p] = near[0:SY]
        far_ref[p] = far[0:SY]

    for p in range(CHOSEN):
        filtered = filtered_plane(lambda q: sens_ref[q], lambda q: near_ref[q], lambda q: far_ref[q], p + 2)
        index = 4 * NODES + p
        design = jnp.concatenate([read(index), side[index]], axis=1)
        solid = jnp.concatenate([read(index + CHOSEN), side[index + CHOSEN]], axis=1) > 0.5
        inside = inverse_ref[p + 2, 0:SY] > 0.0
        scaled = design * jnp.sqrt(filtered / jnp.where(inside, volume_ref[p], 1.0))
        floor_bound = jnp.where(solid, 1.0, jnp.maximum(0.0, design - move_limit))
        ceiling = jnp.where(solid, 1.0, jnp.minimum(1.0, design + move_limit))
        for f, value in enumerate((scaled, floor_bound, ceiling)):
            value = jnp.where(inside, value, 0.0)
            out_ref[f, p] = value
            row = 3 * (CHOSEN * f + p)
            place_pair(even, first_ref, second_ref, value[SY - 3 :], value[0:3], slice(row, row + 3))
    add_volumes(out_ref, volume_ref, part_ref, high_ref, low_ref, value_ref)


def three_parts(value):
    first = value.astype(jnp.bfloat16).astype(F32)
    second = (value - first).astype(jnp.bfloat16).astype(F32)
    return first, second, value - first - second


def add_volumes(bounds_ref, volume_ref, out_ref, high_ref, low_ref, value_ref):
    step = (log_upper - log_lower) / POINTS
    ceilings = jnp.zeros((SY, 128), F32)
    for v in range(2 * SX):
        place = (3 + v // 2, slice(None), slice(128 * (v % 2), 128 * (v % 2 + 1)))
        weight = volume_ref[place]
        scaled, floor_bound, ceiling = [bounds_ref[(f,) + place] for f in range(3)]
        ceilings = ceilings + weight * ceiling
        log_scaled = jnp.log(jnp.maximum(scaled, 1e-30))
        for t, bound in enumerate((ceiling, floor_bound)):
            reached = (2.0 * (log_scaled - jnp.log(jnp.maximum(bound, 1e-30))) - log_lower) / step
            index = jnp.minimum(jnp.maximum(jnp.ceil(reached), 1.0), POINTS + 1.0) - 1.0
            index = jnp.where(bound > 0.0, index, float(POINTS))
            high = jnp.floor(index * (1.0 / 128.0))
            high_ref[t, v] = high
            low_ref[t, v] = index - 128.0 * high
            sign = -1.0 if t == 0 else 1.0
            parts = three_parts(sign * weight * bound) + three_parts(-sign * weight * scaled)
            for n, part in enumerate(parts):
                value_ref[t, n, v] = part

    rows = lax.broadcasted_iota(jnp.int32, (8, 128), 0).astype(F32)
    columns = lax.broadcasted_iota(jnp.int32, (128, 128), 0).astype(F32).astype(jnp.bfloat16)

    def add_group(v, total):
        lefts, rights = [], []
        for t in range(2):
            for r in range(SY):
                hit = rows == high_ref[t, v, r : r + 1, :]
                left = [jnp.where(hit, value_ref[t, n, v, r : r + 1, :], 0.0) for n in range(6)]
                lefts.append(jnp.concatenate(left, axis=0).astype(jnp.bfloat16))
                low = jnp.broadcast_to(low_ref[t, v, r : r + 1, :], (16, 128)).astype(jnp.bfloat16)
                low = jnp.concatenate([low] * 8, axis=0)
                rights.append(jnp.where(columns == low, jnp.bfloat16(1.0), jnp.bfloat16(0.0)))
        return total + lax.dot_general(
            jnp.concatenate(rights, axis=1),
            jnp.concatenate(lefts, axis=1),
            (((1,), (1,)), ((), ())),
            preferred_element_type=F32,
        )

    total = lax.fori_loop(0, 2 * SX, add_group, jnp.zeros((128, 48), F32), unroll=4).T
    constant = total[0:8] + total[8:16] + total[16:24]
    slope = total[24:32] + total[32:40] + total[40:48]
    upto = jnp.where(
        lax.broadcasted_iota(jnp.int32, (128, 128), 0) <= lax.broadcasted_iota(jnp.int32, (128, 128), 1), 1.0, 0.0
    )
    running = lax.dot_general(
        jnp.concatenate([constant, slope], axis=0),
        upto,
        (((1,), (0,)), ((), ())),
        precision=lax.Precision.HIGHEST,
        preferred_element_type=F32,
    )
    row = lax.broadcasted_iota(jnp.int32, (8, 128), 0)
    lane = lax.broadcasted_iota(jnp.int32, (8, 128), 1)
    cumulated = []
    for part in (running[0:8], running[8:16]):
        ends = jnp.broadcast_to(part[:, 127:128], (8, 128))
        before = ends
        for shift in (1, 2, 4):
            before = before + jnp.where(row >= shift, rolled(before, -shift, 0), 0.0)
        cumulated.append(part + (before - ends))
    index = (row * 128 + lane + 1).astype(F32)
    factor = jnp.exp(-0.5 * (log_lower + step * index))
    result = jnp.sum(ceilings) + cumulated[0] + factor * cumulated[1]
    for i in range(out_ref.shape[0]):
        out_ref[i] = result


def repeat_kernel(part_ref, out_ref):
    total = part_ref[0]
    for i in range(1, part_ref.shape[0]):
        total = total + part_ref[i]
    for i in range(out_ref.shape[0]):
        out_ref[i] = total


def final_kernel(
    part_ref, own_ref, y_first, y_second, inverse_ref, mark_ref, new_design_ref, new_physical_ref,
    blocks_ref, chosen_ref, near_ref, far_ref, stiff_ref, *, factors, target
):
    total = part_ref[0]
    for i in range(1, part_ref.shape[0]):
        total = total + part_ref[i]
    low_end = jnp.minimum(jnp.sum(jnp.where(total > target, 1.0, 0.0)), POINTS - 1.0)
    multiplier = log_lower + (log_upper - log_lower) / POINTS * (low_end + 0.5)
    factor = jnp.exp(jnp.broadcast_to(-0.5 * multiplier, (SY, LANES)))
    even = is_even("gy")
    for p in range(CHOSEN):
        tiles = []
        own = [own_ref[f, p] for f in range(3)]
        beside = [row_tile(even, y_first, y_second, CHOSEN * f + p) for f in range(3)]
        for scaled, floor_bound, ceiling in (own, beside):
            tiles.append(jnp.minimum(jnp.maximum(scaled * factor, floor_bound), ceiling))
        chosen = jnp.concatenate(tiles, axis=0)
        chosen_ref[p] = chosen
        near, far = row_pairs(chosen)
        near_ref[p] = near
        far_ref[p] = far
        if 3 <= p < SX + 3:
            new_design_ref[p - 3] = tiles[0][:, 0:SZ]
    for p in range(SX + 1):
        inverse = inverse_ref[p + 4]
        density = (
            filtered_plane(lambda q: chosen_ref[q], lambda q: near_ref[q], lambda q: far_ref[q], p + 2) * inverse
        )
        if p >= 1:
            new_physical_ref[p - 1] = density[0:SY, 0:SZ]
        cube = stiff_floor + density * density * density * (1.0 - stiff_floor)
        stiff_ref[p] = jnp.where(inverse > 0.0, cube, 0.0)
    for p in range(SX):
        below, here = stiff_ref[p], stiff_ref[p + 1]
        x_sum, x_diff = here + below, below - here
        x_sum_back, x_diff_back = rolled(x_sum, -1, 0), rolled(x_diff, -1, 0)
        sum_sum = (x_sum + x_sum_back)[0:SY]
        sum_diff = (x_sum_back - x_sum)[0:SY]
        diff_sum = (x_diff + x_diff_back)[0:SY]
        diff_diff = (x_diff_back - x_diff)[0:SY]
        marked = mark_ref[p] > 0.5
        even = factors[0] * (sum_sum + rolled(sum_sum, -1, 1))[:, 0:SZ]
        even = jnp.where(marked, 1.0, even)
        blocks_ref[0, p] = even
        blocks_ref[1, p] = even
        blocks_ref[2, p] = even
        yz = factors[1] * (rolled(sum_diff, -1, 1) - sum_diff)[:, 0:SZ]
        xz = factors[2] * (rolled(diff_sum, -1, 1) - diff_sum)[:, 0:SZ]
        xy = factors[3] * (diff_diff + rolled(diff_diff, -1, 1))[:, 0:SZ]
        blocks_ref[3, p] = jnp.where(marked, 0.0, yz)
        blocks_ref[4, p] = jnp.where(marked, 0.0, xz)
        blocks_ref[5, p] = jnp.where(marked, 0.0, xy)


def call(kernel, inputs, shapes, scratch, flops, spaces=None, grant=32):
    outs = [jax.ShapeDtypeStruct(shape, F32) for shape in shapes]
    return pl.pallas_call(
        kernel,
        out_shape=outs,
        in_specs=[pl.BlockSpec(memory_space=space) for space in spaces or [pltpu.VMEM] * len(inputs)],
        out_specs=[pl.BlockSpec(memory_space=pltpu.VMEM)] * len(outs),
        scratch_shapes=[pltpu.VMEM(shape, F32) if isinstance(shape, tuple) else shape for shape in scratch],
        compiler_params=pltpu.CompilerParams(vmem_limit_bytes=grant * 2**20),
        cost_estimate=pl.CostEstimate(flops=flops, bytes_accessed=10**6, transcendentals=0),
    )(*inputs)


def exchange(first, second, axis):
    count = lax.axis_size(axis)
    results = []
    for start, faces in enumerate((first, second)):
        pairs = [(i, i + 1) for i in range(start, count - 1, 2)]
        results.append(lax.ppermute(faces, axis, pairs + [(j, i) for i, j in pairs]))
    return results


def other_core(values):
    return lax.ppermute(values, "gz", [(0, 1), (1, 0)])


def body(displacement, physical, design, passive, supports):
    assert design.shape == (SX, SY, SZ) and lax.axis_size("gz") == 2
    sizes = [lax.axis_size(axis) for axis in ("gx", "gy", "gz")]
    extents = (SX * sizes[0], SY * sizes[1], SZ * sizes[2])
    block = (SX, SY, SZ)
    faces = (26, SY, SZ)
    own, *x_faces = call(
        faces_x_kernel, (displacement, physical, design, passive), [(6,) + block, faces, faces],
        [pltpu.VMEM(block, jnp.int32), pltpu.SemaphoreType.DMA((4,))], 10**6, [pltpu.HBM] * 4, 62,
    )
    x_faces = exchange(*x_faces, "gx")
    frame = (ELEMENTS, ROWS, LANES)
    own_frame = (ELEMENTS, SY, LANES)
    weights = call(
        functools.partial(weights_kernel, extents=extents), (own, supports.reshape(1, -1)),
        [(6,) + block, frame, (CHOSEN, SY, LANES), block],
        [own_frame, own_frame, pltpu.SemaphoreType.DMA(())], 10**7, [pltpu.HBM, pltpu.VMEM],
    )
    x_faces, (own, inverse, volume_weight, marks) = lax.optimization_barrier((x_faces, weights))

    faces = (12 * NODES, SZ)
    *y_faces, side = call(
        faces_y_kernel, (own, *x_faces), [faces, faces, (4 * NODES + 2 * CHOSEN, SY, SIDE)], [], 10**6
    )
    y_faces = exchange(*y_faces, "gy")
    side = other_core(side)
    (y_side,) = call(faces_z_kernel, y_faces, [(4 * NODES, SY, SIDE)], [], 10**6)
    y_side = other_core(y_side)

    faces = (9 * CHOSEN, LANES)
    inner, outer = sizes[1] * sizes[2], sizes[0]
    elements = (2 * SX, SY, 128)
    bounds, *y_bounds, part = call(
        functools.partial(design_kernel, groups=energy_groups()),
        (own, *x_faces, *y_faces, side, y_side, inverse, volume_weight),
        [(3, CHOSEN, SY, LANES), faces, faces, (inner, 8, 128)],
        [(4, NODES, ROWS, LANES), own_frame, own_frame, own_frame]
        + [(2,) + elements, (2,) + elements, (2, 6) + elements], 10**7,
    )

    part = lax.all_to_all(part, ("gy", "gz"), 0, 0, tiled=True)
    y_bounds, part = lax.optimization_barrier((y_bounds, part))
    y_bounds = exchange(*y_bounds, "gy")
    (part,) = call(repeat_kernel, (part,), [(outer, 8, 128)], [], 10**5)
    part = lax.all_to_all(part, "gx", 0, 0, tiled=True)

    chosen = (CHOSEN, ROWS, LANES)
    target = volume_share * (extents[0] * extents[1] * extents[2])
    new_design, new_physical, node_blocks = call(
        functools.partial(final_kernel, factors=[float(f) for f in corner_factors()], target=target),
        (part, bounds, *y_bounds, inverse, marks), [block, block, (6,) + block],
        [chosen, chosen, chosen, (SX + 1, ROWS, LANES)], 10**7,
    )
    return (new_design, new_physical, node_blocks)


def solution(mesh):
    in_specs = (
        P(None, "gx", "gy", "gz"),
        P("gx", "gy", "gz"),
        P("gx", "gy", "gz"),
        P("gx", "gy", "gz"),
        P(),
    )
    out_specs = (P("gx", "gy", "gz"), P("gx", "gy", "gz"), P(None, "gx", "gy", "gz"))
    return jax.shard_map(body, mesh=mesh, in_specs=in_specs, out_specs=out_specs, check_vma=False)
```

```python
import functools
import math

import jax
import jax.numpy as jnp
import numpy as np
from jax import lax
from jax.experimental import pallas as pl
from jax.experimental.pallas import tpu as pltpu
from jax.sharding import PartitionSpec as P

STEPS = 10

filter_radius = 2.5
penalty = 3.0
move_limit = 0.2
stiff_floor = 1e-09
volume_share = 0.5
log_lower = -20.0
log_upper = 20.0
poisson = 0.3

SX, SY, SZ = 8, 8, 256
ROWS, LANES, SIDE = 16, 384, 128
NODES, ELEMENTS, CHOSEN = SX + 10, SX + 9, SX + 5
POINTS = 2**STEPS
F32 = jnp.float32


def corner_offsets():
    return [(q // 4, q // 2 % 2, q % 2) for q in range(8)]


def hex_stiffness():
    lame_first = poisson / ((1.0 + poisson) * (1.0 - 2.0 * poisson))
    shear_modulus = 0.5 / (1.0 + poisson)
    elastic = np.zeros((6, 6))
    elastic[:3, :3] = lame_first
    for d in range(3):
        elastic[d, d] += 2.0 * shear_modulus
        elastic[d + 3, d + 3] = shear_modulus
    corners = corner_offsets()
    points = [0.5 - 0.5 / math.sqrt(3.0), 0.5 + 0.5 / math.sqrt(3.0)]
    matrix = np.zeros((24, 24))
    for p in points:
        for q in points:
            for r in points:
                location = [p, q, r]
                gradients = np.zeros((8, 3))
                for n in range(8):
                    factors = [
                        location[e] if corners[n][e] == 1 else 1.0 - location[e] for e in range(3)
                    ]
                    for d in range(3):
                        sign_value = 1.0 if corners[n][d] == 1 else -1.0
                        gradients[n, d] = sign_value * factors[(d + 1) % 3] * factors[(d + 2) % 3]
                strain = np.zeros((6, 24))
                for n in range(8):
                    column = 3 * n
                    strain[0, column] = gradients[n, 0]
                    strain[1, column + 1] = gradients[n, 1]
                    strain[2, column + 2] = gradients[n, 2]
                    strain[3, column + 1] = gradients[n, 2]
                    strain[3, column + 2] = gradients[n, 1]
                    strain[4, column] = gradients[n, 2]
                    strain[4, column + 2] = gradients[n, 0]
                    strain[5, column] = gradients[n, 1]
                    strain[5, column + 1] = gradients[n, 0]
                matrix += strain.T @ elastic @ strain / 8.0
    return matrix


def energy_groups():
    corners = corner_offsets()
    modes = np.zeros((24, 24))
    for s in range(8):
        bits = (s // 4, s // 2 % 2, s % 2)
        for n in range(8):
            sign_value = 1.0
            for e in range(3):
                if bits[e] == 1 and corners[n][e] == 0:
                    sign_value = -sign_value
            for d in range(3):
                modes[3 * n + d, 3 * s + d] = sign_value
    form = modes.T @ hex_stiffness() @ modes / 64.0
    groups = []

    def add(coefficient, members):
        if abs(coefficient) < 1e-9:
            return
        for group in groups:
            if abs(group[0] - coefficient) < 1e-9:
                group[1].append(members)
                return
        groups.append((coefficient, [members]))

    for parity in range(8):
        left = [3 * (parity ^ (4, 2, 1)[d]) + d for d in range(3)]
        while left:
            first = left[0]
            block = [m for m in left if m == first or abs(form[first, m]) > 1e-9]
            left = [m for m in left if m not in block]
            beside = form[block[0], block[1]] if len(block) > 1 else 0.0
            add(beside, block)
            for m in block:
                add(form[m, m] - beside, [m])
    rebuilt = np.zeros((24, 24))
    for coefficient, sums in groups:
        for members in sums:
            rebuilt[np.ix_(members, members)] += coefficient
    assert np.abs(rebuilt - form).max() < 1e-9
    return groups


def corner_factors():
    matrix = hex_stiffness()
    factors = (matrix[0, 0], matrix[1, 2], matrix[0, 2], matrix[0, 1])
    for n, corner in enumerate(corner_offsets()):
        sign = [1.0 if c == 1 else -1.0 for c in corner]
        block = matrix[3 * n : 3 * n + 3, 3 * n : 3 * n + 3]
        assert np.allclose(np.diag(block), factors[0])
        assert np.allclose(block[1, 2], factors[1] * sign[1] * sign[2])
        assert np.allclose(block[0, 2], factors[2] * sign[0] * sign[2])
        assert np.allclose(block[0, 1], factors[3] * sign[0] * sign[1])
    return factors


def tap(square):
    return max(0.0, filter_radius - math.sqrt(square))


def rolled(value, steps, dim):
    return pltpu.roll(value, (-steps) % value.shape[dim], dim)


def row_pairs(plane):
    return (
        rolled(plane, 1, 0) + rolled(plane, -1, 0),
        rolled(plane, 2, 0) + rolled(plane, -2, 0),
    )


def filtered_plane(plane_of, near_of, far_of, p):
    ring_0 = plane_of(p)
    ring_1 = near_of(p) + plane_of(p - 1) + plane_of(p + 1)
    ring_2 = near_of(p - 1) + near_of(p + 1)
    ring_4 = far_of(p) + plane_of(p - 2) + plane_of(p + 2)
    ring_5 = far_of(p - 1) + far_of(p + 1) + near_of(p - 2) + near_of(p + 2)
    layers = []
    for c in (0, 1, 2):
        total = None
        for square, ring in ((0, ring_0), (1, ring_1), (2, ring_2), (4, ring_4), (5, ring_5)):
            weight = tap(square + c * c)
            if weight > 0.0:
                total = weight * ring if total is None else total + weight * ring
        layers.append(total)
    middle, near, far = layers
    return middle + (rolled(near, 1, 1) + rolled(near, -1, 1)) + (rolled(far, 2, 1) + rolled(far, -2, 1))


def weights_kernel(
    own_ref, support_ref, own_copy, inverse_ref, volume_ref, mark_ref, near_ref, far_ref, semaphore, *, extents
):
    copy = pltpu.make_async_copy(own_ref, own_copy, semaphore)
    copy.start()
    total_x, total_y, total_z = extents
    first_x = lax.axis_index("gx") * SX
    first_y = lax.axis_index("gy") * SY
    first_z = lax.axis_index("gz") * SZ
    row = lax.broadcasted_iota(jnp.int32, (ROWS, LANES), 0)
    lane = lax.broadcasted_iota(jnp.int32, (ROWS, LANES), 1)
    y = first_y + jnp.where(row < 12, row, row - ROWS)
    z = first_z + jnp.where(lane < SZ + SIDE // 2, lane, lane - LANES)
    inside = jnp.where((y >= 0) & (y < total_y) & (z >= 0) & (z < total_z), 1.0, 0.0).astype(F32)
    near, far = row_pairs(inside)

    def present(p):
        x = first_x + p
        return jnp.where((x >= 0) & (x < total_x), 1.0, 0.0).astype(F32)

    for p in range(ELEMENTS):
        x = p - 5
        weight_sum = filtered_plane(
            lambda q: inside * present(q), lambda q: near * present(q), lambda q: far * present(q), x
        )
        here = inside * present(x)
        inverse = jnp.where(here > 0.0, 1.0 / jnp.where(here > 0.0, weight_sum, 1.0), 0.0)
        inverse_ref[p] = inverse
        inverse_near, inverse_far = row_pairs(inverse)
        near_ref[p] = inverse_near[0:SY]
        far_ref[p] = inverse_far[0:SY]
    for p in range(CHOSEN):
        volume_ref[p] = filtered_plane(
            lambda q: inverse_ref[q, 0:SY], lambda q: near_ref[q], lambda q: far_ref[q], p + 2
        )
    node = support_ref[...]
    node_x = node // (total_y * total_z) - first_x
    node_y = node // total_z % total_y - first_y
    node_z = node % total_z - first_z
    owned = (node_x >= 0) & (node_x < SX) & (node_y >= 0) & (node_y < SY)
    line = jnp.where(owned, node_x * SY + node_y, -1)
    count = node.shape[1]
    lines = jnp.where(lax.broadcasted_iota(jnp.int32, (SX * SY, count), 0) == line, 1.0, 0.0)
    lanes = jnp.where(lax.broadcasted_iota(jnp.int32, (SZ, count), 0) == node_z, 1.0, 0.0)
    hits = lax.dot_general(
        lines.astype(jnp.bfloat16),
        lanes.astype(jnp.bfloat16),
        (((1,), (1,)), ((), ())),
        preferred_element_type=F32,
    )
    for p in range(SX):
        mark_ref[p] = hits[p * SY : (p + 1) * SY]
    copy.wait()


def is_even(axis):
    return (lax.axis_index(axis) + lax.axis_index("gz")) % 2 == 0


def place_pair(even, first_ref, second_ref, top, bottom, place):
    first_ref[place] = jnp.where(even, top, bottom)
    second_ref[place] = jnp.where(even, bottom, top)


def low_high(even, first_ref, second_ref, place):
    first, second = first_ref[place], second_ref[place]
    return jnp.where(even, second, first), jnp.where(even, first, second)


def row_place(index):
    if index < 3 * NODES:
        return slice(3 * index, 3 * index + 3)
    return slice(2 * index + 3 * NODES, 2 * index + 3 * NODES + 2)


def row_tile(even, first_ref, second_ref, place):
    low, high = low_high(even, first_ref, second_ref, place)
    filler = jnp.zeros((SY - 2 * low.shape[0], low.shape[1]), F32)
    return jnp.concatenate([high, filler, low], axis=0)


def faces_x_kernel(
    shift_ref, physical_ref, design_ref, passive_ref, own_ref, first_ref, second_ref, passive_own, semaphores
):
    pairs = (
        (shift_ref, own_ref.at[0:3]),
        (physical_ref, own_ref.at[3]),
        (design_ref, own_ref.at[4]),
        (passive_ref, passive_own),
    )
    copies = [pltpu.make_async_copy(*pair, semaphores.at[n]) for n, pair in enumerate(pairs)]
    for copy in copies:
        copy.start()
    for copy in copies:
        copy.wait()
    own_ref[5] = passive_own[...].astype(F32)
    even = is_even("gx")
    for f in range(6):
        depth = 5 if f < 4 else 3
        row = 5 * f if f < 4 else 8 + 3 * f
        place_pair(
            even, first_ref, second_ref, own_ref[f, SX - depth :], own_ref[f, 0:depth], slice(row, row + depth)
        )


def plane_reader(own_ref, x_first, x_second):
    even = is_even("gx")

    def read(index):
        if index < 4 * NODES:
            f, x = index // NODES, index % NODES - 5
            depth, base = 5, 5 * f
        else:
            f, x = 4 + (index - 4 * NODES) // CHOSEN, (index - 4 * NODES) % CHOSEN - 3
            depth, base = 3, 8 + 3 * f
        if 0 <= x < SX:
            return own_ref[f, x]
        low, high = low_high(even, x_first, x_second, base + (x + depth if x < 0 else x - SX))
        return low if x < 0 else high

    return read


def faces_y_kernel(
    own_ref, x_first, x_second, first_ref, second_ref, side_ref
):
    even = is_even("gy")
    lower_core = lax.axis_index("gz") == 0
    read = plane_reader(own_ref, x_first, x_second)
    for index in range(4 * NODES + 2 * CHOSEN):
        plane = read(index)
        if index < 4 * NODES:
            rows = row_place(index)
            depth = rows.stop - rows.start
            place_pair(even, first_ref, second_ref, plane[SY - depth :], plane[0:depth], rows)
        side_ref[index] = jnp.where(lower_core, plane[:, SZ - SIDE :], plane[:, 0:SIDE])


def faces_z_kernel(y_first, y_second, side_ref):
    even = is_even("gy")
    lower_core = lax.axis_index("gz") == 0
    for index in range(4 * NODES):
        tile = row_tile(even, y_first, y_second, row_place(index))
        side_ref[index] = jnp.where(lower_core, tile[:, SZ - SIDE :], tile[:, 0:SIDE])


def design_kernel(
    own_ref, x_first, x_second, y_first, y_second, side, y_side, inverse_ref, volume_ref, out_ref, first_ref,
    second_ref, part_ref, ext_ref, sens_ref, near_ref, far_ref, high_ref, low_ref, value_ref, *, groups
):
    lane = lax.broadcasted_iota(jnp.int32, (SY, SIDE), 1)
    start = lax.axis_index("gz") * (SIDE // 2)
    keep = (lane >= start) & (lane < start + SIDE // 2)
    even = is_even("gy")
    read = plane_reader(own_ref, x_first, x_second)
    for f in range(4):
        for p in range(NODES):
            index = NODES * f + p
            ext_ref[f, p, 0:SY, 0:SZ] = read(index)
            ext_ref[f, p, 0:SY, SZ:LANES] = jnp.where(keep, side[index], 0.0)
            ext_ref[f, p, SY:ROWS, 0:SZ] = row_tile(even, y_first, y_second, row_place(index))
            ext_ref[f, p, SY:ROWS, SZ:LANES] = jnp.where(keep, y_side[index], 0.0)
    scale = penalty * (1.0 - stiff_floor)

    @pl.loop(0, ELEMENTS)
    def _(p):
        modes = {}
        for d in range(3):
            here, above = ext_ref[d, p], ext_ref[d, p + 1]
            for a, along_x in enumerate((here + above, above - here)):
                beyond = rolled(along_x, 1, 0)
                for b, along_y in enumerate((along_x + beyond, beyond - along_x)):
                    next_lane = rolled(along_y, 1, 1)
                    for c, mode in enumerate((along_y + next_lane, next_lane - along_y)):
                        modes[3 * (4 * a + 2 * b + c) + d] = mode
        energy = None
        for coefficient, sums in groups:
            squares = None
            for members in sums:
                value = functools.reduce(lambda left, right: left + right, [modes[m] for m in members])
                squares = value * value if squares is None else squares + value * value
            squares = float(coefficient) * squares
            energy = squares if energy is None else energy + squares
        density = ext_ref[3, p]
        sens = scale * density * density * energy * inverse_ref[p]
        sens_ref[p] = sens[0:SY]
        near, far = row_pairs(sens)
        near_ref[p] = near[0:SY]
        far_ref[p] = far[0:SY]

    for p in range(CHOSEN):
        filtered = filtered_plane(lambda q: sens_ref[q], lambda q: near_ref[q], lambda q: far_ref[q], p + 2)
        index = 4 * NODES + p
        design = jnp.concatenate([read(index), side[index]], axis=1)
        solid = jnp.concatenate([read(index + CHOSEN), side[index + CHOSEN]], axis=1) > 0.5
        inside = inverse_ref[p + 2, 0:SY] > 0.0
        scaled = design * jnp.sqrt(filtered / jnp.where(inside, volume_ref[p], 1.0))
        floor_bound = jnp.where(solid, 1.0, jnp.maximum(0.0, design - move_limit))
        ceiling = jnp.where(solid, 1.0, jnp.minimum(1.0, design + move_limit))
        for f, value in enumerate((scaled, floor_bound, ceiling)):
            value = jnp.where(inside, value, 0.0)
            out_ref[f, p] = value
            row = 3 * (CHOSEN * f + p)
            place_pair(even, first_ref, second_ref, value[SY - 3 :], value[0:3], slice(row, row + 3))
    add_volumes(out_ref, volume_ref, part_ref, high_ref, low_ref, value_ref)


def three_parts(value):
    first = value.astype(jnp.bfloat16).astype(F32)
    second = (value - first).astype(jnp.bfloat16).astype(F32)
    return first, second, value - first - second


def add_volumes(bounds_ref, volume_ref, out_ref, high_ref, low_ref, value_ref):
    step = (log_upper - log_lower) / POINTS
    ceilings = jnp.zeros((SY, 128), F32)
    for v in range(2 * SX):
        place = (3 + v // 2, slice(None), slice(128 * (v % 2), 128 * (v % 2 + 1)))
        weight = volume_ref[place]
        scaled, floor_bound, ceiling = [bounds_ref[(f,) + place] for f in range(3)]
        ceilings = ceilings + weight * ceiling
        log_scaled = jnp.log(jnp.maximum(scaled, 1e-30))
        for t, bound in enumerate((ceiling, floor_bound)):
            reached = (2.0 * (log_scaled - jnp.log(jnp.maximum(bound, 1e-30))) - log_lower) / step
            index = jnp.minimum(jnp.maximum(jnp.ceil(reached), 1.0), POINTS + 1.0) - 1.0
            index = jnp.where(bound > 0.0, index, float(POINTS))
            high = jnp.floor(index * (1.0 / 128.0))
            high_ref[t, v] = high
            low_ref[t, v] = index - 128.0 * high
            sign = -1.0 if t == 0 else 1.0
            parts = three_parts(sign * weight * bound) + three_parts(-sign * weight * scaled)
            for n, part in enumerate(parts):
                value_ref[t, n, v] = part

    rows = lax.broadcasted_iota(jnp.int32, (8, 128), 0).astype(F32)
    columns = lax.broadcasted_iota(jnp.int32, (128, 128), 0).astype(F32).astype(jnp.bfloat16)

    def add_group(v, total):
        lefts, rights = [], []
        for t in range(2):
            for r in range(SY):
                hit = rows == high_ref[t, v, r : r + 1, :]
                left = [jnp.where(hit, value_ref[t, n, v, r : r + 1, :], 0.0) for n in range(6)]
                lefts.append(jnp.concatenate(left, axis=0).astype(jnp.bfloat16))
                low = jnp.broadcast_to(low_ref[t, v, r : r + 1, :], (16, 128)).astype(jnp.bfloat16)
                low = jnp.concatenate([low] * 8, axis=0)
                rights.append(jnp.where(columns == low, jnp.bfloat16(1.0), jnp.bfloat16(0.0)))
        return total + lax.dot_general(
            jnp.concatenate(rights, axis=1),
            jnp.concatenate(lefts, axis=1),
            (((1,), (1,)), ((), ())),
            preferred_element_type=F32,
        )

    total = lax.fori_loop(0, 2 * SX, add_group, jnp.zeros((128, 48), F32), unroll=4).T
    constant = total[0:8] + total[8:16] + total[16:24]
    slope = total[24:32] + total[32:40] + total[40:48]
    upto = jnp.where(
        lax.broadcasted_iota(jnp.int32, (128, 128), 0) <= lax.broadcasted_iota(jnp.int32, (128, 128), 1), 1.0, 0.0
    )
    running = lax.dot_general(
        jnp.concatenate([constant, slope], axis=0),
        upto,
        (((1,), (0,)), ((), ())),
        precision=lax.Precision.HIGHEST,
        preferred_element_type=F32,
    )
    row = lax.broadcasted_iota(jnp.int32, (8, 128), 0)
    lane = lax.broadcasted_iota(jnp.int32, (8, 128), 1)
    cumulated = []
    for part in (running[0:8], running[8:16]):
        ends = jnp.broadcast_to(part[:, 127:128], (8, 128))
        before = ends
        for shift in (1, 2, 4):
            before = before + jnp.where(row >= shift, rolled(before, -shift, 0), 0.0)
        cumulated.append(part + (before - ends))
    index = (row * 128 + lane + 1).astype(F32)
    factor = jnp.exp(-0.5 * (log_lower + step * index))
    result = jnp.sum(ceilings) + cumulated[0] + factor * cumulated[1]
    for i in range(out_ref.shape[0]):
        out_ref[i] = result


def repeat_kernel(part_ref, out_ref):
    total = part_ref[0]
    for i in range(1, part_ref.shape[0]):
        total = total + part_ref[i]
    for i in range(out_ref.shape[0]):
        out_ref[i] = total


def final_kernel(
    part_ref, own_ref, y_first, y_second, inverse_ref, mark_ref, new_design_ref, new_physical_ref,
    blocks_ref, chosen_ref, near_ref, far_ref, stiff_ref, *, factors, target
):
    total = part_ref[0]
    for i in range(1, part_ref.shape[0]):
        total = total + part_ref[i]
    low_end = jnp.minimum(jnp.sum(jnp.where(total > target, 1.0, 0.0)), POINTS - 1.0)
    multiplier = log_lower + (log_upper - log_lower) / POINTS * (low_end + 0.5)
    factor = jnp.exp(jnp.broadcast_to(-0.5 * multiplier, (SY, LANES)))
    even = is_even("gy")
    for p in range(CHOSEN):
        tiles = []
        own = [own_ref[f, p] for f in range(3)]
        beside = []
        for f in range(3):
            row = 3 * (CHOSEN * f + p)
            beside.append(row_tile(even, y_first, y_second, slice(row, row + 3)))
        for scaled, floor_bound, ceiling in (own, beside):
            tiles.append(jnp.minimum(jnp.maximum(scaled * factor, floor_bound), ceiling))
        chosen = jnp.concatenate(tiles, axis=0)
        chosen_ref[p] = chosen
        near, far = row_pairs(chosen)
        near_ref[p] = near
        far_ref[p] = far
        if 3 <= p < SX + 3:
            new_design_ref[p - 3] = tiles[0][:, 0:SZ]
    for p in range(SX + 1):
        inverse = inverse_ref[p + 4]
        density = (
            filtered_plane(lambda q: chosen_ref[q], lambda q: near_ref[q], lambda q: far_ref[q], p + 2) * inverse
        )
        if p >= 1:
            new_physical_ref[p - 1] = density[0:SY, 0:SZ]
        cube = stiff_floor + density * density * density * (1.0 - stiff_floor)
        stiff_ref[p] = jnp.where(inverse > 0.0, cube, 0.0)
    for p in range(SX):
        below, here = stiff_ref[p], stiff_ref[p + 1]
        x_sum, x_diff = here + below, below - here
        x_sum_back, x_diff_back = rolled(x_sum, -1, 0), rolled(x_diff, -1, 0)
        sum_sum = (x_sum + x_sum_back)[0:SY]
        sum_diff = (x_sum_back - x_sum)[0:SY]
        diff_sum = (x_diff + x_diff_back)[0:SY]
        diff_diff = (x_diff_back - x_diff)[0:SY]
        marked = mark_ref[p] > 0.5
        even = factors[0] * (sum_sum + rolled(sum_sum, -1, 1))[:, 0:SZ]
        even = jnp.where(marked, 1.0, even)
        blocks_ref[0, p] = even
        blocks_ref[1, p] = even
        blocks_ref[2, p] = even
        yz = factors[1] * (rolled(sum_diff, -1, 1) - sum_diff)[:, 0:SZ]
        xz = factors[2] * (rolled(diff_sum, -1, 1) - diff_sum)[:, 0:SZ]
        xy = factors[3] * (diff_diff + rolled(diff_diff, -1, 1))[:, 0:SZ]
        blocks_ref[3, p] = jnp.where(marked, 0.0, yz)
        blocks_ref[4, p] = jnp.where(marked, 0.0, xz)
        blocks_ref[5, p] = jnp.where(marked, 0.0, xy)


def call(kernel, inputs, shapes, scratch, flops, spaces=None, grant=32):
    outs = [jax.ShapeDtypeStruct(shape, F32) for shape in shapes]
    return pl.pallas_call(
        kernel,
        out_shape=outs,
        in_specs=[pl.BlockSpec(memory_space=space) for space in spaces or [pltpu.VMEM] * len(inputs)],
        out_specs=[pl.BlockSpec(memory_space=pltpu.VMEM)] * len(outs),
        scratch_shapes=[pltpu.VMEM(shape, F32) if isinstance(shape, tuple) else shape for shape in scratch],
        compiler_params=pltpu.CompilerParams(vmem_limit_bytes=grant * 2**20),
        cost_estimate=pl.CostEstimate(flops=flops, bytes_accessed=10**6, transcendentals=0),
    )(*inputs)


def exchange(first, second, axis):
    count = lax.axis_size(axis)
    results = []
    for turn, faces in enumerate((first, second)):
        moves = []
        for core in range(2):
            for i in range((turn + core) % 2, count - 1, 2):
                moves += [(2 * i + core, 2 * i + 2 + core), (2 * i + 2 + core, 2 * i + core)]
        results.append(lax.ppermute(faces, (axis, "gz"), moves))
    return results


def other_core(values):
    return lax.ppermute(values, "gz", [(0, 1), (1, 0)])


def body(displacement, physical, design, passive, supports):
    assert design.shape == (SX, SY, SZ) and lax.axis_size("gz") == 2
    sizes = [lax.axis_size(axis) for axis in ("gx", "gy", "gz")]
    extents = (SX * sizes[0], SY * sizes[1], SZ * sizes[2])
    block = (SX, SY, SZ)
    faces = (26, SY, SZ)
    own, *x_faces = call(
        faces_x_kernel, (displacement, physical, design, passive), [(6,) + block, faces, faces],
        [pltpu.VMEM(block, jnp.int32), pltpu.SemaphoreType.DMA((4,))], 10**6, [pltpu.HBM] * 4, 62,
    )
    x_faces = exchange(*x_faces, "gx")
    frame = (ELEMENTS, ROWS, LANES)
    own_frame = (ELEMENTS, SY, LANES)
    weights = call(
        functools.partial(weights_kernel, extents=extents), (own, supports.reshape(1, -1)),
        [(6,) + block, frame, (CHOSEN, SY, LANES), block],
        [own_frame, own_frame, pltpu.SemaphoreType.DMA(())], 10**7, [pltpu.HBM, pltpu.VMEM],
    )
    x_faces, (own, inverse, volume_weight, marks) = lax.optimization_barrier((x_faces, weights))

    faces = (11 * NODES, SZ)
    *y_faces, side = call(
        faces_y_kernel, (own, *x_faces), [faces, faces, (4 * NODES + 2 * CHOSEN, SY, SIDE)], [], 10**6
    )
    y_faces = exchange(*y_faces, "gy")
    side = other_core(side)
    (y_side,) = call(faces_z_kernel, y_faces, [(4 * NODES, SY, SIDE)], [], 10**6)
    y_side = other_core(y_side)

    faces = (9 * CHOSEN, LANES)
    inner, outer = sizes[1] * sizes[2], sizes[0]
    elements = (2 * SX, SY, 128)
    bounds, *y_bounds, part = call(
        functools.partial(design_kernel, groups=energy_groups()),
        (own, *x_faces, *y_faces, side, y_side, inverse, volume_weight),
        [(3, CHOSEN, SY, LANES), faces, faces, (inner, 8, 128)],
        [(4, NODES, ROWS, LANES), own_frame, own_frame, own_frame]
        + [(2,) + elements, (2,) + elements, (2, 6) + elements], 10**7,
    )

    part = lax.all_to_all(part, ("gy", "gz"), 0, 0, tiled=True)
    y_bounds, part = lax.optimization_barrier((y_bounds, part))
    y_bounds = exchange(*y_bounds, "gy")
    (part,) = call(repeat_kernel, (part,), [(outer, 8, 128)], [], 10**5)
    part = lax.all_to_all(part, "gx", 0, 0, tiled=True)

    chosen = (CHOSEN, ROWS, LANES)
    target = volume_share * (extents[0] * extents[1] * extents[2])
    new_design, new_physical, node_blocks = call(
        functools.partial(final_kernel, factors=[float(f) for f in corner_factors()], target=target),
        (part, bounds, *y_bounds, inverse, marks), [block, block, (6,) + block],
        [chosen, chosen, chosen, (SX + 1, ROWS, LANES)], 10**7,
    )
    return (new_design, new_physical, node_blocks)


def solution(mesh):
    in_specs = (
        P(None, "gx", "gy", "gz"),
        P("gx", "gy", "gz"),
        P("gx", "gy", "gz"),
        P("gx", "gy", "gz"),
        P(),
    )
    out_specs = (P("gx", "gy", "gz"), P("gx", "gy", "gz"), P(None, "gx", "gy", "gz"))
    return jax.shard_map(body, mesh=mesh, in_specs=in_specs, out_specs=out_specs, check_vma=False)
```

```python
import functools
import math

import jax
import jax.numpy as jnp
import numpy as np
from jax import lax
from jax.experimental import pallas as pl
from jax.experimental.pallas import tpu as pltpu
from jax.sharding import PartitionSpec as P

STEPS = 10

filter_radius = 2.5
penalty = 3.0
move_limit = 0.2
stiff_floor = 1e-09
volume_share = 0.5
log_lower = -20.0
log_upper = 20.0
poisson = 0.3

SX, SY, SZ = 8, 8, 256
ROWS, LANES, SIDE = 16, 384, 128
NODES, ELEMENTS, CHOSEN = SX + 10, SX + 9, SX + 5
POINTS = 2**STEPS
F32 = jnp.float32


def corner_offsets():
    return [(q // 4, q // 2 % 2, q % 2) for q in range(8)]


def hex_stiffness():
    lame_first = poisson / ((1.0 + poisson) * (1.0 - 2.0 * poisson))
    shear_modulus = 0.5 / (1.0 + poisson)
    elastic = np.zeros((6, 6))
    elastic[:3, :3] = lame_first
    for d in range(3):
        elastic[d, d] += 2.0 * shear_modulus
        elastic[d + 3, d + 3] = shear_modulus
    corners = corner_offsets()
    points = [0.5 - 0.5 / math.sqrt(3.0), 0.5 + 0.5 / math.sqrt(3.0)]
    matrix = np.zeros((24, 24))
    for p in points:
        for q in points:
            for r in points:
                location = [p, q, r]
                gradients = np.zeros((8, 3))
                for n in range(8):
                    factors = [
                        location[e] if corners[n][e] == 1 else 1.0 - location[e] for e in range(3)
                    ]
                    for d in range(3):
                        sign_value = 1.0 if corners[n][d] == 1 else -1.0
                        gradients[n, d] = sign_value * factors[(d + 1) % 3] * factors[(d + 2) % 3]
                strain = np.zeros((6, 24))
                for n in range(8):
                    column = 3 * n
                    strain[0, column] = gradients[n, 0]
                    strain[1, column + 1] = gradients[n, 1]
                    strain[2, column + 2] = gradients[n, 2]
                    strain[3, column + 1] = gradients[n, 2]
                    strain[3, column + 2] = gradients[n, 1]
                    strain[4, column] = gradients[n, 2]
                    strain[4, column + 2] = gradients[n, 0]
                    strain[5, column] = gradients[n, 1]
                    strain[5, column + 1] = gradients[n, 0]
                matrix += strain.T @ elastic @ strain / 8.0
    return matrix


def energy_groups():
    corners = corner_offsets()
    modes = np.zeros((24, 24))
    for s in range(8):
        bits = (s // 4, s // 2 % 2, s % 2)
        for n in range(8):
            sign_value = 1.0
            for e in range(3):
                if bits[e] == 1 and corners[n][e] == 0:
                    sign_value = -sign_value
            for d in range(3):
                modes[3 * n + d, 3 * s + d] = sign_value
    form = modes.T @ hex_stiffness() @ modes / 64.0
    groups = []

    def add(coefficient, members):
        if abs(coefficient) < 1e-9:
            return
        for group in groups:
            if abs(group[0] - coefficient) < 1e-9:
                group[1].append(members)
                return
        groups.append((coefficient, [members]))

    for parity in range(8):
        left = [3 * (parity ^ (4, 2, 1)[d]) + d for d in range(3)]
        while left:
            first = left[0]
            block = [m for m in left if m == first or abs(form[first, m]) > 1e-9]
            left = [m for m in left if m not in block]
            beside = form[block[0], block[1]] if len(block) > 1 else 0.0
            add(beside, block)
            for m in block:
                add(form[m, m] - beside, [m])
    rebuilt = np.zeros((24, 24))
    for coefficient, sums in groups:
        for members in sums:
            rebuilt[np.ix_(members, members)] += coefficient
    assert np.abs(rebuilt - form).max() < 1e-9
    return groups


def corner_factors():
    matrix = hex_stiffness()
    factors = (matrix[0, 0], matrix[1, 2], matrix[0, 2], matrix[0, 1])
    for n, corner in enumerate(corner_offsets()):
        sign = [1.0 if c == 1 else -1.0 for c in corner]
        block = matrix[3 * n : 3 * n + 3, 3 * n : 3 * n + 3]
        assert np.allclose(np.diag(block), factors[0])
        assert np.allclose(block[1, 2], factors[1] * sign[1] * sign[2])
        assert np.allclose(block[0, 2], factors[2] * sign[0] * sign[2])
        assert np.allclose(block[0, 1], factors[3] * sign[0] * sign[1])
    return factors


def tap(square):
    return max(0.0, filter_radius - math.sqrt(square))


def rolled(value, steps, dim):
    return pltpu.roll(value, (-steps) % value.shape[dim], dim)


def row_pairs(plane):
    return (
        rolled(plane, 1, 0) + rolled(plane, -1, 0),
        rolled(plane, 2, 0) + rolled(plane, -2, 0),
    )


def filtered_plane(plane_of, near_of, far_of, p):
    ring_0 = plane_of(p)
    ring_1 = near_of(p) + plane_of(p - 1) + plane_of(p + 1)
    ring_2 = near_of(p - 1) + near_of(p + 1)
    ring_4 = far_of(p) + plane_of(p - 2) + plane_of(p + 2)
    ring_5 = far_of(p - 1) + far_of(p + 1) + near_of(p - 2) + near_of(p + 2)
    layers = []
    for c in (0, 1, 2):
        total = None
        for square, ring in ((0, ring_0), (1, ring_1), (2, ring_2), (4, ring_4), (5, ring_5)):
            weight = tap(square + c * c)
            if weight > 0.0:
                total = weight * ring if total is None else total + weight * ring
        layers.append(total)
    middle, near, far = layers
    return middle + (rolled(near, 1, 1) + rolled(near, -1, 1)) + (rolled(far, 2, 1) + rolled(far, -2, 1))


def weights_kernel(
    own_ref, support_ref, own_copy, inverse_ref, volume_ref, mark_ref, near_ref, far_ref, semaphore, *, extents
):
    copy = pltpu.make_async_copy(own_ref, own_copy, semaphore)
    copy.start()
    total_x, total_y, total_z = extents
    first_x = lax.axis_index("gx") * SX
    first_y = lax.axis_index("gy") * SY
    first_z = lax.axis_index("gz") * SZ
    row = lax.broadcasted_iota(jnp.int32, (ROWS, LANES), 0)
    lane = lax.broadcasted_iota(jnp.int32, (ROWS, LANES), 1)
    y = first_y + jnp.where(row < 12, row, row - ROWS)
    z = first_z + jnp.where(lane < SZ + SIDE // 2, lane, lane - LANES)
    inside = jnp.where((y >= 0) & (y < total_y) & (z >= 0) & (z < total_z), 1.0, 0.0).astype(F32)
    near, far = row_pairs(inside)

    def present(p):
        x = first_x + p
        return jnp.where((x >= 0) & (x < total_x), 1.0, 0.0).astype(F32)

    for p in range(ELEMENTS):
        x = p - 5
        weight_sum = filtered_plane(
            lambda q: inside * present(q), lambda q: near * present(q), lambda q: far * present(q), x
        )
        here = inside * present(x)
        inverse = jnp.where(here > 0.0, 1.0 / jnp.where(here > 0.0, weight_sum, 1.0), 0.0)
        inverse_ref[p] = inverse
        inverse_near, inverse_far = row_pairs(inverse)
        near_ref[p] = inverse_near[0:SY]
        far_ref[p] = inverse_far[0:SY]
    for p in range(CHOSEN):
        volume_ref[p] = filtered_plane(
            lambda q: inverse_ref[q, 0:SY], lambda q: near_ref[q], lambda q: far_ref[q], p + 2
        )
    node = support_ref[...]
    node_x = node // (total_y * total_z) - first_x
    node_y = node // total_z % total_y - first_y
    node_z = node % total_z - first_z
    owned = (node_x >= 0) & (node_x < SX) & (node_y >= 0) & (node_y < SY)
    line = jnp.where(owned, node_x * SY + node_y, -1)
    count = node.shape[1]
    lines = jnp.where(lax.broadcasted_iota(jnp.int32, (SX * SY, count), 0) == line, 1.0, 0.0)
    lanes = jnp.where(lax.broadcasted_iota(jnp.int32, (SZ, count), 0) == node_z, 1.0, 0.0)
    hits = lax.dot_general(
        lines.astype(jnp.bfloat16),
        lanes.astype(jnp.bfloat16),
        (((1,), (1,)), ((), ())),
        preferred_element_type=F32,
    )
    for p in range(SX):
        mark_ref[p] = hits[p * SY : (p + 1) * SY]
    copy.wait()


def is_even(axis):
    return lax.axis_index(axis) % 2 == 0


def place_pair(even, first_ref, second_ref, top, bottom, place):
    first_ref[place] = jnp.where(even, top, bottom)
    second_ref[place] = jnp.where(even, bottom, top)


def low_high(axis, first_ref, second_ref, place):
    index = lax.axis_index(axis)
    first, second = first_ref[place], second_ref[place]
    low = jnp.where(index == 0, 0.0, jnp.where(index % 2 == 0, second, first))
    high = jnp.where(index == lax.axis_size(axis) - 1, 0.0, jnp.where(index % 2 == 0, first, second))
    return low, high


def row_place(index):
    if index < 3 * NODES:
        return slice(3 * index, 3 * index + 3)
    return slice(2 * index + 3 * NODES, 2 * index + 3 * NODES + 2)


def row_tile(first_ref, second_ref, place):
    low, high = low_high("gy", first_ref, second_ref, place)
    filler = jnp.zeros((SY - 2 * low.shape[0], low.shape[1]), F32)
    return jnp.concatenate([high, filler, low], axis=0)


def faces_x_kernel(
    shift_ref, physical_ref, design_ref, passive_ref, own_ref, first_ref, second_ref, passive_own, semaphores
):
    pairs = (
        (shift_ref, own_ref.at[0:3]),
        (physical_ref, own_ref.at[3]),
        (design_ref, own_ref.at[4]),
        (passive_ref, passive_own),
    )
    copies = [pltpu.make_async_copy(*pair, semaphores.at[n]) for n, pair in enumerate(pairs)]
    for copy in copies:
        copy.start()
    for copy in copies:
        copy.wait()
    own_ref[5] = passive_own[...].astype(F32)
    even = is_even("gx")
    for f in range(6):
        depth = 5 if f < 4 else 3
        row = 5 * f if f < 4 else 8 + 3 * f
        place_pair(
            even, first_ref, second_ref, own_ref[f, SX - depth :], own_ref[f, 0:depth], slice(row, row + depth)
        )


def plane_reader(own_ref, x_first, x_second):
    def read(index):
        if index < 4 * NODES:
            f, x = index // NODES, index % NODES - 5
            depth, base = 5, 5 * f
        else:
            f, x = 4 + (index - 4 * NODES) // CHOSEN, (index - 4 * NODES) % CHOSEN - 3
            depth, base = 3, 8 + 3 * f
        if 0 <= x < SX:
            return own_ref[f, x]
        low, high = low_high("gx", x_first, x_second, base + (x + depth if x < 0 else x - SX))
        return low if x < 0 else high

    return read


def faces_y_kernel(
    own_ref, x_first, x_second, first_ref, second_ref, side_ref
):
    even = is_even("gy")
    lower_core = lax.axis_index("gz") == 0
    read = plane_reader(own_ref, x_first, x_second)
    for index in range(4 * NODES + 2 * CHOSEN):
        plane = read(index)
        if index < 4 * NODES:
            rows = row_place(index)
            depth = rows.stop - rows.start
            place_pair(even, first_ref, second_ref, plane[SY - depth :], plane[0:depth], rows)
        side_ref[index] = jnp.where(lower_core, plane[:, SZ - SIDE :], plane[:, 0:SIDE])


def faces_z_kernel(y_first, y_second, side_ref):
    lower_core = lax.axis_index("gz") == 0
    for index in range(4 * NODES):
        tile = row_tile(y_first, y_second, row_place(index))
        side_ref[index] = jnp.where(lower_core, tile[:, SZ - SIDE :], tile[:, 0:SIDE])


def design_kernel(
    own_ref, x_first, x_second, y_first, y_second, side, y_side, inverse_ref, volume_ref, out_ref, first_ref,
    second_ref, part_ref, ext_ref, sens_ref, near_ref, far_ref, high_ref, low_ref, value_ref, *, groups
):
    lane = lax.broadcasted_iota(jnp.int32, (SY, SIDE), 1)
    start = lax.axis_index("gz") * (SIDE // 2)
    keep = (lane >= start) & (lane < start + SIDE // 2)
    even = is_even("gy")
    read = plane_reader(own_ref, x_first, x_second)
    for f in range(4):
        for p in range(NODES):
            index = NODES * f + p
            ext_ref[f, p, 0:SY, 0:SZ] = read(index)
            ext_ref[f, p, 0:SY, SZ:LANES] = jnp.where(keep, side[index], 0.0)
            ext_ref[f, p, SY:ROWS, 0:SZ] = row_tile(y_first, y_second, row_place(index))
            ext_ref[f, p, SY:ROWS, SZ:LANES] = jnp.where(keep, y_side[index], 0.0)
    scale = penalty * (1.0 - stiff_floor)

    @pl.loop(0, ELEMENTS)
    def _(p):
        modes = {}
        for d in range(3):
            here, above = ext_ref[d, p], ext_ref[d, p + 1]
            for a, along_x in enumerate((here + above, above - here)):
                beyond = rolled(along_x, 1, 0)
                for b, along_y in enumerate((along_x + beyond, beyond - along_x)):
                    next_lane = rolled(along_y, 1, 1)
                    for c, mode in enumerate((along_y + next_lane, next_lane - along_y)):
                        modes[3 * (4 * a + 2 * b + c) + d] = mode
        energy = None
        for coefficient, sums in groups:
            squares = None
            for members in sums:
                value = functools.reduce(lambda left, right: left + right, [modes[m] for m in members])
                squares = value * value if squares is None else squares + value * value
            squares = float(coefficient) * squares
            energy = squares if energy is None else energy + squares
        density = ext_ref[3, p]
        sens = scale * density * density * energy * inverse_ref[p]
        sens_ref[p] = sens[0:SY]
        near, far = row_pairs(sens)
        near_ref[p] = near[0:SY]
        far_ref[p] = far[0:SY]

    for p in range(CHOSEN):
        filtered = filtered_plane(lambda q: sens_ref[q], lambda q: near_ref[q], lambda q: far_ref[q], p + 2)
        index = 4 * NODES + p
        design = jnp.concatenate([read(index), side[index]], axis=1)
        solid = jnp.concatenate([read(index + CHOSEN), side[index + CHOSEN]], axis=1) > 0.5
        inside = inverse_ref[p + 2, 0:SY] > 0.0
        scaled = design * jnp.sqrt(filtered / jnp.where(inside, volume_ref[p], 1.0))
        floor_bound = jnp.where(solid, 1.0, jnp.maximum(0.0, design - move_limit))
        ceiling = jnp.where(solid, 1.0, jnp.minimum(1.0, design + move_limit))
        for f, value in enumerate((scaled, floor_bound, ceiling)):
            value = jnp.where(inside, value, 0.0)
            out_ref[f, p] = value
            row = 3 * (CHOSEN * f + p)
            place_pair(even, first_ref, second_ref, value[SY - 3 :], value[0:3], slice(row, row + 3))
    add_volumes(out_ref, volume_ref, part_ref, high_ref, low_ref, value_ref)


def three_parts(value):
    first = value.astype(jnp.bfloat16).astype(F32)
    second = (value - first).astype(jnp.bfloat16).astype(F32)
    return first, second, value - first - second


def add_volumes(bounds_ref, volume_ref, out_ref, high_ref, low_ref, value_ref):
    step = (log_upper - log_lower) / POINTS
    ceilings = jnp.zeros((SY, 128), F32)
    for v in range(2 * SX):
        place = (3 + v // 2, slice(None), slice(128 * (v % 2), 128 * (v % 2 + 1)))
        weight = volume_ref[place]
        scaled, floor_bound, ceiling = [bounds_ref[(f,) + place] for f in range(3)]
        ceilings = ceilings + weight * ceiling
        log_scaled = jnp.log(jnp.maximum(scaled, 1e-30))
        for t, bound in enumerate((ceiling, floor_bound)):
            reached = (2.0 * (log_scaled - jnp.log(jnp.maximum(bound, 1e-30))) - log_lower) / step
            index = jnp.minimum(jnp.maximum(jnp.ceil(reached), 1.0), POINTS + 1.0) - 1.0
            index = jnp.where(bound > 0.0, index, float(POINTS))
            high = jnp.floor(index * (1.0 / 128.0))
            high_ref[t, v] = high
            low_ref[t, v] = index - 128.0 * high
            sign = -1.0 if t == 0 else 1.0
            parts = three_parts(sign * weight * bound) + three_parts(-sign * weight * scaled)
            for n, part in enumerate(parts):
                value_ref[t, n, v] = part

    rows = lax.broadcasted_iota(jnp.int32, (8, 128), 0).astype(F32)
    columns = lax.broadcasted_iota(jnp.int32, (128, 128), 0).astype(F32).astype(jnp.bfloat16)

    def add_group(v, total):
        lefts, rights = [], []
        for t in range(2):
            for r in range(SY):
                hit = rows == high_ref[t, v, r : r + 1, :]
                left = [jnp.where(hit, value_ref[t, n, v, r : r + 1, :], 0.0) for n in range(6)]
                lefts.append(jnp.concatenate(left, axis=0).astype(jnp.bfloat16))
                low = jnp.broadcast_to(low_ref[t, v, r : r + 1, :], (16, 128)).astype(jnp.bfloat16)
                low = jnp.concatenate([low] * 8, axis=0)
                rights.append(jnp.where(columns == low, jnp.bfloat16(1.0), jnp.bfloat16(0.0)))
        return total + lax.dot_general(
            jnp.concatenate(rights, axis=1),
            jnp.concatenate(lefts, axis=1),
            (((1,), (1,)), ((), ())),
            preferred_element_type=F32,
        )

    total = lax.fori_loop(0, 2 * SX, add_group, jnp.zeros((128, 48), F32), unroll=4).T
    constant = total[0:8] + total[8:16] + total[16:24]
    slope = total[24:32] + total[32:40] + total[40:48]
    upto = jnp.where(
        lax.broadcasted_iota(jnp.int32, (128, 128), 0) <= lax.broadcasted_iota(jnp.int32, (128, 128), 1), 1.0, 0.0
    )
    running = lax.dot_general(
        jnp.concatenate([constant, slope], axis=0),
        upto,
        (((1,), (0,)), ((), ())),
        precision=lax.Precision.HIGHEST,
        preferred_element_type=F32,
    )
    row = lax.broadcasted_iota(jnp.int32, (8, 128), 0)
    lane = lax.broadcasted_iota(jnp.int32, (8, 128), 1)
    cumulated = []
    for part in (running[0:8], running[8:16]):
        ends = jnp.broadcast_to(part[:, 127:128], (8, 128))
        before = ends
        for shift in (1, 2, 4):
            before = before + jnp.where(row >= shift, rolled(before, -shift, 0), 0.0)
        cumulated.append(part + (before - ends))
    index = (row * 128 + lane + 1).astype(F32)
    factor = jnp.exp(-0.5 * (log_lower + step * index))
    result = jnp.sum(ceilings) + cumulated[0] + factor * cumulated[1]
    for i in range(out_ref.shape[0]):
        out_ref[i] = result


def repeat_kernel(part_ref, out_ref):
    total = part_ref[0]
    for i in range(1, part_ref.shape[0]):
        total = total + part_ref[i]
    for i in range(out_ref.shape[0]):
        out_ref[i] = total


def final_kernel(
    part_ref, own_ref, y_first, y_second, inverse_ref, mark_ref, new_design_ref, new_physical_ref,
    blocks_ref, chosen_ref, near_ref, far_ref, stiff_ref, *, factors, target
):
    total = part_ref[0]
    for i in range(1, part_ref.shape[0]):
        total = total + part_ref[i]
    low_end = jnp.minimum(jnp.sum(jnp.where(total > target, 1.0, 0.0)), POINTS - 1.0)
    multiplier = log_lower + (log_upper - log_lower) / POINTS * (low_end + 0.5)
    factor = jnp.exp(jnp.broadcast_to(-0.5 * multiplier, (SY, LANES)))
    for p in range(CHOSEN):
        tiles = []
        own = [own_ref[f, p] for f in range(3)]
        beside = []
        for f in range(3):
            row = 3 * (CHOSEN * f + p)
            beside.append(row_tile(y_first, y_second, slice(row, row + 3)))
        for scaled, floor_bound, ceiling in (own, beside):
            tiles.append(jnp.minimum(jnp.maximum(scaled * factor, floor_bound), ceiling))
        chosen = jnp.concatenate(tiles, axis=0)
        chosen_ref[p] = chosen
        near, far = row_pairs(chosen)
        near_ref[p] = near
        far_ref[p] = far
        if 3 <= p < SX + 3:
            new_design_ref[p - 3] = tiles[0][:, 0:SZ]
    for p in range(SX + 1):
        inverse = inverse_ref[p + 4]
        density = (
            filtered_plane(lambda q: chosen_ref[q], lambda q: near_ref[q], lambda q: far_ref[q], p + 2) * inverse
        )
        if p >= 1:
            new_physical_ref[p - 1] = density[0:SY, 0:SZ]
        cube = stiff_floor + density * density * density * (1.0 - stiff_floor)
        stiff_ref[p] = jnp.where(inverse > 0.0, cube, 0.0)
    for p in range(SX):
        below, here = stiff_ref[p], stiff_ref[p + 1]
        x_sum, x_diff = here + below, below - here
        x_sum_back, x_diff_back = rolled(x_sum, -1, 0), rolled(x_diff, -1, 0)
        sum_sum = (x_sum + x_sum_back)[0:SY]
        sum_diff = (x_sum_back - x_sum)[0:SY]
        diff_sum = (x_diff + x_diff_back)[0:SY]
        diff_diff = (x_diff_back - x_diff)[0:SY]
        marked = mark_ref[p] > 0.5
        even = factors[0] * (sum_sum + rolled(sum_sum, -1, 1))[:, 0:SZ]
        even = jnp.where(marked, 1.0, even)
        blocks_ref[0, p] = even
        blocks_ref[1, p] = even
        blocks_ref[2, p] = even
        yz = factors[1] * (rolled(sum_diff, -1, 1) - sum_diff)[:, 0:SZ]
        xz = factors[2] * (rolled(diff_sum, -1, 1) - diff_sum)[:, 0:SZ]
        xy = factors[3] * (diff_diff + rolled(diff_diff, -1, 1))[:, 0:SZ]
        blocks_ref[3, p] = jnp.where(marked, 0.0, yz)
        blocks_ref[4, p] = jnp.where(marked, 0.0, xz)
        blocks_ref[5, p] = jnp.where(marked, 0.0, xy)


def call(kernel, inputs, shapes, scratch, flops, spaces=None, grant=32):
    outs = [jax.ShapeDtypeStruct(shape, F32) for shape in shapes]
    return pl.pallas_call(
        kernel,
        out_shape=outs,
        in_specs=[pl.BlockSpec(memory_space=space) for space in spaces or [pltpu.VMEM] * len(inputs)],
        out_specs=[pl.BlockSpec(memory_space=pltpu.VMEM)] * len(outs),
        scratch_shapes=[pltpu.VMEM(shape, F32) if isinstance(shape, tuple) else shape for shape in scratch],
        compiler_params=pltpu.CompilerParams(vmem_limit_bytes=grant * 2**20),
        cost_estimate=pl.CostEstimate(flops=flops, bytes_accessed=10**6, transcendentals=0),
    )(*inputs)


def exchange(first, second, axis):
    count = lax.axis_size(axis)
    results = []
    for start, faces in enumerate((first, second)):
        pairs = [(i, (i + 1) % count) for i in range(start, count, 2)]
        results.append(lax.ppermute(faces, axis, pairs + [(j, i) for i, j in pairs]))
    return results


def other_core(values):
    return lax.ppermute(values, "gz", [(0, 1), (1, 0)])


def body(displacement, physical, design, passive, supports):
    assert design.shape == (SX, SY, SZ) and lax.axis_size("gz") == 2
    sizes = [lax.axis_size(axis) for axis in ("gx", "gy", "gz")]
    extents = (SX * sizes[0], SY * sizes[1], SZ * sizes[2])
    block = (SX, SY, SZ)
    faces = (26, SY, SZ)
    own, *x_faces = call(
        faces_x_kernel, (displacement, physical, design, passive), [(6,) + block, faces, faces],
        [pltpu.VMEM(block, jnp.int32), pltpu.SemaphoreType.DMA((4,))], 10**6, [pltpu.HBM] * 4, 62,
    )
    x_faces = exchange(*x_faces, "gx")
    frame = (ELEMENTS, ROWS, LANES)
    own_frame = (ELEMENTS, SY, LANES)
    weights = call(
        functools.partial(weights_kernel, extents=extents), (own, supports.reshape(1, -1)),
        [(6,) + block, frame, (CHOSEN, SY, LANES), block],
        [own_frame, own_frame, pltpu.SemaphoreType.DMA(())], 10**7, [pltpu.HBM, pltpu.VMEM],
    )
    x_faces, (own, inverse, volume_weight, marks) = lax.optimization_barrier((x_faces, weights))

    faces = (11 * NODES, SZ)
    *y_faces, side = call(
        faces_y_kernel, (own, *x_faces), [faces, faces, (4 * NODES + 2 * CHOSEN, SY, SIDE)], [], 10**6
    )
    y_faces = exchange(*y_faces, "gy")
    side = other_core(side)
    (y_side,) = call(faces_z_kernel, y_faces, [(4 * NODES, SY, SIDE)], [], 10**6)
    y_side = other_core(y_side)

    faces = (9 * CHOSEN, LANES)
    inner, outer = sizes[1] * sizes[2], sizes[0]
    elements = (2 * SX, SY, 128)
    bounds, *y_bounds, part = call(
        functools.partial(design_kernel, groups=energy_groups()),
        (own, *x_faces, *y_faces, side, y_side, inverse, volume_weight),
        [(3, CHOSEN, SY, LANES), faces, faces, (inner, 8, 128)],
        [(4, NODES, ROWS, LANES), own_frame, own_frame, own_frame]
        + [(2,) + elements, (2,) + elements, (2, 6) + elements], 10**7,
    )

    part = lax.all_to_all(part, ("gy", "gz"), 0, 0, tiled=True)
    y_bounds, part = lax.optimization_barrier((y_bounds, part))
    y_bounds = exchange(*y_bounds, "gy")
    (part,) = call(repeat_kernel, (part,), [(outer, 8, 128)], [], 10**5)
    part = lax.all_to_all(part, "gx", 0, 0, tiled=True)

    chosen = (CHOSEN, ROWS, LANES)
    target = volume_share * (extents[0] * extents[1] * extents[2])
    new_design, new_physical, node_blocks = call(
        functools.partial(final_kernel, factors=[float(f) for f in corner_factors()], target=target),
        (part, bounds, *y_bounds, inverse, marks), [block, block, (6,) + block],
        [chosen, chosen, chosen, (SX + 1, ROWS, LANES)], 10**7,
    )
    return (new_design, new_physical, node_blocks)


def solution(mesh):
    in_specs = (
        P(None, "gx", "gy", "gz"),
        P("gx", "gy", "gz"),
        P("gx", "gy", "gz"),
        P("gx", "gy", "gz"),
        P(),
    )
    out_specs = (P("gx", "gy", "gz"), P("gx", "gy", "gz"), P(None, "gx", "gy", "gz"))
    return jax.shard_map(body, mesh=mesh, in_specs=in_specs, out_specs=out_specs, check_vma=False)
```

```python
import functools
import math

import jax
import jax.numpy as jnp
import numpy as np
from jax import lax
from jax.experimental import pallas as pl
from jax.experimental.pallas import tpu as pltpu
from jax.sharding import PartitionSpec as P

STEPS = 10

filter_radius = 2.5
penalty = 3.0
move_limit = 0.2
stiff_floor = 1e-09
volume_share = 0.5
log_lower = -20.0
log_upper = 20.0
poisson = 0.3

SX, SY, SZ = 8, 8, 256
ROWS, LANES, SIDE = 16, 384, 128
NODES, ELEMENTS, CHOSEN = SX + 10, SX + 9, SX + 5
POINTS = 2**STEPS
F32 = jnp.float32


def corner_offsets():
    return [(q // 4, q // 2 % 2, q % 2) for q in range(8)]


def hex_stiffness():
    lame_first = poisson / ((1.0 + poisson) * (1.0 - 2.0 * poisson))
    shear_modulus = 0.5 / (1.0 + poisson)
    elastic = np.zeros((6, 6))
    elastic[:3, :3] = lame_first
    for d in range(3):
        elastic[d, d] += 2.0 * shear_modulus
        elastic[d + 3, d + 3] = shear_modulus
    corners = corner_offsets()
    points = [0.5 - 0.5 / math.sqrt(3.0), 0.5 + 0.5 / math.sqrt(3.0)]
    matrix = np.zeros((24, 24))
    for p in points:
        for q in points:
            for r in points:
                location = [p, q, r]
                gradients = np.zeros((8, 3))
                for n in range(8):
                    factors = [
                        location[e] if corners[n][e] == 1 else 1.0 - location[e] for e in range(3)
                    ]
                    for d in range(3):
                        sign_value = 1.0 if corners[n][d] == 1 else -1.0
                        gradients[n, d] = sign_value * factors[(d + 1) % 3] * factors[(d + 2) % 3]
                strain = np.zeros((6, 24))
                for n in range(8):
                    column = 3 * n
                    strain[0, column] = gradients[n, 0]
                    strain[1, column + 1] = gradients[n, 1]
                    strain[2, column + 2] = gradients[n, 2]
                    strain[3, column + 1] = gradients[n, 2]
                    strain[3, column + 2] = gradients[n, 1]
                    strain[4, column] = gradients[n, 2]
                    strain[4, column + 2] = gradients[n, 0]
                    strain[5, column] = gradients[n, 1]
                    strain[5, column + 1] = gradients[n, 0]
                matrix += strain.T @ elastic @ strain / 8.0
    return matrix


def energy_groups():
    corners = corner_offsets()
    modes = np.zeros((24, 24))
    for s in range(8):
        bits = (s // 4, s // 2 % 2, s % 2)
        for n in range(8):
            sign_value = 1.0
            for e in range(3):
                if bits[e] == 1 and corners[n][e] == 0:
                    sign_value = -sign_value
            for d in range(3):
                modes[3 * n + d, 3 * s + d] = sign_value
    form = modes.T @ hex_stiffness() @ modes / 64.0
    groups = []

    def add(coefficient, members):
        if abs(coefficient) < 1e-9:
            return
        for group in groups:
            if abs(group[0] - coefficient) < 1e-9:
                group[1].append(members)
                return
        groups.append((coefficient, [members]))

    for parity in range(8):
        left = [3 * (parity ^ (4, 2, 1)[d]) + d for d in range(3)]
        while left:
            first = left[0]
            block = [m for m in left if m == first or abs(form[first, m]) > 1e-9]
            left = [m for m in left if m not in block]
            beside = form[block[0], block[1]] if len(block) > 1 else 0.0
            add(beside, block)
            for m in block:
                add(form[m, m] - beside, [m])
    rebuilt = np.zeros((24, 24))
    for coefficient, sums in groups:
        for members in sums:
            rebuilt[np.ix_(members, members)] += coefficient
    assert np.abs(rebuilt - form).max() < 1e-9
    return groups


def corner_factors():
    matrix = hex_stiffness()
    factors = (matrix[0, 0], matrix[1, 2], matrix[0, 2], matrix[0, 1])
    for n, corner in enumerate(corner_offsets()):
        sign = [1.0 if c == 1 else -1.0 for c in corner]
        block = matrix[3 * n : 3 * n + 3, 3 * n : 3 * n + 3]
        assert np.allclose(np.diag(block), factors[0])
        assert np.allclose(block[1, 2], factors[1] * sign[1] * sign[2])
        assert np.allclose(block[0, 2], factors[2] * sign[0] * sign[2])
        assert np.allclose(block[0, 1], factors[3] * sign[0] * sign[1])
    return factors


def tap(square):
    return max(0.0, filter_radius - math.sqrt(square))


def rolled(value, steps, dim):
    return pltpu.roll(value, (-steps) % value.shape[dim], dim)


def row_pairs(plane):
    return (
        rolled(plane, 1, 0) + rolled(plane, -1, 0),
        rolled(plane, 2, 0) + rolled(plane, -2, 0),
    )


def filtered_plane(plane_of, near_of, far_of, p):
    ring_0 = plane_of(p)
    ring_1 = near_of(p) + plane_of(p - 1) + plane_of(p + 1)
    ring_2 = near_of(p - 1) + near_of(p + 1)
    ring_4 = far_of(p) + plane_of(p - 2) + plane_of(p + 2)
    ring_5 = far_of(p - 1) + far_of(p + 1) + near_of(p - 2) + near_of(p + 2)
    layers = []
    for c in (0, 1, 2):
        total = None
        for square, ring in ((0, ring_0), (1, ring_1), (2, ring_2), (4, ring_4), (5, ring_5)):
            weight = tap(square + c * c)
            if weight > 0.0:
                total = weight * ring if total is None else total + weight * ring
        layers.append(total)
    middle, near, far = layers
    return middle + (rolled(near, 1, 1) + rolled(near, -1, 1)) + (rolled(far, 2, 1) + rolled(far, -2, 1))


def weights_kernel(support_ref, inverse_ref, volume_ref, mark_ref, near_ref, far_ref, *, extents):
    total_x, total_y, total_z = extents
    first_x = lax.axis_index("gx") * SX
    first_y = lax.axis_index("gy") * SY
    first_z = lax.axis_index("gz") * SZ
    row = lax.broadcasted_iota(jnp.int32, (ROWS, LANES), 0)
    lane = lax.broadcasted_iota(jnp.int32, (ROWS, LANES), 1)
    y = first_y + jnp.where(row < 12, row, row - ROWS)
    z = first_z + jnp.where(lane < SZ + SIDE // 2, lane, lane - LANES)
    inside = jnp.where((y >= 0) & (y < total_y) & (z >= 0) & (z < total_z), 1.0, 0.0).astype(F32)
    near, far = row_pairs(inside)

    def present(p):
        x = first_x + p
        return jnp.where((x >= 0) & (x < total_x), 1.0, 0.0).astype(F32)

    for p in range(ELEMENTS):
        x = p - 5
        weight_sum = filtered_plane(
            lambda q: inside * present(q), lambda q: near * present(q), lambda q: far * present(q), x
        )
        here = inside * present(x)
        inverse = jnp.where(here > 0.0, 1.0 / jnp.where(here > 0.0, weight_sum, 1.0), 0.0)
        inverse_ref[p] = inverse
        inverse_near, inverse_far = row_pairs(inverse)
        near_ref[p] = inverse_near[0:SY]
        far_ref[p] = inverse_far[0:SY]
    for p in range(CHOSEN):
        volume_ref[p] = filtered_plane(
            lambda q: inverse_ref[q, 0:SY], lambda q: near_ref[q], lambda q: far_ref[q], p + 2
        )
    node = support_ref[...]
    node_x = node // (total_y * total_z) - first_x
    node_y = node // total_z % total_y - first_y
    node_z = node % total_z - first_z
    owned = (node_x >= 0) & (node_x < SX) & (node_y >= 0) & (node_y < SY)
    line = jnp.where(owned, node_x * SY + node_y, -1)
    count = node.shape[1]
    lines = jnp.where(lax.broadcasted_iota(jnp.int32, (SX * SY, count), 0) == line, 1.0, 0.0)
    lanes = jnp.where(lax.broadcasted_iota(jnp.int32, (SZ, count), 0) == node_z, 1.0, 0.0)
    hits = lax.dot_general(
        lines.astype(jnp.bfloat16),
        lanes.astype(jnp.bfloat16),
        (((1,), (1,)), ((), ())),
        preferred_element_type=F32,
    )
    for p in range(SX):
        mark_ref[p] = hits[p * SY : (p + 1) * SY]


def is_even(axis):
    return lax.axis_index(axis) % 2 == 0


def place_pair(even, first_ref, second_ref, top, bottom, place):
    first_ref[place] = jnp.where(even, top, bottom)
    second_ref[place] = jnp.where(even, bottom, top)


def low_high(axis, first_ref, second_ref, place):
    index = lax.axis_index(axis)
    first, second = first_ref[place], second_ref[place]
    low = jnp.where(index == 0, 0.0, jnp.where(index % 2 == 0, second, first))
    high = jnp.where(index == lax.axis_size(axis) - 1, 0.0, jnp.where(index % 2 == 0, first, second))
    return low, high


def row_place(index):
    if index < 3 * NODES:
        return slice(3 * index, 3 * index + 3)
    return slice(2 * index + 3 * NODES, 2 * index + 3 * NODES + 2)


def row_tile(first_ref, second_ref, place):
    low, high = low_high("gy", first_ref, second_ref, place)
    filler = jnp.zeros((SY - 2 * low.shape[0], low.shape[1]), F32)
    return jnp.concatenate([high, filler, low], axis=0)


def plane_reader(shift_ref, physical_ref, x_first, x_second):
    def read(index):
        f, x = index // NODES, index % NODES - 5
        if 0 <= x < SX:
            return shift_ref[f, x] if f < 3 else physical_ref[x]
        low, high = low_high("gx", x_first, x_second, (f, x + 5 if x < 0 else x - SX))
        return low if x < 0 else high

    return read


def design_reader(design_ref, passive_ref, x_first, x_second):
    def read(index):
        f, x = index // CHOSEN, index % CHOSEN - 3
        if 0 <= x < SX:
            return design_ref[x] if f == 0 else passive_ref[x].astype(F32)
        low, high = low_high("gx", x_first, x_second, (f, x + 3 if x < 0 else x - SX))
        return low if x < 0 else high

    return read


def near_half(plane):
    return jnp.where(lax.axis_index("gz") == 0, plane[:, SZ - SIDE :], plane[:, 0:SIDE])


def faces_y_kernel(shift_ref, physical_ref, x_first, x_second, first_ref, second_ref, side_ref):
    even = is_even("gy")
    read = plane_reader(shift_ref, physical_ref, x_first, x_second)
    for index in range(4 * NODES):
        plane = read(index)
        rows = row_place(index)
        depth = rows.stop - rows.start
        place_pair(even, first_ref, second_ref, plane[SY - depth :], plane[0:depth], rows)
        side_ref[index] = near_half(plane)


def faces_z_kernel(y_first, y_second, design_ref, passive_ref, d_first, d_second, side_ref):
    for index in range(4 * NODES):
        side_ref[index] = near_half(row_tile(y_first, y_second, row_place(index)))
    read = design_reader(design_ref, passive_ref, d_first, d_second)
    for index in range(2 * CHOSEN):
        side_ref[4 * NODES + index] = near_half(read(index))


def design_kernel(
    shift_ref, physical_ref, design_ref, passive_ref, x_first, x_second, y_first, y_second, d_first, d_second,
    side, y_side, inverse_ref, volume_ref, out_ref, first_ref, second_ref, part_ref, ext_ref, sens_ref, near_ref, far_ref, high_ref, low_ref, value_ref, *, groups
):
    lane = lax.broadcasted_iota(jnp.int32, (SY, SIDE), 1)
    start = lax.axis_index("gz") * (SIDE // 2)
    keep = (lane >= start) & (lane < start + SIDE // 2)
    even = is_even("gy")
    read = plane_reader(shift_ref, physical_ref, x_first, x_second)
    for f in range(4):
        for p in range(NODES):
            index = NODES * f + p
            ext_ref[f, p, 0:SY, 0:SZ] = read(index)
            ext_ref[f, p, 0:SY, SZ:LANES] = jnp.where(keep, side[index], 0.0)
            ext_ref[f, p, SY:ROWS, 0:SZ] = row_tile(y_first, y_second, row_place(index))
            ext_ref[f, p, SY:ROWS, SZ:LANES] = jnp.where(keep, y_side[index], 0.0)
    scale = penalty * (1.0 - stiff_floor)

    @pl.loop(0, ELEMENTS)
    def _(p):
        modes = {}
        for d in range(3):
            here, above = ext_ref[d, p], ext_ref[d, p + 1]
            for a, along_x in enumerate((here + above, above - here)):
                beyond = rolled(along_x, 1, 0)
                for b, along_y in enumerate((along_x + beyond, beyond - along_x)):
                    next_lane = rolled(along_y, 1, 1)
                    for c, mode in enumerate((along_y + next_lane, next_lane - along_y)):
                        modes[3 * (4 * a + 2 * b + c) + d] = mode
        energy = None
        for coefficient, sums in groups:
            squares = None
            for members in sums:
                value = functools.reduce(lambda left, right: left + right, [modes[m] for m in members])
                squares = value * value if squares is None else squares + value * value
            squares = float(coefficient) * squares
            energy = squares if energy is None else energy + squares
        density = ext_ref[3, p]
        sens = scale * density * density * energy * inverse_ref[p]
        sens_ref[p] = sens[0:SY]
        near, far = row_pairs(sens)
        near_ref[p] = near[0:SY]
        far_ref[p] = far[0:SY]

    read_design = design_reader(design_ref, passive_ref, d_first, d_second)
    for p in range(CHOSEN):
        filtered = filtered_plane(lambda q: sens_ref[q], lambda q: near_ref[q], lambda q: far_ref[q], p + 2)
        index = 4 * NODES + p
        design = jnp.concatenate([read_design(p), y_side[index]], axis=1)
        solid = jnp.concatenate([read_design(p + CHOSEN), y_side[index + CHOSEN]], axis=1) > 0.5
        inside = inverse_ref[p + 2, 0:SY] > 0.0
        scaled = design * jnp.sqrt(filtered / jnp.where(inside, volume_ref[p], 1.0))
        floor_bound = jnp.where(solid, 1.0, jnp.maximum(0.0, design - move_limit))
        ceiling = jnp.where(solid, 1.0, jnp.minimum(1.0, design + move_limit))
        for f, value in enumerate((scaled, floor_bound, ceiling)):
            value = jnp.where(inside, value, 0.0)
            out_ref[f, p] = value
            row = 3 * (CHOSEN * f + p)
            place_pair(even, first_ref, second_ref, value[SY - 3 :], value[0:3], slice(row, row + 3))
    add_volumes(out_ref, volume_ref, part_ref, high_ref, low_ref, value_ref)


def three_parts(value):
    first = value.astype(jnp.bfloat16).astype(F32)
    second = (value - first).astype(jnp.bfloat16).astype(F32)
    return first, second, value - first - second


def add_volumes(bounds_ref, volume_ref, out_ref, high_ref, low_ref, value_ref):
    step = (log_upper - log_lower) / POINTS
    ceilings = jnp.zeros((SY, 128), F32)
    for v in range(2 * SX):
        place = (3 + v // 2, slice(None), slice(128 * (v % 2), 128 * (v % 2 + 1)))
        weight = volume_ref[place]
        scaled, floor_bound, ceiling = [bounds_ref[(f,) + place] for f in range(3)]
        ceilings = ceilings + weight * ceiling
        log_scaled = jnp.log(jnp.maximum(scaled, 1e-30))
        for t, bound in enumerate((ceiling, floor_bound)):
            reached = (2.0 * (log_scaled - jnp.log(jnp.maximum(bound, 1e-30))) - log_lower) / step
            index = jnp.minimum(jnp.maximum(jnp.ceil(reached), 1.0), POINTS + 1.0) - 1.0
            index = jnp.where(bound > 0.0, index, float(POINTS))
            high = jnp.floor(index * (1.0 / 128.0))
            high_ref[t, v] = high
            low_ref[t, v] = index - 128.0 * high
            sign = -1.0 if t == 0 else 1.0
            parts = three_parts(sign * weight * bound) + three_parts(-sign * weight * scaled)
            for n, part in enumerate(parts):
                value_ref[t, n, v] = part

    rows = lax.broadcasted_iota(jnp.int32, (8, 128), 0).astype(F32)
    columns = lax.broadcasted_iota(jnp.int32, (128, 128), 0).astype(F32).astype(jnp.bfloat16)

    def add_group(v, total):
        lefts, rights = [], []
        for t in range(2):
            for r in range(SY):
                hit = rows == high_ref[t, v, r : r + 1, :]
                left = [jnp.where(hit, value_ref[t, n, v, r : r + 1, :], 0.0) for n in range(6)]
                lefts.append(jnp.concatenate(left, axis=0).astype(jnp.bfloat16))
                low = jnp.broadcast_to(low_ref[t, v, r : r + 1, :], (16, 128)).astype(jnp.bfloat16)
                low = jnp.concatenate([low] * 8, axis=0)
                rights.append(jnp.where(columns == low, jnp.bfloat16(1.0), jnp.bfloat16(0.0)))
        return total + lax.dot_general(
            jnp.concatenate(rights, axis=1),
            jnp.concatenate(lefts, axis=1),
            (((1,), (1,)), ((), ())),
            preferred_element_type=F32,
        )

    total = lax.fori_loop(0, 2 * SX, add_group, jnp.zeros((128, 48), F32), unroll=4).T
    constant = total[0:8] + total[8:16] + total[16:24]
    slope = total[24:32] + total[32:40] + total[40:48]
    upto = jnp.where(
        lax.broadcasted_iota(jnp.int32, (128, 128), 0) <= lax.broadcasted_iota(jnp.int32, (128, 128), 1), 1.0, 0.0
    )
    running = lax.dot_general(
        jnp.concatenate([constant, slope], axis=0),
        upto,
        (((1,), (0,)), ((), ())),
        precision=lax.Precision.HIGHEST,
        preferred_element_type=F32,
    )
    row = lax.broadcasted_iota(jnp.int32, (8, 128), 0)
    lane = lax.broadcasted_iota(jnp.int32, (8, 128), 1)
    cumulated = []
    for part in (running[0:8], running[8:16]):
        ends = jnp.broadcast_to(part[:, 127:128], (8, 128))
        before = ends
        for shift in (1, 2, 4):
            before = before + jnp.where(row >= shift, rolled(before, -shift, 0), 0.0)
        cumulated.append(part + (before - ends))
    index = (row * 128 + lane + 1).astype(F32)
    factor = jnp.exp(-0.5 * (log_lower + step * index))
    result = jnp.sum(ceilings) + cumulated[0] + factor * cumulated[1]
    for i in range(out_ref.shape[0]):
        out_ref[i] = result


def repeat_kernel(part_ref, out_ref):
    total = part_ref[0]
    for i in range(1, part_ref.shape[0]):
        total = total + part_ref[i]
    for i in range(out_ref.shape[0]):
        out_ref[i] = total


def final_kernel(
    part_ref, own_ref, y_first, y_second, inverse_ref, mark_ref, new_design_ref, new_physical_ref,
    blocks_ref, chosen_ref, near_ref, far_ref, stiff_ref, *, factors, target
):
    total = part_ref[0]
    for i in range(1, part_ref.shape[0]):
        total = total + part_ref[i]
    low_end = jnp.minimum(jnp.sum(jnp.where(total > target, 1.0, 0.0)), POINTS - 1.0)
    multiplier = log_lower + (log_upper - log_lower) / POINTS * (low_end + 0.5)
    factor = jnp.exp(jnp.broadcast_to(-0.5 * multiplier, (SY, LANES)))
    for p in range(CHOSEN):
        tiles = []
        own = [own_ref[f, p] for f in range(3)]
        beside = []
        for f in range(3):
            row = 3 * (CHOSEN * f + p)
            beside.append(row_tile(y_first, y_second, slice(row, row + 3)))
        for scaled, floor_bound, ceiling in (own, beside):
            tiles.append(jnp.minimum(jnp.maximum(scaled * factor, floor_bound), ceiling))
        chosen = jnp.concatenate(tiles, axis=0)
        chosen_ref[p] = chosen
        near, far = row_pairs(chosen)
        near_ref[p] = near
        far_ref[p] = far
        if 3 <= p < SX + 3:
            new_design_ref[p - 3] = tiles[0][:, 0:SZ]
    for p in range(SX + 1):
        inverse = inverse_ref[p + 4]
        density = (
            filtered_plane(lambda q: chosen_ref[q], lambda q: near_ref[q], lambda q: far_ref[q], p + 2) * inverse
        )
        if p >= 1:
            new_physical_ref[p - 1] = density[0:SY, 0:SZ]
        cube = stiff_floor + density * density * density * (1.0 - stiff_floor)
        stiff_ref[p] = jnp.where(inverse > 0.0, cube, 0.0)
    for p in range(SX):
        below, here = stiff_ref[p], stiff_ref[p + 1]
        x_sum, x_diff = here + below, below - here
        x_sum_back, x_diff_back = rolled(x_sum, -1, 0), rolled(x_diff, -1, 0)
        sum_sum = (x_sum + x_sum_back)[0:SY]
        sum_diff = (x_sum_back - x_sum)[0:SY]
        diff_sum = (x_diff + x_diff_back)[0:SY]
        diff_diff = (x_diff_back - x_diff)[0:SY]
        marked = mark_ref[p] > 0.5
        even = factors[0] * (sum_sum + rolled(sum_sum, -1, 1))[:, 0:SZ]
        even = jnp.where(marked, 1.0, even)
        blocks_ref[0, p] = even
        blocks_ref[1, p] = even
        blocks_ref[2, p] = even
        yz = factors[1] * (rolled(sum_diff, -1, 1) - sum_diff)[:, 0:SZ]
        xz = factors[2] * (rolled(diff_sum, -1, 1) - diff_sum)[:, 0:SZ]
        xy = factors[3] * (diff_diff + rolled(diff_diff, -1, 1))[:, 0:SZ]
        blocks_ref[3, p] = jnp.where(marked, 0.0, yz)
        blocks_ref[4, p] = jnp.where(marked, 0.0, xz)
        blocks_ref[5, p] = jnp.where(marked, 0.0, xy)


def call(kernel, inputs, shapes, scratch, flops, spaces=None, grant=32):
    outs = [jax.ShapeDtypeStruct(shape, F32) for shape in shapes]
    return pl.pallas_call(
        kernel,
        out_shape=outs,
        in_specs=[pl.BlockSpec(memory_space=space) for space in spaces or [pltpu.VMEM] * len(inputs)],
        out_specs=[pl.BlockSpec(memory_space=pltpu.VMEM)] * len(outs),
        scratch_shapes=[pltpu.VMEM(shape, F32) if isinstance(shape, tuple) else shape for shape in scratch],
        compiler_params=pltpu.CompilerParams(vmem_limit_bytes=grant * 2**20),
        cost_estimate=pl.CostEstimate(flops=flops, bytes_accessed=10**6, transcendentals=0),
    )(*inputs)


def exchange(first, second, axis):
    count = lax.axis_size(axis)
    results = []
    for start, faces in enumerate((first, second)):
        pairs = [(i, (i + 1) % count) for i in range(start, count, 2)]
        results.append(lax.ppermute(faces, axis, pairs + [(j, i) for i, j in pairs]))
    return results


def other_core(values):
    return lax.ppermute(values, "gz", [(0, 1), (1, 0)])


def body(displacement, physical, design, passive, supports):
    assert design.shape == (SX, SY, SZ) and lax.axis_size("gz") == 2
    sizes = [lax.axis_size(axis) for axis in ("gx", "gy", "gz")]
    extents = (SX * sizes[0], SY * sizes[1], SZ * sizes[2])
    block = (SX, SY, SZ)
    even = lax.axis_index("gx") % 2 == 0

    def swaps(fields, depth):
        top, bottom = fields[:, SX - depth :], fields[:, 0:depth]
        return jnp.where(even, top, bottom), jnp.where(even, bottom, top)

    x_faces = exchange(*swaps(jnp.concatenate([displacement, physical[None]], axis=0), 5), "gx")
    frame = (ELEMENTS, ROWS, LANES)
    own_frame = (ELEMENTS, SY, LANES)
    weights = call(
        functools.partial(weights_kernel, extents=extents), (supports.reshape(1, -1),),
        [frame, (CHOSEN, SY, LANES), block], [own_frame, own_frame], 10**7,
    )
    design_faces = swaps(jnp.stack([design, passive.astype(F32)]), 3)
    x_faces, design_faces, (inverse, volume_weight, marks) = lax.optimization_barrier(
        (x_faces, design_faces, weights)
    )

    faces = (11 * NODES, SZ)
    *y_faces, side = call(
        faces_y_kernel, (displacement, physical, *x_faces), [faces, faces, (4 * NODES, SY, SIDE)], [], 10**6
    )
    y_faces, side, design_faces = lax.optimization_barrier((y_faces, side, design_faces))
    y_faces = exchange(*y_faces, "gy")
    design_faces = exchange(*design_faces, "gx")
    y_faces, side = lax.optimization_barrier((y_faces, other_core(side)))
    (y_side,) = call(
        faces_z_kernel, (*y_faces, design, passive, *design_faces), [(4 * NODES + 2 * CHOSEN, SY, SIDE)], [], 10**6
    )
    y_side = other_core(y_side)

    faces = (9 * CHOSEN, LANES)
    inner, outer = sizes[1] * sizes[2], sizes[0]
    elements = (2 * SX, SY, 128)
    bounds, *y_bounds, part = call(
        functools.partial(design_kernel, groups=energy_groups()),
        (displacement, physical, design, passive, *x_faces, *y_faces, *design_faces, side, y_side, inverse,
         volume_weight),
        [(3, CHOSEN, SY, LANES), faces, faces, (inner, 8, 128)],
        [(4, NODES, ROWS, LANES), own_frame, own_frame, own_frame]
        + [(2,) + elements, (2,) + elements, (2, 6) + elements], 10**7,
    )

    part = lax.all_to_all(part, ("gy", "gz"), 0, 0, tiled=True)
    y_bounds, part = lax.optimization_barrier((y_bounds, part))
    y_bounds = exchange(*y_bounds, "gy")
    (part,) = call(repeat_kernel, (part,), [(outer, 8, 128)], [], 10**5)
    part = lax.all_to_all(part, "gx", 0, 0, tiled=True)

    chosen = (CHOSEN, ROWS, LANES)
    target = volume_share * (extents[0] * extents[1] * extents[2])
    new_design, new_physical, node_blocks = call(
        functools.partial(final_kernel, factors=[float(f) for f in corner_factors()], target=target),
        (part, bounds, *y_bounds, inverse, marks), [block, block, (6,) + block],
        [chosen, chosen, chosen, (SX + 1, ROWS, LANES)], 10**7,
    )
    return (new_design, new_physical, node_blocks)


def solution(mesh):
    in_specs = (
        P(None, "gx", "gy", "gz"),
        P("gx", "gy", "gz"),
        P("gx", "gy", "gz"),
        P("gx", "gy", "gz"),
        P(),
    )
    out_specs = (P("gx", "gy", "gz"), P("gx", "gy", "gz"), P(None, "gx", "gy", "gz"))
    return jax.shard_map(body, mesh=mesh, in_specs=in_specs, out_specs=out_specs, check_vma=False)
```

```python
import functools
import math

import jax
import jax.numpy as jnp
import numpy as np
from jax import lax
from jax.experimental import pallas as pl
from jax.experimental.pallas import tpu as pltpu
from jax.sharding import PartitionSpec as P

STEPS = 10

filter_radius = 2.5
penalty = 3.0
move_limit = 0.2
stiff_floor = 1e-09
volume_share = 0.5
log_lower = -20.0
log_upper = 20.0
poisson = 0.3

SX, SY, SZ = 8, 8, 256
ROWS, LANES, SIDE = 16, 384, 128
NODES, ELEMENTS, CHOSEN = SX + 10, SX + 9, SX + 5
POINTS = 2**STEPS
F32 = jnp.float32


def corner_offsets():
    return [(q // 4, q // 2 % 2, q % 2) for q in range(8)]


def hex_stiffness():
    lame_first = poisson / ((1.0 + poisson) * (1.0 - 2.0 * poisson))
    shear_modulus = 0.5 / (1.0 + poisson)
    elastic = np.zeros((6, 6))
    elastic[:3, :3] = lame_first
    for d in range(3):
        elastic[d, d] += 2.0 * shear_modulus
        elastic[d + 3, d + 3] = shear_modulus
    corners = corner_offsets()
    points = [0.5 - 0.5 / math.sqrt(3.0), 0.5 + 0.5 / math.sqrt(3.0)]
    matrix = np.zeros((24, 24))
    for p in points:
        for q in points:
            for r in points:
                location = [p, q, r]
                gradients = np.zeros((8, 3))
                for n in range(8):
                    factors = [
                        location[e] if corners[n][e] == 1 else 1.0 - location[e] for e in range(3)
                    ]
                    for d in range(3):
                        sign_value = 1.0 if corners[n][d] == 1 else -1.0
                        gradients[n, d] = sign_value * factors[(d + 1) % 3] * factors[(d + 2) % 3]
                strain = np.zeros((6, 24))
                for n in range(8):
                    column = 3 * n
                    strain[0, column] = gradients[n, 0]
                    strain[1, column + 1] = gradients[n, 1]
                    strain[2, column + 2] = gradients[n, 2]
                    strain[3, column + 1] = gradients[n, 2]
                    strain[3, column + 2] = gradients[n, 1]
                    strain[4, column] = gradients[n, 2]
                    strain[4, column + 2] = gradients[n, 0]
                    strain[5, column] = gradients[n, 1]
                    strain[5, column + 1] = gradients[n, 0]
                matrix += strain.T @ elastic @ strain / 8.0
    return matrix


def energy_groups():
    corners = corner_offsets()
    modes = np.zeros((24, 24))
    for s in range(8):
        bits = (s // 4, s // 2 % 2, s % 2)
        for n in range(8):
            sign_value = 1.0
            for e in range(3):
                if bits[e] == 1 and corners[n][e] == 0:
                    sign_value = -sign_value
            for d in range(3):
                modes[3 * n + d, 3 * s + d] = sign_value
    form = modes.T @ hex_stiffness() @ modes / 64.0
    groups = []

    def add(coefficient, members):
        if abs(coefficient) < 1e-9:
            return
        for group in groups:
            if abs(group[0] - coefficient) < 1e-9:
                group[1].append(members)
                return
        groups.append((coefficient, [members]))

    for parity in range(8):
        left = [3 * (parity ^ (4, 2, 1)[d]) + d for d in range(3)]
        while left:
            first = left[0]
            block = [m for m in left if m == first or abs(form[first, m]) > 1e-9]
            left = [m for m in left if m not in block]
            beside = form[block[0], block[1]] if len(block) > 1 else 0.0
            add(beside, block)
            for m in block:
                add(form[m, m] - beside, [m])
    rebuilt = np.zeros((24, 24))
    for coefficient, sums in groups:
        for members in sums:
            rebuilt[np.ix_(members, members)] += coefficient
    assert np.abs(rebuilt - form).max() < 1e-9
    return groups


def corner_factors():
    matrix = hex_stiffness()
    factors = (matrix[0, 0], matrix[1, 2], matrix[0, 2], matrix[0, 1])
    for n, corner in enumerate(corner_offsets()):
        sign = [1.0 if c == 1 else -1.0 for c in corner]
        block = matrix[3 * n : 3 * n + 3, 3 * n : 3 * n + 3]
        assert np.allclose(np.diag(block), factors[0])
        assert np.allclose(block[1, 2], factors[1] * sign[1] * sign[2])
        assert np.allclose(block[0, 2], factors[2] * sign[0] * sign[2])
        assert np.allclose(block[0, 1], factors[3] * sign[0] * sign[1])
    return factors


def tap(square):
    return max(0.0, filter_radius - math.sqrt(square))


def rolled(value, steps, dim):
    return pltpu.roll(value, (-steps) % value.shape[dim], dim)


def row_pairs(plane):
    return (
        rolled(plane, 1, 0) + rolled(plane, -1, 0),
        rolled(plane, 2, 0) + rolled(plane, -2, 0),
    )


def filtered_plane(plane_of, near_of, far_of, p):
    ring_0 = plane_of(p)
    ring_1 = near_of(p) + plane_of(p - 1) + plane_of(p + 1)
    ring_2 = near_of(p - 1) + near_of(p + 1)
    ring_4 = far_of(p) + plane_of(p - 2) + plane_of(p + 2)
    ring_5 = far_of(p - 1) + far_of(p + 1) + near_of(p - 2) + near_of(p + 2)
    layers = []
    for c in (0, 1, 2):
        total = None
        for square, ring in ((0, ring_0), (1, ring_1), (2, ring_2), (4, ring_4), (5, ring_5)):
            weight = tap(square + c * c)
            if weight > 0.0:
                total = weight * ring if total is None else total + weight * ring
        layers.append(total)
    middle, near, far = layers
    return middle + (rolled(near, 1, 1) + rolled(near, -1, 1)) + (rolled(far, 2, 1) + rolled(far, -2, 1))


def weights_kernel(support_ref, inverse_ref, edge_ref, volume_ref, mark_ref, near_ref, far_ref, *, extents):
    total_x, total_y, total_z = extents
    first_x = lax.axis_index("gx") * SX
    first_y = lax.axis_index("gy") * SY
    first_z = lax.axis_index("gz") * SZ
    row = lax.broadcasted_iota(jnp.int32, (ROWS, LANES), 0)
    lane = lax.broadcasted_iota(jnp.int32, (ROWS, LANES), 1)
    y = first_y + jnp.where(row < 12, row, row - ROWS)
    z = first_z + jnp.where(lane < SZ + SIDE // 2, lane, lane - LANES)
    inside = jnp.where((y >= 0) & (y < total_y) & (z >= 0) & (z < total_z), 1.0, 0.0).astype(F32)
    near, far = row_pairs(inside)

    def present(p):
        x = first_x + p
        return jnp.where((x >= 0) & (x < total_x), 1.0, 0.0).astype(F32)

    for p in range(ELEMENTS):
        x = p - 5
        weight_sum = filtered_plane(
            lambda q: inside * present(q), lambda q: near * present(q), lambda q: far * present(q), x
        )
        here = inside * present(x)
        inverse = jnp.where(here > 0.0, 1.0 / jnp.where(here > 0.0, weight_sum, 1.0), 0.0)
        inverse_ref[p] = inverse
        edge_ref[p] = jnp.concatenate([inverse[7:11], inverse[14:16], inverse[0:2]], axis=0)
        inverse_near, inverse_far = row_pairs(inverse)
        near_ref[p] = inverse_near[0:SY]
        far_ref[p] = inverse_far[0:SY]
    for p in range(CHOSEN):
        volume_ref[p] = filtered_plane(
            lambda q: inverse_ref[q, 0:SY], lambda q: near_ref[q], lambda q: far_ref[q], p + 2
        )
    node = support_ref[...]
    node_x = node // (total_y * total_z) - first_x
    node_y = node // total_z % total_y - first_y
    node_z = node % total_z - first_z
    owned = (node_x >= 0) & (node_x < SX) & (node_y >= 0) & (node_y < SY)
    line = jnp.where(owned, node_x * SY + node_y, -1)
    count = node.shape[1]
    lines = jnp.where(lax.broadcasted_iota(jnp.int32, (SX * SY, count), 0) == line, 1.0, 0.0)
    lanes = jnp.where(lax.broadcasted_iota(jnp.int32, (SZ, count), 0) == node_z, 1.0, 0.0)
    hits = lax.dot_general(
        lines.astype(jnp.bfloat16),
        lanes.astype(jnp.bfloat16),
        (((1,), (1,)), ((), ())),
        preferred_element_type=F32,
    )
    for p in range(SX):
        mark_ref[p] = hits[p * SY : (p + 1) * SY]


def is_even(axis):
    return lax.axis_index(axis) % 2 == 0


def place_pair(even, first_ref, second_ref, top, bottom, place):
    first_ref[place] = jnp.where(even, top, bottom)
    second_ref[place] = jnp.where(even, bottom, top)


def low_high(axis, first_ref, second_ref, place):
    index = lax.axis_index(axis)
    first, second = first_ref[place], second_ref[place]
    low = jnp.where(index == 0, 0.0, jnp.where(index % 2 == 0, second, first))
    high = jnp.where(index == lax.axis_size(axis) - 1, 0.0, jnp.where(index % 2 == 0, first, second))
    return low, high


def row_place(index):
    if index < 3 * NODES:
        return slice(3 * index, 3 * index + 3)
    return slice(2 * index + 3 * NODES, 2 * index + 3 * NODES + 2)


def row_tile(first_ref, second_ref, place):
    low, high = low_high("gy", first_ref, second_ref, place)
    filler = jnp.zeros((SY - 2 * low.shape[0], low.shape[1]), F32)
    return jnp.concatenate([high, filler, low], axis=0)


def plane_reader(shift_ref, physical_ref, x_first, x_second):
    def read(index):
        f, x = index // NODES, index % NODES - 5
        if 0 <= x < SX:
            return shift_ref[f, x] if f < 3 else physical_ref[x]
        low, high = low_high("gx", x_first, x_second, (f, x + 5 if x < 0 else x - SX))
        return low if x < 0 else high

    return read


def design_reader(design_ref, passive_ref, x_first, x_second):
    def read(index):
        f, x = index // CHOSEN, index % CHOSEN - 3
        if 0 <= x < SX:
            return design_ref[x] if f == 0 else passive_ref[x].astype(F32)
        low, high = low_high("gx", x_first, x_second, (f, x + 3 if x < 0 else x - SX))
        return low if x < 0 else high

    return read


def near_half(plane):
    return jnp.where(lax.axis_index("gz") == 0, plane[:, SZ - SIDE :], plane[:, 0:SIDE])


def edge_tile(plane, low, high):
    missing = 3 - high.shape[0]
    filler = [jnp.zeros((missing, SZ), F32)] if missing else []
    return jnp.concatenate([plane[7:8], high, *filler, low[low.shape[0] - 2 :], plane[0:2]], axis=0)


def faces_y_kernel(shift_ref, physical_ref, x_first, x_second, first_ref, second_ref):
    even = is_even("gy")
    read = plane_reader(shift_ref, physical_ref, x_first, x_second)
    for index in range(4 * NODES):
        plane = read(index)
        rows = row_place(index)
        depth = rows.stop - rows.start
        place_pair(even, first_ref, second_ref, plane[SY - depth :], plane[0:depth], rows)


def faces_side_kernel(shift_ref, physical_ref, x_first, x_second, side_ref):
    read = plane_reader(shift_ref, physical_ref, x_first, x_second)
    for index in range(4 * NODES):
        side_ref[index] = near_half(read(index))


def faces_edge_kernel(
    shift_ref, physical_ref, x_first, x_second, y_first, y_second, design_ref, passive_ref, d_first, d_second,
    edge_ref, side_ref
):
    read = plane_reader(shift_ref, physical_ref, x_first, x_second)
    for index in range(4 * NODES):
        low, high = low_high("gy", y_first, y_second, row_place(index))
        tile = edge_tile(read(index), low, high)
        edge_ref[index] = tile
        side_ref[index] = near_half(tile)
    read = design_reader(design_ref, passive_ref, d_first, d_second)
    for index in range(2 * CHOSEN):
        side_ref[4 * NODES + index] = near_half(read(index))


def scaled_energy(ext_ref, read, side, inverse_of, out_ref, groups):
    lane = lax.broadcasted_iota(jnp.int32, (SY, SIDE), 1)
    start = lax.axis_index("gz") * (SIDE // 2)
    keep = (lane >= start) & (lane < start + SIDE // 2)
    for f in range(4):
        for p in range(NODES):
            index = NODES * f + p
            ext_ref[f, p, :, 0:SZ] = read(index)
            ext_ref[f, p, :, SZ:LANES] = jnp.where(keep, side[index], 0.0)
    scale = penalty * (1.0 - stiff_floor)

    @pl.loop(0, ELEMENTS)
    def _(p):
        modes = {}
        for d in range(3):
            here, above = ext_ref[d, p], ext_ref[d, p + 1]
            for a, along_x in enumerate((here + above, above - here)):
                beyond = rolled(along_x, 1, 0)
                for b, along_y in enumerate((along_x + beyond, beyond - along_x)):
                    next_lane = rolled(along_y, 1, 1)
                    for c, mode in enumerate((along_y + next_lane, next_lane - along_y)):
                        modes[3 * (4 * a + 2 * b + c) + d] = mode
        energy = None
        for coefficient, sums in groups:
            squares = None
            for members in sums:
                value = functools.reduce(lambda left, right: left + right, [modes[m] for m in members])
                squares = value * value if squares is None else squares + value * value
            squares = float(coefficient) * squares
            energy = squares if energy is None else energy + squares
        density = ext_ref[3, p]
        out_ref[p] = scale * density * density * energy * inverse_of(p)


def inner_kernel(shift_ref, physical_ref, x_first, x_second, side, inverse_ref, out_ref, ext_ref, *, groups):
    read = plane_reader(shift_ref, physical_ref, x_first, x_second)
    scaled_energy(ext_ref, read, side, lambda p: inverse_ref[p, 0:SY], out_ref, groups)


def design_kernel(
    design_ref, passive_ref, d_first, d_second, inner_ref, edge_tiles, edge_side, inverse_ref, edge_ref, volume_ref,
    out_ref, first_ref, second_ref, part_ref, ext_ref, outer_ref, sens_ref, near_ref, far_ref, high_ref, low_ref,
    value_ref, *, groups
):
    even = is_even("gy")
    scaled_energy(
        ext_ref, lambda index: edge_tiles[index], edge_side, lambda p: edge_ref[p], outer_ref, groups
    )
    row = lax.broadcasted_iota(jnp.int32, (SY, LANES), 0)
    for p in range(ELEMENTS):
        outer = outer_ref[p]
        own = jnp.where(row == 7, rolled(outer, -7, 0), inner_ref[p])
        beyond = jnp.where(row < 4, rolled(outer, 1, 0), rolled(outer, -2, 0))
        sens_ref[p] = own
        near, far = row_pairs(jnp.concatenate([own, beyond], axis=0))
        near_ref[p] = near[0:SY]
        far_ref[p] = far[0:SY]

    read_design = design_reader(design_ref, passive_ref, d_first, d_second)
    for p in range(CHOSEN):
        filtered = filtered_plane(lambda q: sens_ref[q], lambda q: near_ref[q], lambda q: far_ref[q], p + 2)
        index = 4 * NODES + p
        design = jnp.concatenate([read_design(p), edge_side[index]], axis=1)
        solid = jnp.concatenate([read_design(p + CHOSEN), edge_side[index + CHOSEN]], axis=1) > 0.5
        inside = inverse_ref[p + 2, 0:SY] > 0.0
        scaled = design * jnp.sqrt(filtered / jnp.where(inside, volume_ref[p], 1.0))
        floor_bound = jnp.where(solid, 1.0, jnp.maximum(0.0, design - move_limit))
        ceiling = jnp.where(solid, 1.0, jnp.minimum(1.0, design + move_limit))
        for f, value in enumerate((scaled, floor_bound, ceiling)):
            value = jnp.where(inside, value, 0.0)
            out_ref[f, p] = value
            row = 3 * (CHOSEN * f + p)
            place_pair(even, first_ref, second_ref, value[SY - 3 :], value[0:3], slice(row, row + 3))
    add_volumes(out_ref, volume_ref, part_ref, high_ref, low_ref, value_ref)


def three_parts(value):
    first = value.astype(jnp.bfloat16).astype(F32)
    second = (value - first).astype(jnp.bfloat16).astype(F32)
    return first, second, value - first - second


def add_volumes(bounds_ref, volume_ref, out_ref, high_ref, low_ref, value_ref):
    step = (log_upper - log_lower) / POINTS
    ceilings = jnp.zeros((SY, 128), F32)
    for v in range(2 * SX):
        place = (3 + v // 2, slice(None), slice(128 * (v % 2), 128 * (v % 2 + 1)))
        weight = volume_ref[place]
        scaled, floor_bound, ceiling = [bounds_ref[(f,) + place] for f in range(3)]
        ceilings = ceilings + weight * ceiling
        log_scaled = jnp.log(jnp.maximum(scaled, 1e-30))
        for t, bound in enumerate((ceiling, floor_bound)):
            reached = (2.0 * (log_scaled - jnp.log(jnp.maximum(bound, 1e-30))) - log_lower) / step
            index = jnp.minimum(jnp.maximum(jnp.ceil(reached), 1.0), POINTS + 1.0) - 1.0
            index = jnp.where(bound > 0.0, index, float(POINTS))
            high = jnp.floor(index * (1.0 / 128.0))
            high_ref[t, v] = high
            low_ref[t, v] = index - 128.0 * high
            sign = -1.0 if t == 0 else 1.0
            parts = three_parts(sign * weight * bound) + three_parts(-sign * weight * scaled)
            for n, part in enumerate(parts):
                value_ref[t, n, v] = part

    rows = lax.broadcasted_iota(jnp.int32, (8, 128), 0).astype(F32)
    columns = lax.broadcasted_iota(jnp.int32, (128, 128), 0).astype(F32).astype(jnp.bfloat16)

    def add_group(v, total):
        lefts, rights = [], []
        for t in range(2):
            for r in range(SY):
                hit = rows == high_ref[t, v, r : r + 1, :]
                left = [jnp.where(hit, value_ref[t, n, v, r : r + 1, :], 0.0) for n in range(6)]
                lefts.append(jnp.concatenate(left, axis=0).astype(jnp.bfloat16))
                low = jnp.broadcast_to(low_ref[t, v, r : r + 1, :], (16, 128)).astype(jnp.bfloat16)
                low = jnp.concatenate([low] * 8, axis=0)
                rights.append(jnp.where(columns == low, jnp.bfloat16(1.0), jnp.bfloat16(0.0)))
        return total + lax.dot_general(
            jnp.concatenate(rights, axis=1),
            jnp.concatenate(lefts, axis=1),
            (((1,), (1,)), ((), ())),
            preferred_element_type=F32,
        )

    total = lax.fori_loop(0, 2 * SX, add_group, jnp.zeros((128, 48), F32), unroll=4).T
    constant = total[0:8] + total[8:16] + total[16:24]
    slope = total[24:32] + total[32:40] + total[40:48]
    upto = jnp.where(
        lax.broadcasted_iota(jnp.int32, (128, 128), 0) <= lax.broadcasted_iota(jnp.int32, (128, 128), 1), 1.0, 0.0
    )
    running = lax.dot_general(
        jnp.concatenate([constant, slope], axis=0),
        upto,
        (((1,), (0,)), ((), ())),
        precision=lax.Precision.HIGHEST,
        preferred_element_type=F32,
    )
    row = lax.broadcasted_iota(jnp.int32, (8, 128), 0)
    lane = lax.broadcasted_iota(jnp.int32, (8, 128), 1)
    cumulated = []
    for part in (running[0:8], running[8:16]):
        ends = jnp.broadcast_to(part[:, 127:128], (8, 128))
        before = ends
        for shift in (1, 2, 4):
            before = before + jnp.where(row >= shift, rolled(before, -shift, 0), 0.0)
        cumulated.append(part + (before - ends))
    index = (row * 128 + lane + 1).astype(F32)
    factor = jnp.exp(-0.5 * (log_lower + step * index))
    result = jnp.sum(ceilings) + cumulated[0] + factor * cumulated[1]
    for i in range(out_ref.shape[0]):
        out_ref[i] = result


def repeat_kernel(part_ref, out_ref):
    total = part_ref[0]
    for i in range(1, part_ref.shape[0]):
        total = total + part_ref[i]
    for i in range(out_ref.shape[0]):
        out_ref[i] = total


def final_kernel(
    part_ref, own_ref, y_first, y_second, inverse_ref, mark_ref, new_design_ref, new_physical_ref,
    blocks_ref, chosen_ref, near_ref, far_ref, stiff_ref, *, factors, target
):
    total = part_ref[0]
    for i in range(1, part_ref.shape[0]):
        total = total + part_ref[i]
    low_end = jnp.minimum(jnp.sum(jnp.where(total > target, 1.0, 0.0)), POINTS - 1.0)
    multiplier = log_lower + (log_upper - log_lower) / POINTS * (low_end + 0.5)
    factor = jnp.exp(jnp.broadcast_to(-0.5 * multiplier, (SY, LANES)))
    for p in range(CHOSEN):
        tiles = []
        own = [own_ref[f, p] for f in range(3)]
        beside = []
        for f in range(3):
            row = 3 * (CHOSEN * f + p)
            beside.append(row_tile(y_first, y_second, slice(row, row + 3)))
        for scaled, floor_bound, ceiling in (own, beside):
            tiles.append(jnp.minimum(jnp.maximum(scaled * factor, floor_bound), ceiling))
        chosen = jnp.concatenate(tiles, axis=0)
        chosen_ref[p] = chosen
        near, far = row_pairs(chosen)
        near_ref[p] = near
        far_ref[p] = far
        if 3 <= p < SX + 3:
            new_design_ref[p - 3] = tiles[0][:, 0:SZ]
    for p in range(SX + 1):
        inverse = inverse_ref[p + 4]
        density = (
            filtered_plane(lambda q: chosen_ref[q], lambda q: near_ref[q], lambda q: far_ref[q], p + 2) * inverse
        )
        if p >= 1:
            new_physical_ref[p - 1] = density[0:SY, 0:SZ]
        cube = stiff_floor + density * density * density * (1.0 - stiff_floor)
        stiff_ref[p] = jnp.where(inverse > 0.0, cube, 0.0)
    for p in range(SX):
        below, here = stiff_ref[p], stiff_ref[p + 1]
        x_sum, x_diff = here + below, below - here
        x_sum_back, x_diff_back = rolled(x_sum, -1, 0), rolled(x_diff, -1, 0)
        sum_sum = (x_sum + x_sum_back)[0:SY]
        sum_diff = (x_sum_back - x_sum)[0:SY]
        diff_sum = (x_diff + x_diff_back)[0:SY]
        diff_diff = (x_diff_back - x_diff)[0:SY]
        marked = mark_ref[p] > 0.5
        even = factors[0] * (sum_sum + rolled(sum_sum, -1, 1))[:, 0:SZ]
        even = jnp.where(marked, 1.0, even)
        blocks_ref[0, p] = even
        blocks_ref[1, p] = even
        blocks_ref[2, p] = even
        yz = factors[1] * (rolled(sum_diff, -1, 1) - sum_diff)[:, 0:SZ]
        xz = factors[2] * (rolled(diff_sum, -1, 1) - diff_sum)[:, 0:SZ]
        xy = factors[3] * (diff_diff + rolled(diff_diff, -1, 1))[:, 0:SZ]
        blocks_ref[3, p] = jnp.where(marked, 0.0, yz)
        blocks_ref[4, p] = jnp.where(marked, 0.0, xz)
        blocks_ref[5, p] = jnp.where(marked, 0.0, xy)


def call(kernel, inputs, shapes, scratch, flops, spaces=None, grant=32):
    outs = [jax.ShapeDtypeStruct(shape, F32) for shape in shapes]
    return pl.pallas_call(
        kernel,
        out_shape=outs,
        in_specs=[pl.BlockSpec(memory_space=space) for space in spaces or [pltpu.VMEM] * len(inputs)],
        out_specs=[pl.BlockSpec(memory_space=pltpu.VMEM)] * len(outs),
        scratch_shapes=[pltpu.VMEM(shape, F32) if isinstance(shape, tuple) else shape for shape in scratch],
        compiler_params=pltpu.CompilerParams(vmem_limit_bytes=grant * 2**20),
        cost_estimate=pl.CostEstimate(flops=flops, bytes_accessed=min(flops, 10**6), transcendentals=0),
    )(*inputs)


def exchange(first, second, axis):
    count = lax.axis_size(axis)
    results = []
    for start, faces in enumerate((first, second)):
        pairs = [(i, (i + 1) % count) for i in range(start, count, 2)]
        results.append(lax.ppermute(faces, axis, pairs + [(j, i) for i, j in pairs]))
    return results


def other_core(values):
    return lax.ppermute(values, "gz", [(0, 1), (1, 0)])


def body(displacement, physical, design, passive, supports):
    assert design.shape == (SX, SY, SZ) and lax.axis_size("gz") == 2
    sizes = [lax.axis_size(axis) for axis in ("gx", "gy", "gz")]
    extents = (SX * sizes[0], SY * sizes[1], SZ * sizes[2])
    block = (SX, SY, SZ)
    even = lax.axis_index("gx") % 2 == 0

    def swaps(fields, depth):
        top, bottom = fields[:, SX - depth :], fields[:, 0:depth]
        return jnp.where(even, top, bottom), jnp.where(even, bottom, top)

    x_faces = exchange(*swaps(jnp.concatenate([displacement, physical[None]], axis=0), 5), "gx")
    frame = (ELEMENTS, ROWS, LANES)
    own_frame = (ELEMENTS, SY, LANES)
    weights = call(
        functools.partial(weights_kernel, extents=extents), (supports.reshape(1, -1),),
        [frame, own_frame, (CHOSEN, SY, LANES), block], [own_frame, own_frame], 10**7,
    )
    design_faces = swaps(jnp.stack([design, passive.astype(F32)]), 3)
    x_faces, design_faces, (inverse, edge, volume_weight, marks) = lax.optimization_barrier(
        (x_faces, design_faces, weights)
    )

    groups = energy_groups()
    faces = (11 * NODES, SZ)
    tiles = (4 * NODES, SY, SZ)
    ext = (4, NODES, SY, LANES)
    y_faces = call(faces_y_kernel, (displacement, physical, *x_faces), [faces, faces], [], 10**6)
    y_faces, x_faces, design_faces = lax.optimization_barrier((y_faces, x_faces, design_faces))
    y_faces = exchange(*y_faces, "gy")
    design_faces = exchange(*design_faces, "gx")
    (side,) = call(faces_side_kernel, (displacement, physical, *x_faces), [(4 * NODES, SY, SIDE)], [], 1)
    (inner_part,) = call(
        functools.partial(inner_kernel, groups=groups),
        (displacement, physical, *x_faces, other_core(side), inverse), [own_frame], [ext], 1,
    )
    y_faces, inner_part = lax.optimization_barrier((y_faces, inner_part))
    edge_tiles, side = call(
        faces_edge_kernel, (displacement, physical, *x_faces, *y_faces, design, passive, *design_faces),
        [tiles, (4 * NODES + 2 * CHOSEN, SY, SIDE)], [], 10**6,
    )
    side = other_core(side)

    faces = (9 * CHOSEN, LANES)
    inner, outer = sizes[1] * sizes[2], sizes[0]
    elements = (2 * SX, SY, 128)
    bounds, *y_bounds, part = call(
        functools.partial(design_kernel, groups=groups),
        (design, passive, *design_faces, inner_part, edge_tiles, side, inverse, edge, volume_weight),
        [(3, CHOSEN, SY, LANES), faces, faces, (inner, 8, 128)],
        [ext, own_frame, own_frame, own_frame, own_frame]
        + [(2,) + elements, (2,) + elements, (2, 6) + elements], 10**7,
    )

    part = lax.all_to_all(part, ("gy", "gz"), 0, 0, tiled=True)
    y_bounds, part = lax.optimization_barrier((y_bounds, part))
    y_bounds = exchange(*y_bounds, "gy")
    (part,) = call(repeat_kernel, (part,), [(outer, 8, 128)], [], 10**5)
    part = lax.all_to_all(part, "gx", 0, 0, tiled=True)

    chosen = (CHOSEN, ROWS, LANES)
    target = volume_share * (extents[0] * extents[1] * extents[2])
    new_design, new_physical, node_blocks = call(
        functools.partial(final_kernel, factors=[float(f) for f in corner_factors()], target=target),
        (part, bounds, *y_bounds, inverse, marks), [block, block, (6,) + block],
        [chosen, chosen, chosen, (SX + 1, ROWS, LANES)], 10**7,
    )
    return (new_design, new_physical, node_blocks)


def solution(mesh):
    in_specs = (
        P(None, "gx", "gy", "gz"),
        P("gx", "gy", "gz"),
        P("gx", "gy", "gz"),
        P("gx", "gy", "gz"),
        P(),
    )
    out_specs = (P("gx", "gy", "gz"), P("gx", "gy", "gz"), P(None, "gx", "gy", "gz"))
    return jax.shard_map(body, mesh=mesh, in_specs=in_specs, out_specs=out_specs, check_vma=False)
```

```python
import functools
import math

import jax
import jax.numpy as jnp
import numpy as np
from jax import lax
from jax.experimental import pallas as pl
from jax.experimental.pallas import tpu as pltpu
from jax.sharding import PartitionSpec as P

STEPS = 10

filter_radius = 2.5
penalty = 3.0
move_limit = 0.2
stiff_floor = 1e-09
volume_share = 0.5
log_lower = -20.0
log_upper = 20.0
poisson = 0.3

SX, SY, SZ = 8, 8, 256
ROWS, LANES, SIDE = 16, 384, 128
NODES, ELEMENTS, CHOSEN = SX + 10, SX + 9, SX + 5
POINTS = 2**STEPS
F32 = jnp.float32


def corner_offsets():
    return [(q // 4, q // 2 % 2, q % 2) for q in range(8)]


def hex_stiffness():
    lame_first = poisson / ((1.0 + poisson) * (1.0 - 2.0 * poisson))
    shear_modulus = 0.5 / (1.0 + poisson)
    elastic = np.zeros((6, 6))
    elastic[:3, :3] = lame_first
    for d in range(3):
        elastic[d, d] += 2.0 * shear_modulus
        elastic[d + 3, d + 3] = shear_modulus
    corners = corner_offsets()
    points = [0.5 - 0.5 / math.sqrt(3.0), 0.5 + 0.5 / math.sqrt(3.0)]
    matrix = np.zeros((24, 24))
    for p in points:
        for q in points:
            for r in points:
                location = [p, q, r]
                gradients = np.zeros((8, 3))
                for n in range(8):
                    factors = [
                        location[e] if corners[n][e] == 1 else 1.0 - location[e] for e in range(3)
                    ]
                    for d in range(3):
                        sign_value = 1.0 if corners[n][d] == 1 else -1.0
                        gradients[n, d] = sign_value * factors[(d + 1) % 3] * factors[(d + 2) % 3]
                strain = np.zeros((6, 24))
                for n in range(8):
                    column = 3 * n
                    strain[0, column] = gradients[n, 0]
                    strain[1, column + 1] = gradients[n, 1]
                    strain[2, column + 2] = gradients[n, 2]
                    strain[3, column + 1] = gradients[n, 2]
                    strain[3, column + 2] = gradients[n, 1]
                    strain[4, column] = gradients[n, 2]
                    strain[4, column + 2] = gradients[n, 0]
                    strain[5, column] = gradients[n, 1]
                    strain[5, column + 1] = gradients[n, 0]
                matrix += strain.T @ elastic @ strain / 8.0
    return matrix


def energy_groups():
    corners = corner_offsets()
    modes = np.zeros((24, 24))
    for s in range(8):
        bits = (s // 4, s // 2 % 2, s % 2)
        for n in range(8):
            sign_value = 1.0
            for e in range(3):
                if bits[e] == 1 and corners[n][e] == 0:
                    sign_value = -sign_value
            for d in range(3):
                modes[3 * n + d, 3 * s + d] = sign_value
    form = modes.T @ hex_stiffness() @ modes / 64.0
    groups = []

    def add(coefficient, members):
        if abs(coefficient) < 1e-9:
            return
        for group in groups:
            if abs(group[0] - coefficient) < 1e-9:
                group[1].append(members)
                return
        groups.append((coefficient, [members]))

    for parity in range(8):
        left = [3 * (parity ^ (4, 2, 1)[d]) + d for d in range(3)]
        while left:
            first = left[0]
            block = [m for m in left if m == first or abs(form[first, m]) > 1e-9]
            left = [m for m in left if m not in block]
            beside = form[block[0], block[1]] if len(block) > 1 else 0.0
            add(beside, block)
            for m in block:
                add(form[m, m] - beside, [m])
    rebuilt = np.zeros((24, 24))
    for coefficient, sums in groups:
        for members in sums:
            rebuilt[np.ix_(members, members)] += coefficient
    assert np.abs(rebuilt - form).max() < 1e-9
    return groups


def corner_factors():
    matrix = hex_stiffness()
    factors = (matrix[0, 0], matrix[1, 2], matrix[0, 2], matrix[0, 1])
    for n, corner in enumerate(corner_offsets()):
        sign = [1.0 if c == 1 else -1.0 for c in corner]
        block = matrix[3 * n : 3 * n + 3, 3 * n : 3 * n + 3]
        assert np.allclose(np.diag(block), factors[0])
        assert np.allclose(block[1, 2], factors[1] * sign[1] * sign[2])
        assert np.allclose(block[0, 2], factors[2] * sign[0] * sign[2])
        assert np.allclose(block[0, 1], factors[3] * sign[0] * sign[1])
    return factors


def tap(square):
    return max(0.0, filter_radius - math.sqrt(square))


def rolled(value, steps, dim):
    return pltpu.roll(value, (-steps) % value.shape[dim], dim)


def row_pairs(plane):
    return (
        rolled(plane, 1, 0) + rolled(plane, -1, 0),
        rolled(plane, 2, 0) + rolled(plane, -2, 0),
    )


def filtered_plane(plane_of, near_of, far_of, p):
    ring_0 = plane_of(p)
    ring_1 = near_of(p) + plane_of(p - 1) + plane_of(p + 1)
    ring_2 = near_of(p - 1) + near_of(p + 1)
    ring_4 = far_of(p) + plane_of(p - 2) + plane_of(p + 2)
    ring_5 = far_of(p - 1) + far_of(p + 1) + near_of(p - 2) + near_of(p + 2)
    layers = []
    for c in (0, 1, 2):
        total = None
        for square, ring in ((0, ring_0), (1, ring_1), (2, ring_2), (4, ring_4), (5, ring_5)):
            weight = tap(square + c * c)
            if weight > 0.0:
                total = weight * ring if total is None else total + weight * ring
        layers.append(total)
    middle, near, far = layers
    return middle + (rolled(near, 1, 1) + rolled(near, -1, 1)) + (rolled(far, 2, 1) + rolled(far, -2, 1))


def weights_kernel(support_ref, inverse_ref, edge_ref, volume_ref, mark_ref, near_ref, far_ref, *, extents):
    total_x, total_y, total_z = extents
    first_x = lax.axis_index("gx") * SX
    first_y = lax.axis_index("gy") * SY
    first_z = lax.axis_index("gz") * SZ
    row = lax.broadcasted_iota(jnp.int32, (ROWS, LANES), 0)
    lane = lax.broadcasted_iota(jnp.int32, (ROWS, LANES), 1)
    y = first_y + jnp.where(row < 12, row, row - ROWS)
    z = first_z + jnp.where(lane < SZ + SIDE // 2, lane, lane - LANES)
    inside = jnp.where((y >= 0) & (y < total_y) & (z >= 0) & (z < total_z), 1.0, 0.0).astype(F32)
    near, far = row_pairs(inside)

    def present(p):
        x = first_x + p
        return jnp.where((x >= 0) & (x < total_x), 1.0, 0.0).astype(F32)

    for p in range(ELEMENTS):
        x = p - 5
        weight_sum = filtered_plane(
            lambda q: inside * present(q), lambda q: near * present(q), lambda q: far * present(q), x
        )
        here = inside * present(x)
        inverse = jnp.where(here > 0.0, 1.0 / jnp.where(here > 0.0, weight_sum, 1.0), 0.0)
        inverse_ref[p] = inverse
        edge_ref[p] = jnp.concatenate([inverse[7:11], inverse[14:16], inverse[0:2]], axis=0)
        inverse_near, inverse_far = row_pairs(inverse)
        near_ref[p] = inverse_near[0:SY]
        far_ref[p] = inverse_far[0:SY]
    for p in range(CHOSEN):
        volume_ref[p] = filtered_plane(
            lambda q: inverse_ref[q, 0:SY], lambda q: near_ref[q], lambda q: far_ref[q], p + 2
        )
    node = support_ref[...]
    node_x = node // (total_y * total_z) - first_x
    node_y = node // total_z % total_y - first_y
    node_z = node % total_z - first_z
    owned = (node_x >= 0) & (node_x < SX) & (node_y >= 0) & (node_y < SY)
    line = jnp.where(owned, node_x * SY + node_y, -1)
    count = node.shape[1]
    lines = jnp.where(lax.broadcasted_iota(jnp.int32, (SX * SY, count), 0) == line, 1.0, 0.0)
    lanes = jnp.where(lax.broadcasted_iota(jnp.int32, (SZ, count), 0) == node_z, 1.0, 0.0)
    hits = lax.dot_general(
        lines.astype(jnp.bfloat16),
        lanes.astype(jnp.bfloat16),
        (((1,), (1,)), ((), ())),
        preferred_element_type=F32,
    )
    for p in range(SX):
        mark_ref[p] = hits[p * SY : (p + 1) * SY]


def is_even(axis):
    return lax.axis_index(axis) % 2 == 0


def place_pair(even, first_ref, second_ref, top, bottom, place):
    first_ref[place] = jnp.where(even, top, bottom)
    second_ref[place] = jnp.where(even, bottom, top)


def low_high(axis, first_ref, second_ref, place):
    index = lax.axis_index(axis)
    first, second = first_ref[place], second_ref[place]
    low = jnp.where(index == 0, 0.0, jnp.where(index % 2 == 0, second, first))
    high = jnp.where(index == lax.axis_size(axis) - 1, 0.0, jnp.where(index % 2 == 0, first, second))
    return low, high


def row_place(index):
    if index < 3 * NODES:
        return slice(3 * index, 3 * index + 3)
    return slice(2 * index + 3 * NODES, 2 * index + 3 * NODES + 2)


def row_tile(first_ref, second_ref, place):
    low, high = low_high("gy", first_ref, second_ref, place)
    filler = jnp.zeros((SY - 2 * low.shape[0], low.shape[1]), F32)
    return jnp.concatenate([high, filler, low], axis=0)


def plane_reader(shift_ref, physical_ref, x_first, x_second):
    def read(index):
        f, x = index // NODES, index % NODES - 5
        if 0 <= x < SX:
            return shift_ref[f, x] if f < 3 else physical_ref[x]
        low, high = low_high("gx", x_first, x_second, (f, x + 5 if x < 0 else x - SX))
        return low if x < 0 else high

    return read


def design_reader(design_ref, passive_ref, x_first, x_second):
    def read(index):
        f, x = index // CHOSEN, index % CHOSEN - 3
        if 0 <= x < SX:
            return design_ref[x] if f == 0 else passive_ref[x].astype(F32)
        low, high = low_high("gx", x_first, x_second, (f, x + 3 if x < 0 else x - SX))
        return low if x < 0 else high

    return read


def near_half(plane):
    return jnp.where(lax.axis_index("gz") == 0, plane[:, SZ - SIDE :], plane[:, 0:SIDE])


def edge_tile(plane, low, high):
    missing = 3 - high.shape[0]
    filler = [jnp.zeros((missing, SZ), F32)] if missing else []
    return jnp.concatenate([plane[7:8], high, *filler, low[low.shape[0] - 2 :], plane[0:2]], axis=0)


def faces_y_kernel(shift_ref, physical_ref, x_first, x_second, first_ref, second_ref):
    even = is_even("gy")
    read = plane_reader(shift_ref, physical_ref, x_first, x_second)
    for index in range(4 * NODES):
        plane = read(index)
        rows = row_place(index)
        depth = rows.stop - rows.start
        place_pair(even, first_ref, second_ref, plane[SY - depth :], plane[0:depth], rows)


def faces_side_kernel(shift_ref, physical_ref, x_first, x_second, side_ref):
    read = plane_reader(shift_ref, physical_ref, x_first, x_second)
    for index in range(4 * NODES):
        side_ref[index] = near_half(read(index))


def faces_edge_kernel(
    shift_ref, physical_ref, x_first, x_second, y_first, y_second, design_ref, passive_ref, d_first, d_second,
    edge_ref, side_ref
):
    read = plane_reader(shift_ref, physical_ref, x_first, x_second)
    for index in range(4 * NODES):
        low, high = low_high("gy", y_first, y_second, row_place(index))
        tile = edge_tile(read(index), low, high)
        edge_ref[index] = tile
        side_ref[index] = near_half(tile)
    read = design_reader(design_ref, passive_ref, d_first, d_second)
    for index in range(2 * CHOSEN):
        side_ref[4 * NODES + index] = near_half(read(index))


def scaled_energy(ext_ref, read, side, inverse_of, out_ref, groups):
    lane = lax.broadcasted_iota(jnp.int32, (SY, SIDE), 1)
    start = lax.axis_index("gz") * (SIDE // 2)
    keep = (lane >= start) & (lane < start + SIDE // 2)
    for f in range(4):
        for p in range(NODES):
            index = NODES * f + p
            ext_ref[f, p, :, 0:SZ] = read(index)
            ext_ref[f, p, :, SZ:LANES] = jnp.where(keep, side[index], 0.0)
    scale = penalty * (1.0 - stiff_floor)

    @pl.loop(0, ELEMENTS, unroll=True)
    def _(p):
        modes = {}
        for d in range(3):
            here, above = ext_ref[d, p], ext_ref[d, p + 1]
            for a, along_x in enumerate((here + above, above - here)):
                beyond = rolled(along_x, 1, 0)
                for b, along_y in enumerate((along_x + beyond, beyond - along_x)):
                    next_lane = rolled(along_y, 1, 1)
                    for c, mode in enumerate((along_y + next_lane, next_lane - along_y)):
                        modes[3 * (4 * a + 2 * b + c) + d] = mode
        energy = None
        for coefficient, sums in groups:
            squares = None
            for members in sums:
                value = functools.reduce(lambda left, right: left + right, [modes[m] for m in members])
                squares = value * value if squares is None else squares + value * value
            squares = float(coefficient) * squares
            energy = squares if energy is None else energy + squares
        density = ext_ref[3, p]
        out_ref[p] = scale * density * density * energy * inverse_of(p)


def inner_kernel(shift_ref, physical_ref, x_first, x_second, side, inverse_ref, out_ref, ext_ref, *, groups):
    read = plane_reader(shift_ref, physical_ref, x_first, x_second)
    scaled_energy(ext_ref, read, side, lambda p: inverse_ref[p, 0:SY], out_ref, groups)


def design_kernel(
    design_ref, passive_ref, d_first, d_second, inner_ref, edge_tiles, edge_side, inverse_ref, edge_ref, volume_ref,
    out_ref, first_ref, second_ref, part_ref, ext_ref, outer_ref, sens_ref, near_ref, far_ref, high_ref, low_ref,
    value_ref, *, groups
):
    even = is_even("gy")
    scaled_energy(
        ext_ref, lambda index: edge_tiles[index], edge_side, lambda p: edge_ref[p], outer_ref, groups
    )
    row = lax.broadcasted_iota(jnp.int32, (SY, LANES), 0)
    for p in range(ELEMENTS):
        outer = outer_ref[p]
        own = jnp.where(row == 7, rolled(outer, -7, 0), inner_ref[p])
        beyond = jnp.where(row < 4, rolled(outer, 1, 0), rolled(outer, -2, 0))
        sens_ref[p] = own
        near, far = row_pairs(jnp.concatenate([own, beyond], axis=0))
        near_ref[p] = near[0:SY]
        far_ref[p] = far[0:SY]

    read_design = design_reader(design_ref, passive_ref, d_first, d_second)
    for p in range(CHOSEN):
        filtered = filtered_plane(lambda q: sens_ref[q], lambda q: near_ref[q], lambda q: far_ref[q], p + 2)
        index = 4 * NODES + p
        design = jnp.concatenate([read_design(p), edge_side[index]], axis=1)
        solid = jnp.concatenate([read_design(p + CHOSEN), edge_side[index + CHOSEN]], axis=1) > 0.5
        inside = inverse_ref[p + 2, 0:SY] > 0.0
        scaled = design * jnp.sqrt(filtered / jnp.where(inside, volume_ref[p], 1.0))
        floor_bound = jnp.where(solid, 1.0, jnp.maximum(0.0, design - move_limit))
        ceiling = jnp.where(solid, 1.0, jnp.minimum(1.0, design + move_limit))
        for f, value in enumerate((scaled, floor_bound, ceiling)):
            value = jnp.where(inside, value, 0.0)
            out_ref[f, p] = value
            row = 3 * (CHOSEN * f + p)
            place_pair(even, first_ref, second_ref, value[SY - 3 :], value[0:3], slice(row, row + 3))
    add_volumes(out_ref, volume_ref, part_ref, high_ref, low_ref, value_ref)


def three_parts(value):
    first = value.astype(jnp.bfloat16).astype(F32)
    second = (value - first).astype(jnp.bfloat16).astype(F32)
    return first, second, value - first - second


def add_volumes(bounds_ref, volume_ref, out_ref, high_ref, low_ref, value_ref):
    step = (log_upper - log_lower) / POINTS
    ceilings = jnp.zeros((SY, 128), F32)
    for v in range(2 * SX):
        place = (3 + v // 2, slice(None), slice(128 * (v % 2), 128 * (v % 2 + 1)))
        weight = volume_ref[place]
        scaled, floor_bound, ceiling = [bounds_ref[(f,) + place] for f in range(3)]
        ceilings = ceilings + weight * ceiling
        log_scaled = jnp.log(jnp.maximum(scaled, 1e-30))
        for t, bound in enumerate((ceiling, floor_bound)):
            reached = (2.0 * (log_scaled - jnp.log(jnp.maximum(bound, 1e-30))) - log_lower) / step
            index = jnp.minimum(jnp.maximum(jnp.ceil(reached), 1.0), POINTS + 1.0) - 1.0
            index = jnp.where(bound > 0.0, index, float(POINTS))
            high = jnp.floor(index * (1.0 / 128.0))
            high_ref[t, v] = high
            low_ref[t, v] = index - 128.0 * high
            sign = -1.0 if t == 0 else 1.0
            parts = three_parts(sign * weight * bound) + three_parts(-sign * weight * scaled)
            for n, part in enumerate(parts):
                value_ref[t, n, v] = part

    rows = lax.broadcasted_iota(jnp.int32, (8, 128), 0).astype(F32)
    columns = lax.broadcasted_iota(jnp.int32, (128, 128), 0).astype(F32).astype(jnp.bfloat16)

    def add_group(v, total):
        lefts, rights = [], []
        for t in range(2):
            for r in range(SY):
                hit = rows == high_ref[t, v, r : r + 1, :]
                left = [jnp.where(hit, value_ref[t, n, v, r : r + 1, :], 0.0) for n in range(6)]
                lefts.append(jnp.concatenate(left, axis=0).astype(jnp.bfloat16))
                low = jnp.broadcast_to(low_ref[t, v, r : r + 1, :], (16, 128)).astype(jnp.bfloat16)
                low = jnp.concatenate([low] * 8, axis=0)
                rights.append(jnp.where(columns == low, jnp.bfloat16(1.0), jnp.bfloat16(0.0)))
        return total + lax.dot_general(
            jnp.concatenate(rights, axis=1),
            jnp.concatenate(lefts, axis=1),
            (((1,), (1,)), ((), ())),
            preferred_element_type=F32,
        )

    total = lax.fori_loop(0, 2 * SX, add_group, jnp.zeros((128, 48), F32), unroll=8).T
    constant = total[0:8] + total[8:16] + total[16:24]
    slope = total[24:32] + total[32:40] + total[40:48]
    upto = jnp.where(
        lax.broadcasted_iota(jnp.int32, (128, 128), 0) <= lax.broadcasted_iota(jnp.int32, (128, 128), 1), 1.0, 0.0
    )
    running = lax.dot_general(
        jnp.concatenate([constant, slope], axis=0),
        upto,
        (((1,), (0,)), ((), ())),
        precision=lax.Precision.HIGHEST,
        preferred_element_type=F32,
    )
    row = lax.broadcasted_iota(jnp.int32, (8, 128), 0)
    lane = lax.broadcasted_iota(jnp.int32, (8, 128), 1)
    cumulated = []
    for part in (running[0:8], running[8:16]):
        ends = jnp.broadcast_to(part[:, 127:128], (8, 128))
        before = ends
        for shift in (1, 2, 4):
            before = before + jnp.where(row >= shift, rolled(before, -shift, 0), 0.0)
        cumulated.append(part + (before - ends))
    index = (row * 128 + lane + 1).astype(F32)
    factor = jnp.exp(-0.5 * (log_lower + step * index))
    result = jnp.sum(ceilings) + cumulated[0] + factor * cumulated[1]
    for i in range(out_ref.shape[0]):
        out_ref[i] = result


def repeat_kernel(part_ref, out_ref):
    total = part_ref[0]
    for i in range(1, part_ref.shape[0]):
        total = total + part_ref[i]
    for i in range(out_ref.shape[0]):
        out_ref[i] = total


def final_kernel(
    part_ref, own_ref, y_first, y_second, inverse_ref, mark_ref, new_design_ref, new_physical_ref,
    blocks_ref, chosen_ref, near_ref, far_ref, stiff_ref, *, factors, target
):
    total = part_ref[0]
    for i in range(1, part_ref.shape[0]):
        total = total + part_ref[i]
    low_end = jnp.minimum(jnp.sum(jnp.where(total > target, 1.0, 0.0)), POINTS - 1.0)
    multiplier = log_lower + (log_upper - log_lower) / POINTS * (low_end + 0.5)
    factor = jnp.exp(jnp.broadcast_to(-0.5 * multiplier, (SY, LANES)))
    for p in range(CHOSEN):
        tiles = []
        own = [own_ref[f, p] for f in range(3)]
        beside = []
        for f in range(3):
            row = 3 * (CHOSEN * f + p)
            beside.append(row_tile(y_first, y_second, slice(row, row + 3)))
        for scaled, floor_bound, ceiling in (own, beside):
            tiles.append(jnp.minimum(jnp.maximum(scaled * factor, floor_bound), ceiling))
        chosen = jnp.concatenate(tiles, axis=0)
        chosen_ref[p] = chosen
        near, far = row_pairs(chosen)
        near_ref[p] = near
        far_ref[p] = far
        if 3 <= p < SX + 3:
            new_design_ref[p - 3] = tiles[0][:, 0:SZ]
    for p in range(SX + 1):
        inverse = inverse_ref[p + 4]
        density = (
            filtered_plane(lambda q: chosen_ref[q], lambda q: near_ref[q], lambda q: far_ref[q], p + 2) * inverse
        )
        if p >= 1:
            new_physical_ref[p - 1] = density[0:SY, 0:SZ]
        cube = stiff_floor + density * density * density * (1.0 - stiff_floor)
        stiff_ref[p] = jnp.where(inverse > 0.0, cube, 0.0)
    for p in range(SX):
        below, here = stiff_ref[p], stiff_ref[p + 1]
        x_sum, x_diff = here + below, below - here
        x_sum_back, x_diff_back = rolled(x_sum, -1, 0), rolled(x_diff, -1, 0)
        sum_sum = (x_sum + x_sum_back)[0:SY]
        sum_diff = (x_sum_back - x_sum)[0:SY]
        diff_sum = (x_diff + x_diff_back)[0:SY]
        diff_diff = (x_diff_back - x_diff)[0:SY]
        marked = mark_ref[p] > 0.5
        even = factors[0] * (sum_sum + rolled(sum_sum, -1, 1))[:, 0:SZ]
        even = jnp.where(marked, 1.0, even)
        blocks_ref[0, p] = even
        blocks_ref[1, p] = even
        blocks_ref[2, p] = even
        yz = factors[1] * (rolled(sum_diff, -1, 1) - sum_diff)[:, 0:SZ]
        xz = factors[2] * (rolled(diff_sum, -1, 1) - diff_sum)[:, 0:SZ]
        xy = factors[3] * (diff_diff + rolled(diff_diff, -1, 1))[:, 0:SZ]
        blocks_ref[3, p] = jnp.where(marked, 0.0, yz)
        blocks_ref[4, p] = jnp.where(marked, 0.0, xz)
        blocks_ref[5, p] = jnp.where(marked, 0.0, xy)


def call(kernel, inputs, shapes, scratch, flops, spaces=None, grant=32):
    outs = [jax.ShapeDtypeStruct(shape, F32) for shape in shapes]
    return pl.pallas_call(
        kernel,
        out_shape=outs,
        in_specs=[pl.BlockSpec(memory_space=space) for space in spaces or [pltpu.VMEM] * len(inputs)],
        out_specs=[pl.BlockSpec(memory_space=pltpu.VMEM)] * len(outs),
        scratch_shapes=[pltpu.VMEM(shape, F32) if isinstance(shape, tuple) else shape for shape in scratch],
        compiler_params=pltpu.CompilerParams(vmem_limit_bytes=grant * 2**20),
        cost_estimate=pl.CostEstimate(flops=flops, bytes_accessed=min(flops, 10**6), transcendentals=0),
    )(*inputs)


def exchange(first, second, axis):
    count = lax.axis_size(axis)
    results = []
    for start, faces in enumerate((first, second)):
        pairs = [(i, (i + 1) % count) for i in range(start, count, 2)]
        results.append(lax.ppermute(faces, axis, pairs + [(j, i) for i, j in pairs]))
    return results


def other_core(values):
    return lax.ppermute(values, "gz", [(0, 1), (1, 0)])


def body(displacement, physical, design, passive, supports):
    assert design.shape == (SX, SY, SZ) and lax.axis_size("gz") == 2
    sizes = [lax.axis_size(axis) for axis in ("gx", "gy", "gz")]
    extents = (SX * sizes[0], SY * sizes[1], SZ * sizes[2])
    block = (SX, SY, SZ)
    even = lax.axis_index("gx") % 2 == 0

    def swaps(fields, depth):
        top, bottom = fields[:, SX - depth :], fields[:, 0:depth]
        return jnp.where(even, top, bottom), jnp.where(even, bottom, top)

    x_faces = exchange(*swaps(jnp.concatenate([displacement, physical[None]], axis=0), 5), "gx")
    frame = (ELEMENTS, ROWS, LANES)
    own_frame = (ELEMENTS, SY, LANES)
    weights = call(
        functools.partial(weights_kernel, extents=extents), (supports.reshape(1, -1),),
        [frame, own_frame, (CHOSEN, SY, LANES), block], [own_frame, own_frame], 10**7,
    )
    design_faces = swaps(jnp.stack([design, passive.astype(F32)]), 3)
    x_faces, design_faces, (inverse, edge, volume_weight, marks) = lax.optimization_barrier(
        (x_faces, design_faces, weights)
    )

    groups = energy_groups()
    faces = (11 * NODES, SZ)
    tiles = (4 * NODES, SY, SZ)
    ext = (4, NODES, SY, LANES)
    y_faces = call(faces_y_kernel, (displacement, physical, *x_faces), [faces, faces], [], 10**6)
    y_faces, x_faces, design_faces = lax.optimization_barrier((y_faces, x_faces, design_faces))
    y_faces = exchange(*y_faces, "gy")
    design_faces = exchange(*design_faces, "gx")
    (side,) = call(faces_side_kernel, (displacement, physical, *x_faces), [(4 * NODES, SY, SIDE)], [], 1)
    (inner_part,) = call(
        functools.partial(inner_kernel, groups=groups),
        (displacement, physical, *x_faces, other_core(side), inverse), [own_frame], [ext], 1,
    )
    y_faces, inner_part = lax.optimization_barrier((y_faces, inner_part))
    edge_tiles, side = call(
        faces_edge_kernel, (displacement, physical, *x_faces, *y_faces, design, passive, *design_faces),
        [tiles, (4 * NODES + 2 * CHOSEN, SY, SIDE)], [], 10**6,
    )
    side = other_core(side)

    faces = (9 * CHOSEN, LANES)
    inner, outer = sizes[1] * sizes[2], sizes[0]
    elements = (2 * SX, SY, 128)
    bounds, *y_bounds, part = call(
        functools.partial(design_kernel, groups=groups),
        (design, passive, *design_faces, inner_part, edge_tiles, side, inverse, edge, volume_weight),
        [(3, CHOSEN, SY, LANES), faces, faces, (inner, 8, 128)],
        [ext, own_frame, own_frame, own_frame, own_frame]
        + [(2,) + elements, (2,) + elements, (2, 6) + elements], 10**7,
    )

    part = lax.all_to_all(part, ("gy", "gz"), 0, 0, tiled=True)
    y_bounds, part = lax.optimization_barrier((y_bounds, part))
    y_bounds = exchange(*y_bounds, "gy")
    (part,) = call(repeat_kernel, (part,), [(outer, 8, 128)], [], 10**5)
    part = lax.all_to_all(part, "gx", 0, 0, tiled=True)

    chosen = (CHOSEN, ROWS, LANES)
    target = volume_share * (extents[0] * extents[1] * extents[2])
    new_design, new_physical, node_blocks = call(
        functools.partial(final_kernel, factors=[float(f) for f in corner_factors()], target=target),
        (part, bounds, *y_bounds, inverse, marks), [block, block, (6,) + block],
        [chosen, chosen, chosen, (SX + 1, ROWS, LANES)], 10**7,
    )
    return (new_design, new_physical, node_blocks)


def solution(mesh):
    in_specs = (
        P(None, "gx", "gy", "gz"),
        P("gx", "gy", "gz"),
        P("gx", "gy", "gz"),
        P("gx", "gy", "gz"),
        P(),
    )
    out_specs = (P("gx", "gy", "gz"), P("gx", "gy", "gz"), P(None, "gx", "gy", "gz"))
    return jax.shard_map(body, mesh=mesh, in_specs=in_specs, out_specs=out_specs, check_vma=False)
```

```python
import functools
import math

import jax
import jax.numpy as jnp
import numpy as np
from jax import lax
from jax.experimental import pallas as pl
from jax.experimental.pallas import tpu as pltpu
from jax.sharding import PartitionSpec as P

STEPS = 10

filter_radius = 2.5
penalty = 3.0
move_limit = 0.2
stiff_floor = 1e-09
volume_share = 0.5
log_lower = -20.0
log_upper = 20.0
poisson = 0.3

SX, SY, SZ = 8, 8, 256
ROWS, LANES, SIDE = 16, 384, 128
NODES, ELEMENTS, CHOSEN = SX + 10, SX + 9, SX + 5
POINTS = 2**STEPS
F32 = jnp.float32


def corner_offsets():
    return [(q // 4, q // 2 % 2, q % 2) for q in range(8)]


def hex_stiffness():
    lame_first = poisson / ((1.0 + poisson) * (1.0 - 2.0 * poisson))
    shear_modulus = 0.5 / (1.0 + poisson)
    elastic = np.zeros((6, 6))
    elastic[:3, :3] = lame_first
    for d in range(3):
        elastic[d, d] += 2.0 * shear_modulus
        elastic[d + 3, d + 3] = shear_modulus
    corners = corner_offsets()
    points = [0.5 - 0.5 / math.sqrt(3.0), 0.5 + 0.5 / math.sqrt(3.0)]
    matrix = np.zeros((24, 24))
    for p in points:
        for q in points:
            for r in points:
                location = [p, q, r]
                gradients = np.zeros((8, 3))
                for n in range(8):
                    factors = [
                        location[e] if corners[n][e] == 1 else 1.0 - location[e] for e in range(3)
                    ]
                    for d in range(3):
                        sign_value = 1.0 if corners[n][d] == 1 else -1.0
                        gradients[n, d] = sign_value * factors[(d + 1) % 3] * factors[(d + 2) % 3]
                strain = np.zeros((6, 24))
                for n in range(8):
                    column = 3 * n
                    strain[0, column] = gradients[n, 0]
                    strain[1, column + 1] = gradients[n, 1]
                    strain[2, column + 2] = gradients[n, 2]
                    strain[3, column + 1] = gradients[n, 2]
                    strain[3, column + 2] = gradients[n, 1]
                    strain[4, column] = gradients[n, 2]
                    strain[4, column + 2] = gradients[n, 0]
                    strain[5, column] = gradients[n, 1]
                    strain[5, column + 1] = gradients[n, 0]
                matrix += strain.T @ elastic @ strain / 8.0
    return matrix


def energy_groups():
    corners = corner_offsets()
    modes = np.zeros((24, 24))
    for s in range(8):
        bits = (s // 4, s // 2 % 2, s % 2)
        for n in range(8):
            sign_value = 1.0
            for e in range(3):
                if bits[e] == 1 and corners[n][e] == 0:
                    sign_value = -sign_value
            for d in range(3):
                modes[3 * n + d, 3 * s + d] = sign_value
    form = modes.T @ hex_stiffness() @ modes / 64.0
    groups = []

    def add(coefficient, members):
        if abs(coefficient) < 1e-9:
            return
        for group in groups:
            if abs(group[0] - coefficient) < 1e-9:
                group[1].append(members)
                return
        groups.append((coefficient, [members]))

    for parity in range(8):
        left = [3 * (parity ^ (4, 2, 1)[d]) + d for d in range(3)]
        while left:
            first = left[0]
            block = [m for m in left if m == first or abs(form[first, m]) > 1e-9]
            left = [m for m in left if m not in block]
            beside = form[block[0], block[1]] if len(block) > 1 else 0.0
            add(beside, block)
            for m in block:
                add(form[m, m] - beside, [m])
    rebuilt = np.zeros((24, 24))
    for coefficient, sums in groups:
        for members in sums:
            rebuilt[np.ix_(members, members)] += coefficient
    assert np.abs(rebuilt - form).max() < 1e-9
    return groups


def corner_factors():
    matrix = hex_stiffness()
    factors = (matrix[0, 0], matrix[1, 2], matrix[0, 2], matrix[0, 1])
    for n, corner in enumerate(corner_offsets()):
        sign = [1.0 if c == 1 else -1.0 for c in corner]
        block = matrix[3 * n : 3 * n + 3, 3 * n : 3 * n + 3]
        assert np.allclose(np.diag(block), factors[0])
        assert np.allclose(block[1, 2], factors[1] * sign[1] * sign[2])
        assert np.allclose(block[0, 2], factors[2] * sign[0] * sign[2])
        assert np.allclose(block[0, 1], factors[3] * sign[0] * sign[1])
    return factors


def tap(square):
    return max(0.0, filter_radius - math.sqrt(square))


def rolled(value, steps, dim):
    return pltpu.roll(value, (-steps) % value.shape[dim], dim)


def row_pairs(plane):
    return (
        rolled(plane, 1, 0) + rolled(plane, -1, 0),
        rolled(plane, 2, 0) + rolled(plane, -2, 0),
    )


def filtered_plane(plane_of, near_of, far_of, p):
    ring_0 = plane_of(p)
    ring_1 = near_of(p) + plane_of(p - 1) + plane_of(p + 1)
    ring_2 = near_of(p - 1) + near_of(p + 1)
    ring_4 = far_of(p) + plane_of(p - 2) + plane_of(p + 2)
    ring_5 = far_of(p - 1) + far_of(p + 1) + near_of(p - 2) + near_of(p + 2)
    layers = []
    for c in (0, 1, 2):
        total = None
        for square, ring in ((0, ring_0), (1, ring_1), (2, ring_2), (4, ring_4), (5, ring_5)):
            weight = tap(square + c * c)
            if weight > 0.0:
                total = weight * ring if total is None else total + weight * ring
        layers.append(total)
    middle, near, far = layers
    return middle + (rolled(near, 1, 1) + rolled(near, -1, 1)) + (rolled(far, 2, 1) + rolled(far, -2, 1))


def weights_kernel(support_ref, inverse_ref, edge_ref, volume_ref, mark_ref, near_ref, far_ref, *, extents):
    total_x, total_y, total_z = extents
    first_x = lax.axis_index("gx") * SX
    first_y = lax.axis_index("gy") * SY
    first_z = lax.axis_index("gz") * SZ
    row = lax.broadcasted_iota(jnp.int32, (ROWS, LANES), 0)
    lane = lax.broadcasted_iota(jnp.int32, (ROWS, LANES), 1)
    y = first_y + jnp.where(row < 12, row, row - ROWS)
    z = first_z + jnp.where(lane < SZ + SIDE // 2, lane, lane - LANES)
    inside = jnp.where((y >= 0) & (y < total_y) & (z >= 0) & (z < total_z), 1.0, 0.0).astype(F32)
    near, far = row_pairs(inside)

    def present(p):
        x = first_x + p
        return jnp.where((x >= 0) & (x < total_x), 1.0, 0.0).astype(F32)

    for p in range(ELEMENTS):
        x = p - 5
        weight_sum = filtered_plane(
            lambda q: inside * present(q), lambda q: near * present(q), lambda q: far * present(q), x
        )
        here = inside * present(x)
        inverse = jnp.where(here > 0.0, 1.0 / jnp.where(here > 0.0, weight_sum, 1.0), 0.0)
        inverse_ref[p] = inverse
        edge_ref[p] = jnp.concatenate([inverse[7:11], inverse[14:16], inverse[0:2]], axis=0)
        inverse_near, inverse_far = row_pairs(inverse)
        near_ref[p] = inverse_near[0:SY]
        far_ref[p] = inverse_far[0:SY]
    for p in range(CHOSEN):
        volume_ref[p] = filtered_plane(
            lambda q: inverse_ref[q, 0:SY], lambda q: near_ref[q], lambda q: far_ref[q], p + 2
        )
    node = support_ref[...]
    node_x = node // (total_y * total_z) - first_x
    node_y = node // total_z % total_y - first_y
    node_z = node % total_z - first_z
    owned = (node_x >= 0) & (node_x < SX) & (node_y >= 0) & (node_y < SY)
    line = jnp.where(owned, node_x * SY + node_y, -1)
    count = node.shape[1]
    lines = jnp.where(lax.broadcasted_iota(jnp.int32, (SX * SY, count), 0) == line, 1.0, 0.0)
    lanes = jnp.where(lax.broadcasted_iota(jnp.int32, (SZ, count), 0) == node_z, 1.0, 0.0)
    hits = lax.dot_general(
        lines.astype(jnp.bfloat16),
        lanes.astype(jnp.bfloat16),
        (((1,), (1,)), ((), ())),
        preferred_element_type=F32,
    )
    for p in range(SX):
        mark_ref[p] = hits[p * SY : (p + 1) * SY]


def is_first(axis):
    return (lax.axis_index(axis) + (axis == "gy")) % 2 == 0


def place_pair(even, first_ref, second_ref, top, bottom, place):
    first_ref[place] = jnp.where(even, top, bottom)
    second_ref[place] = jnp.where(even, bottom, top)


def low_high(axis, first_ref, second_ref, place):
    index, leads = lax.axis_index(axis), is_first(axis)
    first, second = first_ref[place], second_ref[place]
    low = jnp.where(index == 0, 0.0, jnp.where(leads, second, first))
    high = jnp.where(index == lax.axis_size(axis) - 1, 0.0, jnp.where(leads, first, second))
    return low, high


def row_place(index):
    if index < 3 * NODES:
        return slice(3 * index, 3 * index + 3)
    return slice(2 * index + 3 * NODES, 2 * index + 3 * NODES + 2)


def row_tile(first_ref, second_ref, place):
    low, high = low_high("gy", first_ref, second_ref, place)
    filler = jnp.zeros((SY - 2 * low.shape[0], low.shape[1]), F32)
    return jnp.concatenate([high, filler, low], axis=0)


def plane_reader(shift_ref, physical_ref, x_first, x_second):
    def read(index):
        f, x = index // NODES, index % NODES - 5
        if 0 <= x < SX:
            return shift_ref[f, x] if f < 3 else physical_ref[x]
        low, high = low_high("gx", x_first, x_second, (f, x + 5 if x < 0 else x - SX))
        return low if x < 0 else high

    return read


def design_reader(design_ref, passive_ref, x_first, x_second):
    def read(index):
        f, x = index // CHOSEN, index % CHOSEN - 3
        if 0 <= x < SX:
            return design_ref[x] if f == 0 else passive_ref[x].astype(F32)
        low, high = low_high("gx", x_first, x_second, (f, x + 3 if x < 0 else x - SX))
        return low if x < 0 else high

    return read


def near_half(plane):
    return jnp.where(lax.axis_index("gz") == 0, plane[:, SZ - SIDE :], plane[:, 0:SIDE])


def edge_tile(plane, low, high):
    missing = 3 - high.shape[0]
    filler = [jnp.zeros((missing, SZ), F32)] if missing else []
    return jnp.concatenate([plane[7:8], high, *filler, low[low.shape[0] - 2 :], plane[0:2]], axis=0)


def faces_y_kernel(shift_ref, physical_ref, x_first, x_second, first_ref, second_ref):
    even = is_first("gy")
    read = plane_reader(shift_ref, physical_ref, x_first, x_second)
    for index in range(4 * NODES):
        plane = read(index)
        rows = row_place(index)
        depth = rows.stop - rows.start
        place_pair(even, first_ref, second_ref, plane[SY - depth :], plane[0:depth], rows)


def faces_side_kernel(shift_ref, physical_ref, x_first, x_second, side_ref):
    read = plane_reader(shift_ref, physical_ref, x_first, x_second)
    for index in range(4 * NODES):
        side_ref[index] = near_half(read(index))


def faces_edge_kernel(
    shift_ref, physical_ref, x_first, x_second, y_first, y_second, design_ref, passive_ref, d_first, d_second,
    edge_ref, side_ref
):
    read = plane_reader(shift_ref, physical_ref, x_first, x_second)
    for index in range(4 * NODES):
        low, high = low_high("gy", y_first, y_second, row_place(index))
        tile = edge_tile(read(index), low, high)
        edge_ref[index] = tile
        side_ref[index] = near_half(tile)
    read = design_reader(design_ref, passive_ref, d_first, d_second)
    for index in range(2 * CHOSEN):
        side_ref[4 * NODES + index] = near_half(read(index))


def scaled_energy(ext_ref, read, side, inverse_of, out_ref, groups):
    lane = lax.broadcasted_iota(jnp.int32, (SY, SIDE), 1)
    start = lax.axis_index("gz") * (SIDE // 2)
    keep = (lane >= start) & (lane < start + SIDE // 2)
    for f in range(4):
        for p in range(NODES):
            index = NODES * f + p
            ext_ref[f, p, :, 0:SZ] = read(index)
            ext_ref[f, p, :, SZ:LANES] = jnp.where(keep, side[index], 0.0)
    scale = penalty * (1.0 - stiff_floor)

    @pl.loop(0, ELEMENTS, unroll=True)
    def _(p):
        modes = {}
        for d in range(3):
            here, above = ext_ref[d, p], ext_ref[d, p + 1]
            for a, along_x in enumerate((here + above, above - here)):
                beyond = rolled(along_x, 1, 0)
                for b, along_y in enumerate((along_x + beyond, beyond - along_x)):
                    next_lane = rolled(along_y, 1, 1)
                    for c, mode in enumerate((along_y + next_lane, next_lane - along_y)):
                        modes[3 * (4 * a + 2 * b + c) + d] = mode
        energy = None
        for coefficient, sums in groups:
            squares = None
            for members in sums:
                value = functools.reduce(lambda left, right: left + right, [modes[m] for m in members])
                squares = value * value if squares is None else squares + value * value
            squares = float(coefficient) * squares
            energy = squares if energy is None else energy + squares
        density = ext_ref[3, p]
        out_ref[p] = scale * density * density * energy * inverse_of(p)


def inner_kernel(shift_ref, physical_ref, x_first, x_second, side, inverse_ref, out_ref, ext_ref, *, groups):
    read = plane_reader(shift_ref, physical_ref, x_first, x_second)
    scaled_energy(ext_ref, read, side, lambda p: inverse_ref[p, 0:SY], out_ref, groups)


def design_kernel(
    design_ref, passive_ref, d_first, d_second, inner_ref, edge_tiles, edge_side, inverse_ref, edge_ref, volume_ref,
    out_ref, first_ref, second_ref, part_ref, ext_ref, outer_ref, sens_ref, near_ref, far_ref, high_ref, low_ref,
    value_ref, *, groups
):
    even = is_first("gy")
    scaled_energy(
        ext_ref, lambda index: edge_tiles[index], edge_side, lambda p: edge_ref[p], outer_ref, groups
    )
    row = lax.broadcasted_iota(jnp.int32, (SY, LANES), 0)
    for p in range(ELEMENTS):
        outer = outer_ref[p]
        own = jnp.where(row == 7, rolled(outer, -7, 0), inner_ref[p])
        beyond = jnp.where(row < 4, rolled(outer, 1, 0), rolled(outer, -2, 0))
        sens_ref[p] = own
        near, far = row_pairs(jnp.concatenate([own, beyond], axis=0))
        near_ref[p] = near[0:SY]
        far_ref[p] = far[0:SY]

    read_design = design_reader(design_ref, passive_ref, d_first, d_second)
    for p in range(CHOSEN):
        filtered = filtered_plane(lambda q: sens_ref[q], lambda q: near_ref[q], lambda q: far_ref[q], p + 2)
        index = 4 * NODES + p
        design = jnp.concatenate([read_design(p), edge_side[index]], axis=1)
        solid = jnp.concatenate([read_design(p + CHOSEN), edge_side[index + CHOSEN]], axis=1) > 0.5
        inside = inverse_ref[p + 2, 0:SY] > 0.0
        scaled = design * jnp.sqrt(filtered / jnp.where(inside, volume_ref[p], 1.0))
        floor_bound = jnp.where(solid, 1.0, jnp.maximum(0.0, design - move_limit))
        ceiling = jnp.where(solid, 1.0, jnp.minimum(1.0, design + move_limit))
        for f, value in enumerate((scaled, floor_bound, ceiling)):
            value = jnp.where(inside, value, 0.0)
            out_ref[f, p] = value
            row = 3 * (CHOSEN * f + p)
            place_pair(even, first_ref, second_ref, value[SY - 3 :], value[0:3], slice(row, row + 3))
    add_volumes(out_ref, volume_ref, part_ref, high_ref, low_ref, value_ref)


def three_parts(value):
    first = value.astype(jnp.bfloat16).astype(F32)
    second = (value - first).astype(jnp.bfloat16).astype(F32)
    return first, second, value - first - second


def add_volumes(bounds_ref, volume_ref, out_ref, high_ref, low_ref, value_ref):
    step = (log_upper - log_lower) / POINTS
    ceilings = jnp.zeros((SY, 128), F32)
    for v in range(2 * SX):
        place = (3 + v // 2, slice(None), slice(128 * (v % 2), 128 * (v % 2 + 1)))
        weight = volume_ref[place]
        scaled, floor_bound, ceiling = [bounds_ref[(f,) + place] for f in range(3)]
        ceilings = ceilings + weight * ceiling
        log_scaled = jnp.log(jnp.maximum(scaled, 1e-30))
        for t, bound in enumerate((ceiling, floor_bound)):
            reached = (2.0 * (log_scaled - jnp.log(jnp.maximum(bound, 1e-30))) - log_lower) / step
            index = jnp.minimum(jnp.maximum(jnp.ceil(reached), 1.0), POINTS + 1.0) - 1.0
            index = jnp.where(bound > 0.0, index, float(POINTS))
            high = jnp.floor(index * (1.0 / 128.0))
            high_ref[t, v] = high
            low_ref[t, v] = index - 128.0 * high
            sign = -1.0 if t == 0 else 1.0
            parts = three_parts(sign * weight * bound) + three_parts(-sign * weight * scaled)
            for n, part in enumerate(parts):
                value_ref[t, n, v] = part

    rows = lax.broadcasted_iota(jnp.int32, (8, 128), 0).astype(F32)
    columns = lax.broadcasted_iota(jnp.int32, (128, 128), 0).astype(F32).astype(jnp.bfloat16)

    def add_group(v, total):
        lefts, rights = [], []
        for t in range(2):
            for r in range(SY):
                hit = rows == high_ref[t, v, r : r + 1, :]
                left = [jnp.where(hit, value_ref[t, n, v, r : r + 1, :], 0.0) for n in range(6)]
                lefts.append(jnp.concatenate(left, axis=0).astype(jnp.bfloat16))
                low = jnp.broadcast_to(low_ref[t, v, r : r + 1, :], (16, 128)).astype(jnp.bfloat16)
                low = jnp.concatenate([low] * 8, axis=0)
                rights.append(jnp.where(columns == low, jnp.bfloat16(1.0), jnp.bfloat16(0.0)))
        return total + lax.dot_general(
            jnp.concatenate(rights, axis=1),
            jnp.concatenate(lefts, axis=1),
            (((1,), (1,)), ((), ())),
            preferred_element_type=F32,
        )

    total = lax.fori_loop(0, 2 * SX, add_group, jnp.zeros((128, 48), F32), unroll=8).T
    constant = total[0:8] + total[8:16] + total[16:24]
    slope = total[24:32] + total[32:40] + total[40:48]
    upto = jnp.where(
        lax.broadcasted_iota(jnp.int32, (128, 128), 0) <= lax.broadcasted_iota(jnp.int32, (128, 128), 1), 1.0, 0.0
    )
    running = lax.dot_general(
        jnp.concatenate([constant, slope], axis=0),
        upto,
        (((1,), (0,)), ((), ())),
        precision=lax.Precision.HIGHEST,
        preferred_element_type=F32,
    )
    row = lax.broadcasted_iota(jnp.int32, (8, 128), 0)
    lane = lax.broadcasted_iota(jnp.int32, (8, 128), 1)
    cumulated = []
    for part in (running[0:8], running[8:16]):
        ends = jnp.broadcast_to(part[:, 127:128], (8, 128))
        before = ends
        for shift in (1, 2, 4):
            before = before + jnp.where(row >= shift, rolled(before, -shift, 0), 0.0)
        cumulated.append(part + (before - ends))
    index = (row * 128 + lane + 1).astype(F32)
    factor = jnp.exp(-0.5 * (log_lower + step * index))
    result = jnp.sum(ceilings) + cumulated[0] + factor * cumulated[1]
    for i in range(out_ref.shape[0]):
        out_ref[i] = result


def repeat_kernel(part_ref, out_ref):
    total = part_ref[0]
    for i in range(1, part_ref.shape[0]):
        total = total + part_ref[i]
    for i in range(out_ref.shape[0]):
        out_ref[i] = total


def final_kernel(
    part_ref, own_ref, y_first, y_second, inverse_ref, mark_ref, new_design_ref, new_physical_ref,
    blocks_ref, chosen_ref, near_ref, far_ref, stiff_ref, *, factors, target
):
    total = part_ref[0]
    for i in range(1, part_ref.shape[0]):
        total = total + part_ref[i]
    low_end = jnp.minimum(jnp.sum(jnp.where(total > target, 1.0, 0.0)), POINTS - 1.0)
    multiplier = log_lower + (log_upper - log_lower) / POINTS * (low_end + 0.5)
    factor = jnp.exp(jnp.broadcast_to(-0.5 * multiplier, (SY, LANES)))
    for p in range(CHOSEN):
        tiles = []
        own = [own_ref[f, p] for f in range(3)]
        beside = []
        for f in range(3):
            row = 3 * (CHOSEN * f + p)
            beside.append(row_tile(y_first, y_second, slice(row, row + 3)))
        for scaled, floor_bound, ceiling in (own, beside):
            tiles.append(jnp.minimum(jnp.maximum(scaled * factor, floor_bound), ceiling))
        chosen = jnp.concatenate(tiles, axis=0)
        chosen_ref[p] = chosen
        near, far = row_pairs(chosen)
        near_ref[p] = near
        far_ref[p] = far
        if 3 <= p < SX + 3:
            new_design_ref[p - 3] = tiles[0][:, 0:SZ]
    for p in range(SX + 1):
        inverse = inverse_ref[p + 4]
        density = (
            filtered_plane(lambda q: chosen_ref[q], lambda q: near_ref[q], lambda q: far_ref[q], p + 2) * inverse
        )
        if p >= 1:
            new_physical_ref[p - 1] = density[0:SY, 0:SZ]
        cube = stiff_floor + density * density * density * (1.0 - stiff_floor)
        stiff_ref[p] = jnp.where(inverse > 0.0, cube, 0.0)
    for p in range(SX):
        below, here = stiff_ref[p], stiff_ref[p + 1]
        x_sum, x_diff = here + below, below - here
        x_sum_back, x_diff_back = rolled(x_sum, -1, 0), rolled(x_diff, -1, 0)
        sum_sum = (x_sum + x_sum_back)[0:SY]
        sum_diff = (x_sum_back - x_sum)[0:SY]
        diff_sum = (x_diff + x_diff_back)[0:SY]
        diff_diff = (x_diff_back - x_diff)[0:SY]
        marked = mark_ref[p] > 0.5
        even = factors[0] * (sum_sum + rolled(sum_sum, -1, 1))[:, 0:SZ]
        even = jnp.where(marked, 1.0, even)
        blocks_ref[0, p] = even
        blocks_ref[1, p] = even
        blocks_ref[2, p] = even
        yz = factors[1] * (rolled(sum_diff, -1, 1) - sum_diff)[:, 0:SZ]
        xz = factors[2] * (rolled(diff_sum, -1, 1) - diff_sum)[:, 0:SZ]
        xy = factors[3] * (diff_diff + rolled(diff_diff, -1, 1))[:, 0:SZ]
        blocks_ref[3, p] = jnp.where(marked, 0.0, yz)
        blocks_ref[4, p] = jnp.where(marked, 0.0, xz)
        blocks_ref[5, p] = jnp.where(marked, 0.0, xy)


def call(kernel, inputs, shapes, scratch, flops, spaces=None, grant=32):
    outs = [jax.ShapeDtypeStruct(shape, F32) for shape in shapes]
    return pl.pallas_call(
        kernel,
        out_shape=outs,
        in_specs=[pl.BlockSpec(memory_space=space) for space in spaces or [pltpu.VMEM] * len(inputs)],
        out_specs=[pl.BlockSpec(memory_space=pltpu.VMEM)] * len(outs),
        scratch_shapes=[pltpu.VMEM(shape, F32) if isinstance(shape, tuple) else shape for shape in scratch],
        compiler_params=pltpu.CompilerParams(vmem_limit_bytes=grant * 2**20),
        cost_estimate=pl.CostEstimate(flops=flops, bytes_accessed=min(flops, 10**6), transcendentals=0),
    )(*inputs)


def exchange(first, second, axis):
    count = lax.axis_size(axis)
    results = []
    for start, faces in enumerate((first, second)):
        pairs = [(i, (i + 1) % count) for i in range((start + (axis == "gy")) % 2, count, 2)]
        results.append(lax.ppermute(faces, axis, pairs + [(j, i) for i, j in pairs]))
    return results


def other_core(values):
    return lax.ppermute(values, "gz", [(0, 1), (1, 0)])


def body(displacement, physical, design, passive, supports):
    assert design.shape == (SX, SY, SZ) and lax.axis_size("gz") == 2
    sizes = [lax.axis_size(axis) for axis in ("gx", "gy", "gz")]
    extents = (SX * sizes[0], SY * sizes[1], SZ * sizes[2])
    block = (SX, SY, SZ)
    even = is_first("gx")

    def swaps(fields, depth):
        top, bottom = fields[:, SX - depth :], fields[:, 0:depth]
        return jnp.where(even, top, bottom), jnp.where(even, bottom, top)

    x_faces = exchange(*swaps(jnp.concatenate([displacement, physical[None]], axis=0), 5), "gx")
    frame = (ELEMENTS, ROWS, LANES)
    own_frame = (ELEMENTS, SY, LANES)
    weights = call(
        functools.partial(weights_kernel, extents=extents), (supports.reshape(1, -1),),
        [frame, own_frame, (CHOSEN, SY, LANES), block], [own_frame, own_frame], 10**7,
    )
    design_faces = swaps(jnp.stack([design, passive.astype(F32)]), 3)
    x_faces, design_faces, (inverse, edge, volume_weight, marks) = lax.optimization_barrier(
        (x_faces, design_faces, weights)
    )

    groups = energy_groups()
    faces = (11 * NODES, SZ)
    tiles = (4 * NODES, SY, SZ)
    ext = (4, NODES, SY, LANES)
    y_faces = call(faces_y_kernel, (displacement, physical, *x_faces), [faces, faces], [], 10**6)
    y_faces, x_faces, design_faces = lax.optimization_barrier((y_faces, x_faces, design_faces))
    y_faces = exchange(*y_faces, "gy")
    design_faces = exchange(*design_faces, "gx")
    (side,) = call(faces_side_kernel, (displacement, physical, *x_faces), [(4 * NODES, SY, SIDE)], [], 1)
    (inner_part,) = call(
        functools.partial(inner_kernel, groups=groups),
        (displacement, physical, *x_faces, other_core(side), inverse), [own_frame], [ext], 1,
    )
    y_faces, inner_part = lax.optimization_barrier((y_faces, inner_part))
    edge_tiles, side = call(
        faces_edge_kernel, (displacement, physical, *x_faces, *y_faces, design, passive, *design_faces),
        [tiles, (4 * NODES + 2 * CHOSEN, SY, SIDE)], [], 10**6,
    )
    side = other_core(side)

    faces = (9 * CHOSEN, LANES)
    inner, outer = sizes[1] * sizes[2], sizes[0]
    elements = (2 * SX, SY, 128)
    bounds, *y_bounds, part = call(
        functools.partial(design_kernel, groups=groups),
        (design, passive, *design_faces, inner_part, edge_tiles, side, inverse, edge, volume_weight),
        [(3, CHOSEN, SY, LANES), faces, faces, (inner, 8, 128)],
        [ext, own_frame, own_frame, own_frame, own_frame]
        + [(2,) + elements, (2,) + elements, (2, 6) + elements], 10**7,
    )

    part = lax.all_to_all(part, ("gy", "gz"), 0, 0, tiled=True)
    y_bounds, part = lax.optimization_barrier((y_bounds, part))
    y_bounds = exchange(*y_bounds, "gy")
    (part,) = call(repeat_kernel, (part,), [(outer, 8, 128)], [], 10**5)
    part = lax.all_to_all(part, "gx", 0, 0, tiled=True)

    chosen = (CHOSEN, ROWS, LANES)
    target = volume_share * (extents[0] * extents[1] * extents[2])
    new_design, new_physical, node_blocks = call(
        functools.partial(final_kernel, factors=[float(f) for f in corner_factors()], target=target),
        (part, bounds, *y_bounds, inverse, marks), [block, block, (6,) + block],
        [chosen, chosen, chosen, (SX + 1, ROWS, LANES)], 10**7,
    )
    return (new_design, new_physical, node_blocks)


def solution(mesh):
    in_specs = (
        P(None, "gx", "gy", "gz"),
        P("gx", "gy", "gz"),
        P("gx", "gy", "gz"),
        P("gx", "gy", "gz"),
        P(),
    )
    out_specs = (P("gx", "gy", "gz"), P("gx", "gy", "gz"), P(None, "gx", "gy", "gz"))
    return jax.shard_map(body, mesh=mesh, in_specs=in_specs, out_specs=out_specs, check_vma=False)
```

```python
import functools
import math

import jax
import jax.numpy as jnp
import numpy as np
from jax import lax
from jax.experimental import pallas as pl
from jax.experimental.pallas import tpu as pltpu
from jax.sharding import PartitionSpec as P

STEPS = 10

filter_radius = 2.5
penalty = 3.0
move_limit = 0.2
stiff_floor = 1e-09
volume_share = 0.5
log_lower = -20.0
log_upper = 20.0
poisson = 0.3

SX, SY, SZ = 8, 8, 256
ROWS, LANES, SIDE = 16, 384, 128
NODES, ELEMENTS, CHOSEN = SX + 10, SX + 9, SX + 5
POINTS = 2**STEPS
F32 = jnp.float32


def corner_offsets():
    return [(q // 4, q // 2 % 2, q % 2) for q in range(8)]


def hex_stiffness():
    lame_first = poisson / ((1.0 + poisson) * (1.0 - 2.0 * poisson))
    shear_modulus = 0.5 / (1.0 + poisson)
    elastic = np.zeros((6, 6))
    elastic[:3, :3] = lame_first
    for d in range(3):
        elastic[d, d] += 2.0 * shear_modulus
        elastic[d + 3, d + 3] = shear_modulus
    corners = corner_offsets()
    points = [0.5 - 0.5 / math.sqrt(3.0), 0.5 + 0.5 / math.sqrt(3.0)]
    matrix = np.zeros((24, 24))
    for p in points:
        for q in points:
            for r in points:
                location = [p, q, r]
                gradients = np.zeros((8, 3))
                for n in range(8):
                    factors = [
                        location[e] if corners[n][e] == 1 else 1.0 - location[e] for e in range(3)
                    ]
                    for d in range(3):
                        sign_value = 1.0 if corners[n][d] == 1 else -1.0
                        gradients[n, d] = sign_value * factors[(d + 1) % 3] * factors[(d + 2) % 3]
                strain = np.zeros((6, 24))
                for n in range(8):
                    column = 3 * n
                    strain[0, column] = gradients[n, 0]
                    strain[1, column + 1] = gradients[n, 1]
                    strain[2, column + 2] = gradients[n, 2]
                    strain[3, column + 1] = gradients[n, 2]
                    strain[3, column + 2] = gradients[n, 1]
                    strain[4, column] = gradients[n, 2]
                    strain[4, column + 2] = gradients[n, 0]
                    strain[5, column] = gradients[n, 1]
                    strain[5, column + 1] = gradients[n, 0]
                matrix += strain.T @ elastic @ strain / 8.0
    return matrix


def energy_groups():
    corners = corner_offsets()
    modes = np.zeros((24, 24))
    for s in range(8):
        bits = (s // 4, s // 2 % 2, s % 2)
        for n in range(8):
            sign_value = 1.0
            for e in range(3):
                if bits[e] == 1 and corners[n][e] == 0:
                    sign_value = -sign_value
            for d in range(3):
                modes[3 * n + d, 3 * s + d] = sign_value
    form = modes.T @ hex_stiffness() @ modes / 64.0
    groups = []

    def add(coefficient, members):
        if abs(coefficient) < 1e-9:
            return
        for group in groups:
            if abs(group[0] - coefficient) < 1e-9:
                group[1].append(members)
                return
        groups.append((coefficient, [members]))

    for parity in range(8):
        left = [3 * (parity ^ (4, 2, 1)[d]) + d for d in range(3)]
        while left:
            first = left[0]
            block = [m for m in left if m == first or abs(form[first, m]) > 1e-9]
            left = [m for m in left if m not in block]
            beside = form[block[0], block[1]] if len(block) > 1 else 0.0
            add(beside, block)
            for m in block:
                add(form[m, m] - beside, [m])
    rebuilt = np.zeros((24, 24))
    for coefficient, sums in groups:
        for members in sums:
            rebuilt[np.ix_(members, members)] += coefficient
    assert np.abs(rebuilt - form).max() < 1e-9
    return groups


def corner_factors():
    matrix = hex_stiffness()
    factors = (matrix[0, 0], matrix[1, 2], matrix[0, 2], matrix[0, 1])
    for n, corner in enumerate(corner_offsets()):
        sign = [1.0 if c == 1 else -1.0 for c in corner]
        block = matrix[3 * n : 3 * n + 3, 3 * n : 3 * n + 3]
        assert np.allclose(np.diag(block), factors[0])
        assert np.allclose(block[1, 2], factors[1] * sign[1] * sign[2])
        assert np.allclose(block[0, 2], factors[2] * sign[0] * sign[2])
        assert np.allclose(block[0, 1], factors[3] * sign[0] * sign[1])
    return factors


def tap(square):
    return max(0.0, filter_radius - math.sqrt(square))


def rolled(value, steps, dim):
    return pltpu.roll(value, (-steps) % value.shape[dim], dim)


def row_pairs(plane):
    return (
        rolled(plane, 1, 0) + rolled(plane, -1, 0),
        rolled(plane, 2, 0) + rolled(plane, -2, 0),
    )


def filtered_plane(plane_of, near_of, far_of, p):
    ring_0 = plane_of(p)
    ring_1 = near_of(p) + plane_of(p - 1) + plane_of(p + 1)
    ring_2 = near_of(p - 1) + near_of(p + 1)
    ring_4 = far_of(p) + plane_of(p - 2) + plane_of(p + 2)
    ring_5 = far_of(p - 1) + far_of(p + 1) + near_of(p - 2) + near_of(p + 2)
    layers = []
    for c in (0, 1, 2):
        total = None
        for square, ring in ((0, ring_0), (1, ring_1), (2, ring_2), (4, ring_4), (5, ring_5)):
            weight = tap(square + c * c)
            if weight > 0.0:
                total = weight * ring if total is None else total + weight * ring
        layers.append(total)
    middle, near, far = layers
    return middle + (rolled(near, 1, 1) + rolled(near, -1, 1)) + (rolled(far, 2, 1) + rolled(far, -2, 1))


def weights_kernel(support_ref, inverse_ref, edge_ref, volume_ref, mark_ref, near_ref, far_ref, *, extents):
    total_x, total_y, total_z = extents
    first_x = lax.axis_index("gx") * SX
    first_y = lax.axis_index("gy") * SY
    first_z = lax.axis_index("gz") * SZ
    row = lax.broadcasted_iota(jnp.int32, (ROWS, LANES), 0)
    lane = lax.broadcasted_iota(jnp.int32, (ROWS, LANES), 1)
    y = first_y + jnp.where(row < 12, row, row - ROWS)
    z = first_z + jnp.where(lane < SZ + SIDE // 2, lane, lane - LANES)
    inside = jnp.where((y >= 0) & (y < total_y) & (z >= 0) & (z < total_z), 1.0, 0.0).astype(F32)
    near, far = row_pairs(inside)

    def present(p):
        x = first_x + p
        return jnp.where((x >= 0) & (x < total_x), 1.0, 0.0).astype(F32)

    for p in range(ELEMENTS):
        x = p - 5
        weight_sum = filtered_plane(
            lambda q: inside * present(q), lambda q: near * present(q), lambda q: far * present(q), x
        )
        here = inside * present(x)
        inverse = jnp.where(here > 0.0, 1.0 / jnp.where(here > 0.0, weight_sum, 1.0), 0.0)
        inverse_ref[p] = inverse
        edge_ref[p] = jnp.concatenate([inverse[7:11], inverse[14:16], inverse[0:2]], axis=0)
        inverse_near, inverse_far = row_pairs(inverse)
        near_ref[p] = inverse_near[0:SY]
        far_ref[p] = inverse_far[0:SY]
    for p in range(CHOSEN):
        volume_ref[p] = filtered_plane(
            lambda q: inverse_ref[q, 0:SY], lambda q: near_ref[q], lambda q: far_ref[q], p + 2
        )
    node = support_ref[...]
    node_x = node // (total_y * total_z) - first_x
    node_y = node // total_z % total_y - first_y
    node_z = node % total_z - first_z
    owned = (node_x >= 0) & (node_x < SX) & (node_y >= 0) & (node_y < SY)
    line = jnp.where(owned, node_x * SY + node_y, -1)
    count = node.shape[1]
    lines = jnp.where(lax.broadcasted_iota(jnp.int32, (SX * SY, count), 0) == line, 1.0, 0.0)
    lanes = jnp.where(lax.broadcasted_iota(jnp.int32, (SZ, count), 0) == node_z, 1.0, 0.0)
    hits = lax.dot_general(
        lines.astype(jnp.bfloat16),
        lanes.astype(jnp.bfloat16),
        (((1,), (1,)), ((), ())),
        preferred_element_type=F32,
    )
    for p in range(SX):
        mark_ref[p] = hits[p * SY : (p + 1) * SY]


def is_even(axis):
    return lax.axis_index(axis) % 2 == 0


def place_pair(even, first_ref, second_ref, top, bottom, place):
    first_ref[place] = jnp.where(even, top, bottom)
    second_ref[place] = jnp.where(even, bottom, top)


def low_high(axis, first_ref, second_ref, place):
    index = lax.axis_index(axis)
    first, second = first_ref[place], second_ref[place]
    low = jnp.where(index == 0, 0.0, jnp.where(index % 2 == 0, second, first))
    high = jnp.where(index == lax.axis_size(axis) - 1, 0.0, jnp.where(index % 2 == 0, first, second))
    return low, high


def row_place(index):
    if index < 3 * NODES:
        return slice(3 * index, 3 * index + 3)
    return slice(2 * index + 3 * NODES, 2 * index + 3 * NODES + 2)


def row_tile(first_ref, second_ref, place):
    low, high = low_high("gy", first_ref, second_ref, place)
    filler = jnp.zeros((SY - 2 * low.shape[0], low.shape[1]), F32)
    return jnp.concatenate([high, filler, low], axis=0)


def plane_reader(shift_ref, physical_ref, x_first, x_second):
    def read(index):
        f, x = index // NODES, index % NODES - 5
        if 0 <= x < SX:
            return shift_ref[f, x] if f < 3 else physical_ref[x]
        low, high = low_high("gx", x_first, x_second, (f, x + 5 if x < 0 else x - SX))
        return low if x < 0 else high

    return read


def design_reader(design_ref, passive_ref, x_first, x_second):
    def read(index):
        f, x = index // CHOSEN, index % CHOSEN - 3
        if 0 <= x < SX:
            return design_ref[x] if f == 0 else passive_ref[x].astype(F32)
        low, high = low_high("gx", x_first, x_second, (f, x + 3 if x < 0 else x - SX))
        return low if x < 0 else high

    return read


def near_half(plane):
    return jnp.where(lax.axis_index("gz") == 0, plane[:, SZ - SIDE :], plane[:, 0:SIDE])


def edge_tile(plane, low, high):
    missing = 3 - high.shape[0]
    filler = [jnp.zeros((missing, SZ), F32)] if missing else []
    return jnp.concatenate([plane[7:8], high, *filler, low[low.shape[0] - 2 :], plane[0:2]], axis=0)


def faces_y_kernel(shift_ref, physical_ref, x_first, x_second, first_ref, second_ref):
    even = is_even("gy")
    read = plane_reader(shift_ref, physical_ref, x_first, x_second)
    for index in range(4 * NODES):
        plane = read(index)
        rows = row_place(index)
        depth = rows.stop - rows.start
        place_pair(even, first_ref, second_ref, plane[SY - depth :], plane[0:depth], rows)


def faces_side_kernel(shift_ref, physical_ref, x_first, x_second, side_ref):
    read = plane_reader(shift_ref, physical_ref, x_first, x_second)
    for index in range(4 * NODES):
        side_ref[index] = near_half(read(index))


def faces_edge_kernel(
    shift_ref, physical_ref, x_first, x_second, y_first, y_second, design_ref, passive_ref, d_first, d_second,
    edge_ref, side_ref
):
    read = plane_reader(shift_ref, physical_ref, x_first, x_second)
    for index in range(4 * NODES):
        low, high = low_high("gy", y_first, y_second, row_place(index))
        tile = edge_tile(read(index), low, high)
        edge_ref[index] = tile
        side_ref[index] = near_half(tile)
    read = design_reader(design_ref, passive_ref, d_first, d_second)
    for index in range(2 * CHOSEN):
        side_ref[4 * NODES + index] = near_half(read(index))


def scaled_energy(ext_ref, read, side, inverse_of, out_ref, groups):
    lane = lax.broadcasted_iota(jnp.int32, (SY, SIDE), 1)
    start = lax.axis_index("gz") * (SIDE // 2)
    keep = (lane >= start) & (lane < start + SIDE // 2)
    for f in range(4):
        for p in range(NODES):
            index = NODES * f + p
            ext_ref[f, p, :, 0:SZ] = read(index)
            ext_ref[f, p, :, SZ:LANES] = jnp.where(keep, side[index], 0.0)
    scale = penalty * (1.0 - stiff_floor)

    @pl.loop(0, ELEMENTS, unroll=True)
    def _(p):
        modes = {}
        for d in range(3):
            here, above = ext_ref[d, p], ext_ref[d, p + 1]
            for a, along_x in enumerate((here + above, above - here)):
                beyond = rolled(along_x, 1, 0)
                for b, along_y in enumerate((along_x + beyond, beyond - along_x)):
                    next_lane = rolled(along_y, 1, 1)
                    for c, mode in enumerate((along_y + next_lane, next_lane - along_y)):
                        modes[3 * (4 * a + 2 * b + c) + d] = mode
        energy = None
        for coefficient, sums in groups:
            squares = None
            for members in sums:
                value = functools.reduce(lambda left, right: left + right, [modes[m] for m in members])
                squares = value * value if squares is None else squares + value * value
            squares = float(coefficient) * squares
            energy = squares if energy is None else energy + squares
        density = ext_ref[3, p]
        out_ref[p] = scale * density * density * energy * inverse_of(p)


def inner_kernel(shift_ref, physical_ref, x_first, x_second, side, inverse_ref, out_ref, ext_ref, *, groups):
    read = plane_reader(shift_ref, physical_ref, x_first, x_second)
    scaled_energy(ext_ref, read, side, lambda p: inverse_ref[p, 0:SY], out_ref, groups)


def design_kernel(
    design_ref, passive_ref, d_first, d_second, inner_ref, edge_tiles, edge_side, inverse_ref, edge_ref, volume_ref,
    out_ref, first_ref, second_ref, part_ref, ext_ref, outer_ref, sens_ref, near_ref, far_ref, high_ref, low_ref,
    value_ref, *, groups
):
    even = is_even("gy")
    scaled_energy(
        ext_ref, lambda index: edge_tiles[index], edge_side, lambda p: edge_ref[p], outer_ref, groups
    )
    row = lax.broadcasted_iota(jnp.int32, (SY, LANES), 0)
    for p in range(ELEMENTS):
        outer = outer_ref[p]
        own = jnp.where(row == 7, rolled(outer, -7, 0), inner_ref[p])
        beyond = jnp.where(row < 4, rolled(outer, 1, 0), rolled(outer, -2, 0))
        sens_ref[p] = own
        near, far = row_pairs(jnp.concatenate([own, beyond], axis=0))
        near_ref[p] = near[0:SY]
        far_ref[p] = far[0:SY]

    read_design = design_reader(design_ref, passive_ref, d_first, d_second)
    for p in range(CHOSEN):
        filtered = filtered_plane(lambda q: sens_ref[q], lambda q: near_ref[q], lambda q: far_ref[q], p + 2)
        index = 4 * NODES + p
        design = jnp.concatenate([read_design(p), edge_side[index]], axis=1)
        solid = jnp.concatenate([read_design(p + CHOSEN), edge_side[index + CHOSEN]], axis=1) > 0.5
        inside = inverse_ref[p + 2, 0:SY] > 0.0
        scaled = design * jnp.sqrt(filtered / jnp.where(inside, volume_ref[p], 1.0))
        floor_bound = jnp.where(solid, 1.0, jnp.maximum(0.0, design - move_limit))
        ceiling = jnp.where(solid, 1.0, jnp.minimum(1.0, design + move_limit))
        for f, value in enumerate((scaled, floor_bound, ceiling)):
            value = jnp.where(inside, value, 0.0)
            out_ref[f, p] = value
            row = 3 * (CHOSEN * f + p)
            place_pair(even, first_ref, second_ref, value[SY - 3 :], value[0:3], slice(row, row + 3))
    add_volumes(out_ref, volume_ref, part_ref, high_ref, low_ref, value_ref)


def three_parts(value):
    first = value.astype(jnp.bfloat16).astype(F32)
    second = (value - first).astype(jnp.bfloat16).astype(F32)
    return first, second, value - first - second


def add_volumes(bounds_ref, volume_ref, out_ref, high_ref, low_ref, value_ref):
    step = (log_upper - log_lower) / POINTS
    ceilings = jnp.zeros((SY, 128), F32)
    for v in range(2 * SX):
        place = (3 + v // 2, slice(None), slice(128 * (v % 2), 128 * (v % 2 + 1)))
        weight = volume_ref[place]
        scaled, floor_bound, ceiling = [bounds_ref[(f,) + place] for f in range(3)]
        ceilings = ceilings + weight * ceiling
        log_scaled = jnp.log(jnp.maximum(scaled, 1e-30))
        for t, bound in enumerate((ceiling, floor_bound)):
            reached = (2.0 * (log_scaled - jnp.log(jnp.maximum(bound, 1e-30))) - log_lower) / step
            index = jnp.minimum(jnp.maximum(jnp.ceil(reached), 1.0), POINTS + 1.0) - 1.0
            index = jnp.where(bound > 0.0, index, float(POINTS))
            high = jnp.floor(index * (1.0 / 128.0))
            high_ref[t, v] = high
            low_ref[t, v] = index - 128.0 * high
            sign = -1.0 if t == 0 else 1.0
            parts = three_parts(sign * weight * bound) + three_parts(-sign * weight * scaled)
            for n, part in enumerate(parts):
                value_ref[t, n, v] = part

    rows = lax.broadcasted_iota(jnp.int32, (8, 128), 0).astype(F32)
    columns = lax.broadcasted_iota(jnp.int32, (128, 128), 0).astype(F32).astype(jnp.bfloat16)

    def add_group(v, total):
        lefts, rights = [], []
        for r in range(SY):
            left, right = [], []
            for t in range(2):
                hit = rows == high_ref[t, v, r : r + 1, :]
                left += [jnp.where(hit, value_ref[t, n, v, r : r + 1, :], 0.0) for n in range(6)]
                low = jnp.broadcast_to(low_ref[t, v, r : r + 1, :], (16, 128)).astype(jnp.bfloat16)
                low = jnp.concatenate([low] * 8, axis=0)
                right.append(jnp.where(columns == low, jnp.bfloat16(1.0), jnp.bfloat16(0.0)))
            lefts.append(jnp.concatenate(left, axis=0).astype(jnp.bfloat16))
            rights.append(jnp.concatenate(right, axis=0))
        return total + lax.dot_general(
            jnp.concatenate(rights, axis=1),
            jnp.concatenate(lefts, axis=1),
            (((1,), (1,)), ((), ())),
            preferred_element_type=F32,
        )

    total = lax.fori_loop(0, 2 * SX, add_group, jnp.zeros((256, 96), F32), unroll=8)
    total = (total[0:128, 0:48] + total[128:256, 48:96]).T
    constant = total[0:8] + total[8:16] + total[16:24]
    slope = total[24:32] + total[32:40] + total[40:48]
    upto = jnp.where(
        lax.broadcasted_iota(jnp.int32, (128, 128), 0) <= lax.broadcasted_iota(jnp.int32, (128, 128), 1), 1.0, 0.0
    )
    running = lax.dot_general(
        jnp.concatenate([constant, slope], axis=0),
        upto,
        (((1,), (0,)), ((), ())),
        precision=lax.Precision.HIGHEST,
        preferred_element_type=F32,
    )
    row = lax.broadcasted_iota(jnp.int32, (8, 128), 0)
    lane = lax.broadcasted_iota(jnp.int32, (8, 128), 1)
    cumulated = []
    for part in (running[0:8], running[8:16]):
        ends = jnp.broadcast_to(part[:, 127:128], (8, 128))
        before = ends
        for shift in (1, 2, 4):
            before = before + jnp.where(row >= shift, rolled(before, -shift, 0), 0.0)
        cumulated.append(part + (before - ends))
    index = (row * 128 + lane + 1).astype(F32)
    factor = jnp.exp(-0.5 * (log_lower + step * index))
    result = jnp.sum(ceilings) + cumulated[0] + factor * cumulated[1]
    for i in range(out_ref.shape[0]):
        out_ref[i] = result


def repeat_kernel(part_ref, out_ref):
    total = part_ref[0]
    for i in range(1, part_ref.shape[0]):
        total = total + part_ref[i]
    for i in range(out_ref.shape[0]):
        out_ref[i] = total


def final_kernel(
    part_ref, own_ref, y_first, y_second, inverse_ref, mark_ref, new_design_ref, new_physical_ref,
    blocks_ref, chosen_ref, near_ref, far_ref, stiff_ref, *, factors, target
):
    total = part_ref[0]
    for i in range(1, part_ref.shape[0]):
        total = total + part_ref[i]
    low_end = jnp.minimum(jnp.sum(jnp.where(total > target, 1.0, 0.0)), POINTS - 1.0)
    multiplier = log_lower + (log_upper - log_lower) / POINTS * (low_end + 0.5)
    factor = jnp.exp(jnp.broadcast_to(-0.5 * multiplier, (SY, LANES)))
    for p in range(CHOSEN):
        tiles = []
        own = [own_ref[f, p] for f in range(3)]
        beside = []
        for f in range(3):
            row = 3 * (CHOSEN * f + p)
            beside.append(row_tile(y_first, y_second, slice(row, row + 3)))
        for scaled, floor_bound, ceiling in (own, beside):
            tiles.append(jnp.minimum(jnp.maximum(scaled * factor, floor_bound), ceiling))
        chosen = jnp.concatenate(tiles, axis=0)
        chosen_ref[p] = chosen
        near, far = row_pairs(chosen)
        near_ref[p] = near
        far_ref[p] = far
        if 3 <= p < SX + 3:
            new_design_ref[p - 3] = tiles[0][:, 0:SZ]
    for p in range(SX + 1):
        inverse = inverse_ref[p + 4]
        density = (
            filtered_plane(lambda q: chosen_ref[q], lambda q: near_ref[q], lambda q: far_ref[q], p + 2) * inverse
        )
        if p >= 1:
            new_physical_ref[p - 1] = density[0:SY, 0:SZ]
        cube = stiff_floor + density * density * density * (1.0 - stiff_floor)
        stiff_ref[p] = jnp.where(inverse > 0.0, cube, 0.0)
    for p in range(SX):
        below, here = stiff_ref[p], stiff_ref[p + 1]
        x_sum, x_diff = here + below, below - here
        x_sum_back, x_diff_back = rolled(x_sum, -1, 0), rolled(x_diff, -1, 0)
        sum_sum = (x_sum + x_sum_back)[0:SY]
        sum_diff = (x_sum_back - x_sum)[0:SY]
        diff_sum = (x_diff + x_diff_back)[0:SY]
        diff_diff = (x_diff_back - x_diff)[0:SY]
        marked = mark_ref[p] > 0.5
        even = factors[0] * (sum_sum + rolled(sum_sum, -1, 1))[:, 0:SZ]
        even = jnp.where(marked, 1.0, even)
        blocks_ref[0, p] = even
        blocks_ref[1, p] = even
        blocks_ref[2, p] = even
        yz = factors[1] * (rolled(sum_diff, -1, 1) - sum_diff)[:, 0:SZ]
        xz = factors[2] * (rolled(diff_sum, -1, 1) - diff_sum)[:, 0:SZ]
        xy = factors[3] * (diff_diff + rolled(diff_diff, -1, 1))[:, 0:SZ]
        blocks_ref[3, p] = jnp.where(marked, 0.0, yz)
        blocks_ref[4, p] = jnp.where(marked, 0.0, xz)
        blocks_ref[5, p] = jnp.where(marked, 0.0, xy)


def call(kernel, inputs, shapes, scratch, flops, spaces=None, grant=32):
    outs = [jax.ShapeDtypeStruct(shape, F32) for shape in shapes]
    return pl.pallas_call(
        kernel,
        out_shape=outs,
        in_specs=[pl.BlockSpec(memory_space=space) for space in spaces or [pltpu.VMEM] * len(inputs)],
        out_specs=[pl.BlockSpec(memory_space=pltpu.VMEM)] * len(outs),
        scratch_shapes=[pltpu.VMEM(shape, F32) if isinstance(shape, tuple) else shape for shape in scratch],
        compiler_params=pltpu.CompilerParams(vmem_limit_bytes=grant * 2**20),
        cost_estimate=pl.CostEstimate(flops=flops, bytes_accessed=min(flops, 10**6), transcendentals=0),
    )(*inputs)


def exchange(first, second, axis):
    count = lax.axis_size(axis)
    results = []
    for start, faces in enumerate((first, second)):
        pairs = [(i, (i + 1) % count) for i in range(start, count, 2)]
        results.append(lax.ppermute(faces, axis, pairs + [(j, i) for i, j in pairs]))
    return results


def other_core(values):
    return lax.ppermute(values, "gz", [(0, 1), (1, 0)])


def body(displacement, physical, design, passive, supports):
    assert design.shape == (SX, SY, SZ) and lax.axis_size("gz") == 2
    sizes = [lax.axis_size(axis) for axis in ("gx", "gy", "gz")]
    extents = (SX * sizes[0], SY * sizes[1], SZ * sizes[2])
    block = (SX, SY, SZ)
    even = lax.axis_index("gx") % 2 == 0

    def swaps(fields, depth):
        top, bottom = fields[:, SX - depth :], fields[:, 0:depth]
        return jnp.where(even, top, bottom), jnp.where(even, bottom, top)

    x_faces = exchange(*swaps(jnp.concatenate([displacement, physical[None]], axis=0), 5), "gx")
    frame = (ELEMENTS, ROWS, LANES)
    own_frame = (ELEMENTS, SY, LANES)
    weights = call(
        functools.partial(weights_kernel, extents=extents), (supports.reshape(1, -1),),
        [frame, own_frame, (CHOSEN, SY, LANES), block], [own_frame, own_frame], 10**7,
    )
    design_faces = swaps(jnp.stack([design, passive.astype(F32)]), 3)
    x_faces, design_faces, (inverse, edge, volume_weight, marks) = lax.optimization_barrier(
        (x_faces, design_faces, weights)
    )

    groups = energy_groups()
    faces = (11 * NODES, SZ)
    tiles = (4 * NODES, SY, SZ)
    ext = (4, NODES, SY, LANES)
    y_faces = call(faces_y_kernel, (displacement, physical, *x_faces), [faces, faces], [], 10**6)
    y_faces, x_faces, design_faces = lax.optimization_barrier((y_faces, x_faces, design_faces))
    y_faces = exchange(*y_faces, "gy")
    design_faces = exchange(*design_faces, "gx")
    (side,) = call(faces_side_kernel, (displacement, physical, *x_faces), [(4 * NODES, SY, SIDE)], [], 1)
    (inner_part,) = call(
        functools.partial(inner_kernel, groups=groups),
        (displacement, physical, *x_faces, other_core(side), inverse), [own_frame], [ext], 1,
    )
    y_faces, inner_part = lax.optimization_barrier((y_faces, inner_part))
    edge_tiles, side = call(
        faces_edge_kernel, (displacement, physical, *x_faces, *y_faces, design, passive, *design_faces),
        [tiles, (4 * NODES + 2 * CHOSEN, SY, SIDE)], [], 10**6,
    )
    side = other_core(side)

    faces = (9 * CHOSEN, LANES)
    inner, outer = sizes[1] * sizes[2], sizes[0]
    elements = (2 * SX, SY, 128)
    bounds, *y_bounds, part = call(
        functools.partial(design_kernel, groups=groups),
        (design, passive, *design_faces, inner_part, edge_tiles, side, inverse, edge, volume_weight),
        [(3, CHOSEN, SY, LANES), faces, faces, (inner, 8, 128)],
        [ext, own_frame, own_frame, own_frame, own_frame]
        + [(2,) + elements, (2,) + elements, (2, 6) + elements], 10**7,
    )

    part = lax.all_to_all(part, ("gy", "gz"), 0, 0, tiled=True)
    y_bounds, part = lax.optimization_barrier((y_bounds, part))
    y_bounds = exchange(*y_bounds, "gy")
    (part,) = call(repeat_kernel, (part,), [(outer, 8, 128)], [], 10**5)
    part = lax.all_to_all(part, "gx", 0, 0, tiled=True)

    chosen = (CHOSEN, ROWS, LANES)
    target = volume_share * (extents[0] * extents[1] * extents[2])
    new_design, new_physical, node_blocks = call(
        functools.partial(final_kernel, factors=[float(f) for f in corner_factors()], target=target),
        (part, bounds, *y_bounds, inverse, marks), [block, block, (6,) + block],
        [chosen, chosen, chosen, (SX + 1, ROWS, LANES)], 10**7,
    )
    return (new_design, new_physical, node_blocks)


def solution(mesh):
    in_specs = (
        P(None, "gx", "gy", "gz"),
        P("gx", "gy", "gz"),
        P("gx", "gy", "gz"),
        P("gx", "gy", "gz"),
        P(),
    )
    out_specs = (P("gx", "gy", "gz"), P("gx", "gy", "gz"), P(None, "gx", "gy", "gz"))
    return jax.shard_map(body, mesh=mesh, in_specs=in_specs, out_specs=out_specs, check_vma=False)
```

```python
import functools
import math

import jax
import jax.numpy as jnp
import numpy as np
from jax import lax
from jax.experimental import pallas as pl
from jax.experimental.pallas import tpu as pltpu
from jax.sharding import PartitionSpec as P

STEPS = 10

filter_radius = 2.5
penalty = 3.0
move_limit = 0.2
stiff_floor = 1e-09
volume_share = 0.5
log_lower = -20.0
log_upper = 20.0
poisson = 0.3

SX, SY, SZ = 8, 8, 256
ROWS, LANES, SIDE = 16, 384, 128
NODES, ELEMENTS, CHOSEN = SX + 10, SX + 9, SX + 5
POINTS = 2**STEPS
F32 = jnp.float32


def corner_offsets():
    return [(q // 4, q // 2 % 2, q % 2) for q in range(8)]


def hex_stiffness():
    lame_first = poisson / ((1.0 + poisson) * (1.0 - 2.0 * poisson))
    shear_modulus = 0.5 / (1.0 + poisson)
    elastic = np.zeros((6, 6))
    elastic[:3, :3] = lame_first
    for d in range(3):
        elastic[d, d] += 2.0 * shear_modulus
        elastic[d + 3, d + 3] = shear_modulus
    corners = corner_offsets()
    points = [0.5 - 0.5 / math.sqrt(3.0), 0.5 + 0.5 / math.sqrt(3.0)]
    matrix = np.zeros((24, 24))
    for p in points:
        for q in points:
            for r in points:
                location = [p, q, r]
                gradients = np.zeros((8, 3))
                for n in range(8):
                    factors = [
                        location[e] if corners[n][e] == 1 else 1.0 - location[e] for e in range(3)
                    ]
                    for d in range(3):
                        sign_value = 1.0 if corners[n][d] == 1 else -1.0
                        gradients[n, d] = sign_value * factors[(d + 1) % 3] * factors[(d + 2) % 3]
                strain = np.zeros((6, 24))
                for n in range(8):
                    column = 3 * n
                    strain[0, column] = gradients[n, 0]
                    strain[1, column + 1] = gradients[n, 1]
                    strain[2, column + 2] = gradients[n, 2]
                    strain[3, column + 1] = gradients[n, 2]
                    strain[3, column + 2] = gradients[n, 1]
                    strain[4, column] = gradients[n, 2]
                    strain[4, column + 2] = gradients[n, 0]
                    strain[5, column] = gradients[n, 1]
                    strain[5, column + 1] = gradients[n, 0]
                matrix += strain.T @ elastic @ strain / 8.0
    return matrix


def energy_groups():
    corners = corner_offsets()
    modes = np.zeros((24, 24))
    for s in range(8):
        bits = (s // 4, s // 2 % 2, s % 2)
        for n in range(8):
            sign_value = 1.0
            for e in range(3):
                if bits[e] == 1 and corners[n][e] == 0:
                    sign_value = -sign_value
            for d in range(3):
                modes[3 * n + d, 3 * s + d] = sign_value
    form = modes.T @ hex_stiffness() @ modes / 64.0
    groups = []

    def add(coefficient, members):
        if abs(coefficient) < 1e-9:
            return
        for group in groups:
            if abs(group[0] - coefficient) < 1e-9:
                group[1].append(members)
                return
        groups.append((coefficient, [members]))

    for parity in range(8):
        left = [3 * (parity ^ (4, 2, 1)[d]) + d for d in range(3)]
        while left:
            first = left[0]
            block = [m for m in left if m == first or abs(form[first, m]) > 1e-9]
            left = [m for m in left if m not in block]
            beside = form[block[0], block[1]] if len(block) > 1 else 0.0
            add(beside, block)
            for m in block:
                add(form[m, m] - beside, [m])
    rebuilt = np.zeros((24, 24))
    for coefficient, sums in groups:
        for members in sums:
            rebuilt[np.ix_(members, members)] += coefficient
    assert np.abs(rebuilt - form).max() < 1e-9
    return groups


def corner_factors():
    matrix = hex_stiffness()
    factors = (matrix[0, 0], matrix[1, 2], matrix[0, 2], matrix[0, 1])
    for n, corner in enumerate(corner_offsets()):
        sign = [1.0 if c == 1 else -1.0 for c in corner]
        block = matrix[3 * n : 3 * n + 3, 3 * n : 3 * n + 3]
        assert np.allclose(np.diag(block), factors[0])
        assert np.allclose(block[1, 2], factors[1] * sign[1] * sign[2])
        assert np.allclose(block[0, 2], factors[2] * sign[0] * sign[2])
        assert np.allclose(block[0, 1], factors[3] * sign[0] * sign[1])
    return factors


def tap(square):
    return max(0.0, filter_radius - math.sqrt(square))


def rolled(value, steps, dim):
    return pltpu.roll(value, (-steps) % value.shape[dim], dim)


def row_pairs(plane):
    return (
        rolled(plane, 1, 0) + rolled(plane, -1, 0),
        rolled(plane, 2, 0) + rolled(plane, -2, 0),
    )


def filtered_plane(plane_of, near_of, far_of, p):
    ring_0 = plane_of(p)
    ring_1 = near_of(p) + plane_of(p - 1) + plane_of(p + 1)
    ring_2 = near_of(p - 1) + near_of(p + 1)
    ring_4 = far_of(p) + plane_of(p - 2) + plane_of(p + 2)
    ring_5 = far_of(p - 1) + far_of(p + 1) + near_of(p - 2) + near_of(p + 2)
    layers = []
    for c in (0, 1, 2):
        total = None
        for square, ring in ((0, ring_0), (1, ring_1), (2, ring_2), (4, ring_4), (5, ring_5)):
            weight = tap(square + c * c)
            if weight > 0.0:
                total = weight * ring if total is None else total + weight * ring
        layers.append(total)
    middle, near, far = layers
    return middle + (rolled(near, 1, 1) + rolled(near, -1, 1)) + (rolled(far, 2, 1) + rolled(far, -2, 1))


def weights_kernel(support_ref, inverse_ref, edge_ref, volume_ref, mark_ref, near_ref, far_ref, *, extents):
    total_x, total_y, total_z = extents
    first_x = lax.axis_index("gx") * SX
    first_y = lax.axis_index("gy") * SY
    first_z = lax.axis_index("gz") * SZ
    row = lax.broadcasted_iota(jnp.int32, (ROWS, LANES), 0)
    lane = lax.broadcasted_iota(jnp.int32, (ROWS, LANES), 1)
    y = first_y + jnp.where(row < 12, row, row - ROWS)
    z = first_z + jnp.where(lane < SZ + SIDE // 2, lane, lane - LANES)
    inside = jnp.where((y >= 0) & (y < total_y) & (z >= 0) & (z < total_z), 1.0, 0.0).astype(F32)
    near, far = row_pairs(inside)

    def present(p):
        x = first_x + p
        return jnp.where((x >= 0) & (x < total_x), 1.0, 0.0).astype(F32)

    for p in range(ELEMENTS):
        x = p - 5
        weight_sum = filtered_plane(
            lambda q: inside * present(q), lambda q: near * present(q), lambda q: far * present(q), x
        )
        here = inside * present(x)
        inverse = jnp.where(here > 0.0, 1.0 / jnp.where(here > 0.0, weight_sum, 1.0), 0.0)
        inverse_ref[p] = inverse
        edge_ref[p] = jnp.concatenate([inverse[7:11], inverse[14:16], inverse[0:2]], axis=0)
        inverse_near, inverse_far = row_pairs(inverse)
        near_ref[p] = inverse_near[0:SY]
        far_ref[p] = inverse_far[0:SY]
    for p in range(CHOSEN):
        volume_ref[p] = filtered_plane(
            lambda q: inverse_ref[q, 0:SY], lambda q: near_ref[q], lambda q: far_ref[q], p + 2
        )
    node = support_ref[...]
    node_x = node // (total_y * total_z) - first_x
    node_y = node // total_z % total_y - first_y
    node_z = node % total_z - first_z
    owned = (node_x >= 0) & (node_x < SX) & (node_y >= 0) & (node_y < SY)
    line = jnp.where(owned, node_x * SY + node_y, -1)
    count = node.shape[1]
    lines = jnp.where(lax.broadcasted_iota(jnp.int32, (SX * SY, count), 0) == line, 1.0, 0.0)
    lanes = jnp.where(lax.broadcasted_iota(jnp.int32, (SZ, count), 0) == node_z, 1.0, 0.0)
    hits = lax.dot_general(
        lines.astype(jnp.bfloat16),
        lanes.astype(jnp.bfloat16),
        (((1,), (1,)), ((), ())),
        preferred_element_type=F32,
    )
    for p in range(SX):
        mark_ref[p] = hits[p * SY : (p + 1) * SY]


def is_even(axis):
    return lax.axis_index(axis) % 2 == 0


def place_pair(even, first_ref, second_ref, top, bottom, place):
    first_ref[place] = jnp.where(even, top, bottom)
    second_ref[place] = jnp.where(even, bottom, top)


def low_high(axis, first_ref, second_ref, place):
    index = lax.axis_index(axis)
    first, second = first_ref[place], second_ref[place]
    low = jnp.where(index == 0, 0.0, jnp.where(index % 2 == 0, second, first))
    high = jnp.where(index == lax.axis_size(axis) - 1, 0.0, jnp.where(index % 2 == 0, first, second))
    return low, high


def row_place(index):
    if index < 3 * NODES:
        return slice(3 * index, 3 * index + 3)
    return slice(2 * index + 3 * NODES, 2 * index + 3 * NODES + 2)


def row_tile(first_ref, second_ref, place):
    low, high = low_high("gy", first_ref, second_ref, place)
    filler = jnp.zeros((SY - 2 * low.shape[0], low.shape[1]), F32)
    return jnp.concatenate([high, filler, low], axis=0)


def plane_reader(shift_ref, physical_ref, x_first, x_second):
    def read(index):
        f, x = index // NODES, index % NODES - 5
        if 0 <= x < SX:
            return shift_ref[f, x] if f < 3 else physical_ref[x]
        low, high = low_high("gx", x_first, x_second, (f, x + 5 if x < 0 else x - SX))
        return low if x < 0 else high

    return read


def design_reader(design_ref, passive_ref, x_first, x_second):
    def read(index):
        f, x = index // CHOSEN, index % CHOSEN - 3
        if 0 <= x < SX:
            return design_ref[x] if f == 0 else passive_ref[x].astype(F32)
        low, high = low_high("gx", x_first, x_second, (f, x + 3 if x < 0 else x - SX))
        return low if x < 0 else high

    return read


def near_half(plane):
    return jnp.where(lax.axis_index("gz") == 0, plane[:, SZ - SIDE :], plane[:, 0:SIDE])


def edge_tile(plane, low, high):
    missing = 3 - high.shape[0]
    filler = [jnp.zeros((missing, SZ), F32)] if missing else []
    return jnp.concatenate([plane[7:8], high, *filler, low[low.shape[0] - 2 :], plane[0:2]], axis=0)


def faces_y_kernel(shift_ref, physical_ref, x_first, x_second, first_ref, second_ref, side_ref):
    even = is_even("gy")
    read = plane_reader(shift_ref, physical_ref, x_first, x_second)
    for index in range(4 * NODES):
        plane = read(index)
        rows = row_place(index)
        depth = rows.stop - rows.start
        place_pair(even, first_ref, second_ref, plane[SY - depth :], plane[0:depth], rows)
        side_ref[index] = near_half(plane)


def faces_edge_kernel(
    shift_ref, physical_ref, x_first, x_second, y_first, y_second, design_ref, passive_ref, d_first, d_second,
    edge_ref, side_ref
):
    read = plane_reader(shift_ref, physical_ref, x_first, x_second)
    for index in range(4 * NODES):
        low, high = low_high("gy", y_first, y_second, row_place(index))
        tile = edge_tile(read(index), low, high)
        edge_ref[index] = tile
        side_ref[index] = near_half(tile)
    read = design_reader(design_ref, passive_ref, d_first, d_second)
    for index in range(2 * CHOSEN):
        side_ref[4 * NODES + index] = near_half(read(index))


def scaled_energy(ext_ref, read, side, inverse_of, out_ref, groups):
    lane = lax.broadcasted_iota(jnp.int32, (SY, SIDE), 1)
    start = lax.axis_index("gz") * (SIDE // 2)
    keep = (lane >= start) & (lane < start + SIDE // 2)
    for f in range(4):
        for p in range(NODES):
            index = NODES * f + p
            ext_ref[f, p, :, 0:SZ] = read(index)
            ext_ref[f, p, :, SZ:LANES] = jnp.where(keep, side[index], 0.0)
    scale = penalty * (1.0 - stiff_floor)

    @pl.loop(0, ELEMENTS, unroll=True)
    def _(p):
        modes = {}
        for d in range(3):
            here, above = ext_ref[d, p], ext_ref[d, p + 1]
            for a, along_x in enumerate((here + above, above - here)):
                beyond = rolled(along_x, 1, 0)
                for b, along_y in enumerate((along_x + beyond, beyond - along_x)):
                    next_lane = rolled(along_y, 1, 1)
                    for c, mode in enumerate((along_y + next_lane, next_lane - along_y)):
                        modes[3 * (4 * a + 2 * b + c) + d] = mode
        energy = None
        for coefficient, sums in groups:
            squares = None
            for members in sums:
                value = functools.reduce(lambda left, right: left + right, [modes[m] for m in members])
                squares = value * value if squares is None else squares + value * value
            squares = float(coefficient) * squares
            energy = squares if energy is None else energy + squares
        density = ext_ref[3, p]
        out_ref[p] = scale * density * density * energy * inverse_of(p)


def inner_kernel(shift_ref, physical_ref, x_first, x_second, side, inverse_ref, out_ref, ext_ref, *, groups):
    read = plane_reader(shift_ref, physical_ref, x_first, x_second)
    scaled_energy(ext_ref, read, side, lambda p: inverse_ref[p, 0:SY], out_ref, groups)


def design_kernel(
    design_ref, passive_ref, d_first, d_second, inner_ref, edge_tiles, edge_side, inverse_ref, edge_ref, volume_ref,
    out_ref, first_ref, second_ref, part_ref, ext_ref, outer_ref, sens_ref, near_ref, far_ref, high_ref, low_ref,
    value_ref, *, groups
):
    even = is_even("gy")
    scaled_energy(
        ext_ref, lambda index: edge_tiles[index], edge_side, lambda p: edge_ref[p], outer_ref, groups
    )
    row = lax.broadcasted_iota(jnp.int32, (SY, LANES), 0)
    for p in range(ELEMENTS):
        outer = outer_ref[p]
        own = jnp.where(row == 7, rolled(outer, -7, 0), inner_ref[p])
        beyond = jnp.where(row < 4, rolled(outer, 1, 0), rolled(outer, -2, 0))
        sens_ref[p] = own
        near, far = row_pairs(jnp.concatenate([own, beyond], axis=0))
        near_ref[p] = near[0:SY]
        far_ref[p] = far[0:SY]

    read_design = design_reader(design_ref, passive_ref, d_first, d_second)
    for p in range(CHOSEN):
        filtered = filtered_plane(lambda q: sens_ref[q], lambda q: near_ref[q], lambda q: far_ref[q], p + 2)
        index = 4 * NODES + p
        design = jnp.concatenate([read_design(p), edge_side[index]], axis=1)
        solid = jnp.concatenate([read_design(p + CHOSEN), edge_side[index + CHOSEN]], axis=1) > 0.5
        inside = inverse_ref[p + 2, 0:SY] > 0.0
        scaled = design * jnp.sqrt(filtered / jnp.where(inside, volume_ref[p], 1.0))
        floor_bound = jnp.where(solid, 1.0, jnp.maximum(0.0, design - move_limit))
        ceiling = jnp.where(solid, 1.0, jnp.minimum(1.0, design + move_limit))
        for f, value in enumerate((scaled, floor_bound, ceiling)):
            value = jnp.where(inside, value, 0.0)
            out_ref[f, p] = value
            row = 3 * (CHOSEN * f + p)
            place_pair(even, first_ref, second_ref, value[SY - 3 :], value[0:3], slice(row, row + 3))
    add_volumes(out_ref, volume_ref, part_ref, high_ref, low_ref, value_ref)


def three_parts(value):
    first = value.astype(jnp.bfloat16).astype(F32)
    second = (value - first).astype(jnp.bfloat16).astype(F32)
    return first, second, value - first - second


def add_volumes(bounds_ref, volume_ref, out_ref, high_ref, low_ref, value_ref):
    step = (log_upper - log_lower) / POINTS
    ceilings = jnp.zeros((SY, 128), F32)
    for v in range(2 * SX):
        place = (3 + v // 2, slice(None), slice(128 * (v % 2), 128 * (v % 2 + 1)))
        weight = volume_ref[place]
        scaled, floor_bound, ceiling = [bounds_ref[(f,) + place] for f in range(3)]
        ceilings = ceilings + weight * ceiling
        log_scaled = jnp.log(jnp.maximum(scaled, 1e-30))
        for t, bound in enumerate((ceiling, floor_bound)):
            reached = (2.0 * (log_scaled - jnp.log(jnp.maximum(bound, 1e-30))) - log_lower) / step
            index = jnp.minimum(jnp.maximum(jnp.ceil(reached), 1.0), POINTS + 1.0) - 1.0
            index = jnp.where(bound > 0.0, index, float(POINTS))
            high = jnp.floor(index * (1.0 / 128.0))
            high_ref[t, v] = high
            low_ref[t, v] = index - 128.0 * high
            sign = -1.0 if t == 0 else 1.0
            parts = three_parts(sign * weight * bound) + three_parts(-sign * weight * scaled)
            for n, part in enumerate(parts):
                value_ref[t, n, v] = part

    rows = lax.broadcasted_iota(jnp.int32, (8, 128), 0).astype(F32)
    columns = lax.broadcasted_iota(jnp.int32, (128, 128), 0).astype(F32).astype(jnp.bfloat16)

    def add_group(v, total):
        lefts, rights = [], []
        for r in range(SY):
            left, right = [], []
            for t in range(2):
                hit = rows == high_ref[t, v, r : r + 1, :]
                left += [jnp.where(hit, value_ref[t, n, v, r : r + 1, :], 0.0) for n in range(6)]
                low = jnp.broadcast_to(low_ref[t, v, r : r + 1, :], (16, 128)).astype(jnp.bfloat16)
                low = jnp.concatenate([low] * 8, axis=0)
                right.append(jnp.where(columns == low, jnp.bfloat16(1.0), jnp.bfloat16(0.0)))
            lefts.append(jnp.concatenate(left, axis=0).astype(jnp.bfloat16))
            rights.append(jnp.concatenate(right, axis=0))
        return total + lax.dot_general(
            jnp.concatenate(rights, axis=1),
            jnp.concatenate(lefts, axis=1),
            (((1,), (1,)), ((), ())),
            preferred_element_type=F32,
        )

    total = lax.fori_loop(0, 2 * SX, add_group, jnp.zeros((256, 96), F32), unroll=8)
    total = (total[0:128, 0:48] + total[128:256, 48:96]).T
    constant = total[0:8] + total[8:16] + total[16:24]
    slope = total[24:32] + total[32:40] + total[40:48]
    upto = jnp.where(
        lax.broadcasted_iota(jnp.int32, (128, 128), 0) <= lax.broadcasted_iota(jnp.int32, (128, 128), 1), 1.0, 0.0
    )
    running = lax.dot_general(
        jnp.concatenate([constant, slope], axis=0),
        upto,
        (((1,), (0,)), ((), ())),
        precision=lax.Precision.HIGHEST,
        preferred_element_type=F32,
    )
    row = lax.broadcasted_iota(jnp.int32, (8, 128), 0)
    lane = lax.broadcasted_iota(jnp.int32, (8, 128), 1)
    cumulated = []
    for part in (running[0:8], running[8:16]):
        ends = jnp.broadcast_to(part[:, 127:128], (8, 128))
        before = ends
        for shift in (1, 2, 4):
            before = before + jnp.where(row >= shift, rolled(before, -shift, 0), 0.0)
        cumulated.append(part + (before - ends))
    index = (row * 128 + lane + 1).astype(F32)
    factor = jnp.exp(-0.5 * (log_lower + step * index))
    result = jnp.sum(ceilings) + cumulated[0] + factor * cumulated[1]
    for i in range(out_ref.shape[0]):
        out_ref[i] = result


def repeat_kernel(part_ref, out_ref):
    total = part_ref[0]
    for i in range(1, part_ref.shape[0]):
        total = total + part_ref[i]
    for i in range(out_ref.shape[0]):
        out_ref[i] = total


def final_kernel(
    part_ref, own_ref, y_first, y_second, inverse_ref, mark_ref, new_design_ref, new_physical_ref,
    blocks_ref, chosen_ref, near_ref, far_ref, stiff_ref, *, factors, target
):
    total = part_ref[0]
    for i in range(1, part_ref.shape[0]):
        total = total + part_ref[i]
    low_end = jnp.minimum(jnp.sum(jnp.where(total > target, 1.0, 0.0)), POINTS - 1.0)
    multiplier = log_lower + (log_upper - log_lower) / POINTS * (low_end + 0.5)
    factor = jnp.exp(jnp.broadcast_to(-0.5 * multiplier, (SY, LANES)))
    for p in range(CHOSEN):
        tiles = []
        own = [own_ref[f, p] for f in range(3)]
        beside = []
        for f in range(3):
            row = 3 * (CHOSEN * f + p)
            beside.append(row_tile(y_first, y_second, slice(row, row + 3)))
        for scaled, floor_bound, ceiling in (own, beside):
            tiles.append(jnp.minimum(jnp.maximum(scaled * factor, floor_bound), ceiling))
        chosen = jnp.concatenate(tiles, axis=0)
        chosen_ref[p] = chosen
        near, far = row_pairs(chosen)
        near_ref[p] = near
        far_ref[p] = far
        if 3 <= p < SX + 3:
            new_design_ref[p - 3] = tiles[0][:, 0:SZ]
    for p in range(SX + 1):
        inverse = inverse_ref[p + 4]
        density = (
            filtered_plane(lambda q: chosen_ref[q], lambda q: near_ref[q], lambda q: far_ref[q], p + 2) * inverse
        )
        if p >= 1:
            new_physical_ref[p - 1] = density[0:SY, 0:SZ]
        cube = stiff_floor + density * density * density * (1.0 - stiff_floor)
        stiff_ref[p] = jnp.where(inverse > 0.0, cube, 0.0)
    for p in range(SX):
        below, here = stiff_ref[p], stiff_ref[p + 1]
        x_sum, x_diff = here + below, below - here
        x_sum_back, x_diff_back = rolled(x_sum, -1, 0), rolled(x_diff, -1, 0)
        sum_sum = (x_sum + x_sum_back)[0:SY]
        sum_diff = (x_sum_back - x_sum)[0:SY]
        diff_sum = (x_diff + x_diff_back)[0:SY]
        diff_diff = (x_diff_back - x_diff)[0:SY]
        marked = mark_ref[p] > 0.5
        even = factors[0] * (sum_sum + rolled(sum_sum, -1, 1))[:, 0:SZ]
        even = jnp.where(marked, 1.0, even)
        blocks_ref[0, p] = even
        blocks_ref[1, p] = even
        blocks_ref[2, p] = even
        yz = factors[1] * (rolled(sum_diff, -1, 1) - sum_diff)[:, 0:SZ]
        xz = factors[2] * (rolled(diff_sum, -1, 1) - diff_sum)[:, 0:SZ]
        xy = factors[3] * (diff_diff + rolled(diff_diff, -1, 1))[:, 0:SZ]
        blocks_ref[3, p] = jnp.where(marked, 0.0, yz)
        blocks_ref[4, p] = jnp.where(marked, 0.0, xz)
        blocks_ref[5, p] = jnp.where(marked, 0.0, xy)


def call(kernel, inputs, shapes, scratch, flops, spaces=None, grant=32):
    outs = [jax.ShapeDtypeStruct(shape, F32) for shape in shapes]
    return pl.pallas_call(
        kernel,
        out_shape=outs,
        in_specs=[pl.BlockSpec(memory_space=space) for space in spaces or [pltpu.VMEM] * len(inputs)],
        out_specs=[pl.BlockSpec(memory_space=pltpu.VMEM)] * len(outs),
        scratch_shapes=[pltpu.VMEM(shape, F32) if isinstance(shape, tuple) else shape for shape in scratch],
        compiler_params=pltpu.CompilerParams(vmem_limit_bytes=grant * 2**20),
        cost_estimate=pl.CostEstimate(flops=flops, bytes_accessed=min(flops, 10**6), transcendentals=0),
    )(*inputs)


def exchange(first, second, axis):
    count = lax.axis_size(axis)
    results = []
    for start, faces in enumerate((first, second)):
        pairs = [(i, (i + 1) % count) for i in range(start, count, 2)]
        results.append(lax.ppermute(faces, axis, pairs + [(j, i) for i, j in pairs]))
    return results


def other_core(values):
    return lax.ppermute(values, "gz", [(0, 1), (1, 0)])


def body(displacement, physical, design, passive, supports):
    assert design.shape == (SX, SY, SZ) and lax.axis_size("gz") == 2
    sizes = [lax.axis_size(axis) for axis in ("gx", "gy", "gz")]
    extents = (SX * sizes[0], SY * sizes[1], SZ * sizes[2])
    block = (SX, SY, SZ)
    even = lax.axis_index("gx") % 2 == 0

    def swaps(fields, depth):
        top, bottom = fields[:, SX - depth :], fields[:, 0:depth]
        return jnp.where(even, top, bottom), jnp.where(even, bottom, top)

    x_faces = exchange(*swaps(jnp.concatenate([displacement, physical[None]], axis=0), 5), "gx")
    frame = (ELEMENTS, ROWS, LANES)
    own_frame = (ELEMENTS, SY, LANES)
    weights = call(
        functools.partial(weights_kernel, extents=extents), (supports.reshape(1, -1),),
        [frame, own_frame, (CHOSEN, SY, LANES), block], [own_frame, own_frame], 10**7,
    )
    design_faces = swaps(jnp.stack([design, passive.astype(F32)]), 3)
    x_faces, design_faces, (inverse, edge, volume_weight, marks) = lax.optimization_barrier(
        (x_faces, design_faces, weights)
    )

    groups = energy_groups()
    faces = (11 * NODES, SZ)
    tiles = (4 * NODES, SY, SZ)
    ext = (4, NODES, SY, LANES)
    *y_faces, side = call(
        faces_y_kernel, (displacement, physical, *x_faces), [faces, faces, (4 * NODES, SY, SIDE)], [], 10**6
    )
    y_faces, side, design_faces = lax.optimization_barrier((y_faces, side, design_faces))
    y_faces = exchange(*y_faces, "gy")
    design_faces = exchange(*design_faces, "gx")
    (inner_part,) = call(
        functools.partial(inner_kernel, groups=groups),
        (displacement, physical, *x_faces, other_core(side), inverse), [own_frame], [ext], 1,
    )
    y_faces, inner_part = lax.optimization_barrier((y_faces, inner_part))
    edge_tiles, side = call(
        faces_edge_kernel, (displacement, physical, *x_faces, *y_faces, design, passive, *design_faces),
        [tiles, (4 * NODES + 2 * CHOSEN, SY, SIDE)], [], 10**6,
    )
    side = other_core(side)

    faces = (9 * CHOSEN, LANES)
    inner, outer = sizes[1] * sizes[2], sizes[0]
    elements = (2 * SX, SY, 128)
    bounds, *y_bounds, part = call(
        functools.partial(design_kernel, groups=groups),
        (design, passive, *design_faces, inner_part, edge_tiles, side, inverse, edge, volume_weight),
        [(3, CHOSEN, SY, LANES), faces, faces, (inner, 8, 128)],
        [ext, own_frame, own_frame, own_frame, own_frame]
        + [(2,) + elements, (2,) + elements, (2, 6) + elements], 10**7,
    )

    part = lax.all_to_all(part, ("gy", "gz"), 0, 0, tiled=True)
    y_bounds, part = lax.optimization_barrier((y_bounds, part))
    y_bounds = exchange(*y_bounds, "gy")
    (part,) = call(repeat_kernel, (part,), [(outer, 8, 128)], [], 10**5)
    part = lax.all_to_all(part, "gx", 0, 0, tiled=True)

    chosen = (CHOSEN, ROWS, LANES)
    target = volume_share * (extents[0] * extents[1] * extents[2])
    new_design, new_physical, node_blocks = call(
        functools.partial(final_kernel, factors=[float(f) for f in corner_factors()], target=target),
        (part, bounds, *y_bounds, inverse, marks), [block, block, (6,) + block],
        [chosen, chosen, chosen, (SX + 1, ROWS, LANES)], 10**7,
    )
    return (new_design, new_physical, node_blocks)


def solution(mesh):
    in_specs = (
        P(None, "gx", "gy", "gz"),
        P("gx", "gy", "gz"),
        P("gx", "gy", "gz"),
        P("gx", "gy", "gz"),
        P(),
    )
    out_specs = (P("gx", "gy", "gz"), P("gx", "gy", "gz"), P(None, "gx", "gy", "gz"))
    return jax.shard_map(body, mesh=mesh, in_specs=in_specs, out_specs=out_specs, check_vma=False)
```
